256 devices in a mesh: step: 8 (over x, core), seq: 32 (over z, y).
Axes of the slice: x: 4, y: 4, z: 8, core: 2. Of those that a mesh axis runs over, the one named last changes fastest.
Arguments:
- start_latent: float32 [1536, 64], P('seq'), may hold values from -6 to 6
- noise: bfloat16 [16, 1536, 64], P('step', 'seq'), may hold values from -6 to 6
- window_start: int32 [1], replicated, may hold values from 0 to 12
- w_embed: bfloat16 [64, 3072], replicated, may hold values from -0.75 to 0.75
- w_time: bfloat16 [256, 3072], replicated, may hold values from -0.375 to 0.375
- norm_gain: float32 [3072], replicated, may hold values from 0.5 to 2
- w_query: bfloat16 [3072, 2048], P(None, 'step'), may hold values from -0.109375 to 0.109375
- w_key: bfloat16 [3072, 2048], P(None, 'step'), may hold values from -0.109375 to 0.109375
- w_value: bfloat16 [3072, 2048], P(None, 'step'), may hold values from -0.109375 to 0.109375
- query_gain: float32 [128], replicated, may hold values from 1 to 2.5
- key_gain: float32 [128], replicated, may hold values from 1 to 2.5
- w_out: bfloat16 [2048, 3072], P('step'), may hold values from -0.125 to 0.125
- w_final: bfloat16 [3072, 64], replicated, may hold values from -0.109375 to 0.109375
Outputs:
- step_outputs: float32 [16, 1536, 64], P('step', 'seq')
- errors: float32 [16], P('step')
The draws below stay inside these ranges and needn't reach their ends.
All inputs are finite; a program needn't handle non-finite values.
Results may differ from the reference program's by a relative error of at most 0.0034.
Values may be sent and summed in bfloat16 or wider, within the bound.
A program may use at most 128 MiB of HBM per device.

```python
import math
import jax
import jax.numpy as jnp
from jax import lax

D = 3072
C = 64
HEADS = 16
HEAD = 128
FREQ = 256
NSCHED = 28
ITERS = 2
STEPS = 16
LEN = 1536


def block_scale(rng, dims, shards, low, largest):
    loudness, own = 1.0, jax.random.fold_in(rng, 6)
    for dim, parts in shards:
        steps = jnp.exp(jax.random.uniform(jax.random.fold_in(own, dim), (parts,), jnp.float32, low / len(shards), largest / len(shards)))
        loudness = loudness * jnp.repeat(steps, dims[dim] // parts).reshape([-1 if axis == dim else 1 for axis in range(len(dims))])
    return loudness


def normal_values(key, extent, scale, limit, shards=(), kind=jnp.bfloat16):
    values = scale * jax.random.normal(key, extent, jnp.float32)
    if shards:
        values = values * block_scale(key, extent, shards, -0.22, 0.18)
    return jnp.clip(values, -limit, limit).astype(kind)


def setup_inputs(seed: int = 0) -> dict:
    key_list = jax.random.split(jax.random.key(seed), 14)
    start_latent = normal_values(key_list[0], (LEN, C), 1.0, 6.0, ((0, 32),), jnp.float32)
    noise = normal_values(key_list[1], (STEPS, LEN, C), 1.0, 6.0, ((0, 8), (1, 32)))
    window_start = jax.random.randint(key_list[2], (1,), 0, NSCHED - STEPS + 1).astype(jnp.int32)
    w_embed = normal_values(key_list[3], (C, D), C ** -0.5, 0.75)
    w_time = normal_values(key_list[4], (FREQ, D), FREQ ** -0.5, 0.375)
    norm_gain = jnp.clip(jnp.exp(jax.random.uniform(key_list[5], (D,), jnp.float32, math.log(0.5), math.log(2.0))), 0.5, 2.0)
    w_query = normal_values(key_list[6], (D, HEADS * HEAD), D ** -0.5, 0.109375, ((1, 8),))
    w_key = normal_values(key_list[7], (D, HEADS * HEAD), D ** -0.5, 0.109375, ((1, 8),))
    w_value = normal_values(key_list[8], (D, HEADS * HEAD), D ** -0.5, 0.109375, ((1, 8),))
    query_gain = jnp.clip(jnp.exp(jax.random.uniform(key_list[9], (HEAD,), jnp.float32, math.log(1.0), math.log(2.5))), 1.0, 2.5)
    key_gain = jnp.clip(jnp.exp(jax.random.uniform(key_list[10], (HEAD,), jnp.float32, math.log(1.0), math.log(2.5))), 1.0, 2.5)
    w_out = normal_values(key_list[11], (HEADS * HEAD, D), (HEADS * HEAD) ** -0.5, 0.125, ((0, 8),))
    w_final = normal_values(key_list[12], (D, C), D ** -0.5, 0.109375)
    return dict(start_latent=start_latent, noise=noise, window_start=window_start, w_embed=w_embed, w_time=w_time, norm_gain=norm_gain, w_query=w_query, w_key=w_key, w_value=w_value, query_gain=query_gain, key_gain=key_gain, w_out=w_out, w_final=w_final)


EPS = 1e-06
SHIFT = 3.0
ETA = 0.5

def sigma_of(indices):
    fraction = 1.0 - indices.astype(jnp.float32) / NSCHED
    return SHIFT * fraction / (1.0 + (SHIFT - 1.0) * fraction)

def time_embed(sigma, w_time):
    half_count = w_time.shape[0] // 2
    frequency = jnp.exp(-math.log(10000.0) * jnp.arange(half_count, dtype=jnp.float32) / half_count)
    angles = 1000.0 * sigma[:, None] * frequency[None, :]
    features = jnp.concatenate([jnp.cos(angles), jnp.sin(angles)], axis=1)
    features = jax.nn.silu(features).astype(jnp.bfloat16)
    return jnp.dot(features, w_time, preferred_element_type=jnp.float32)

def rms_scale(values, scaling):
    return values * lax.rsqrt(lax.optimization_barrier(jnp.mean(values * values, axis=-1, keepdims=True)) + EPS) * scaling

def reference(start_latent, noise, window_start, w_embed, w_time, norm_gain, w_query, w_key, w_value, query_gain, key_gain, w_out, w_final):
    indices = window_start[0] + jnp.arange(STEPS, dtype=jnp.int32)
    sigma_now = sigma_of(indices)
    step_delta = sigma_of(indices + 1) - sigma_now
    noise_coeff = ETA * jnp.sqrt(-step_delta)
    temb_all = time_embed(sigma_now, w_time)
    final_wide = w_final.astype(jnp.float32)

    def velocity_of(pair):
        latent, temb = pair
        hidden = jnp.dot(latent, w_embed, preferred_element_type=jnp.float32) + temb[None, :]
        normed = rms_scale(hidden, norm_gain).astype(jnp.bfloat16)
        queries = rms_scale(jnp.dot(normed, w_query, preferred_element_type=jnp.float32).reshape(LEN, HEADS, HEAD), query_gain)
        queries = queries.astype(jnp.bfloat16).transpose(1, 0, 2)
        key_rows = rms_scale(jnp.dot(normed, w_key, preferred_element_type=jnp.float32).reshape(LEN, HEADS, HEAD), key_gain)
        key_rows = key_rows.astype(jnp.bfloat16).transpose(1, 0, 2)
        value_rows = jnp.dot(normed, w_value, preferred_element_type=jnp.float32).astype(jnp.bfloat16)
        value_rows = value_rows.reshape(LEN, HEADS, HEAD).transpose(1, 0, 2)

        def attend_head(triple):
            one_query, one_key, one_value = triple
            scores = jnp.dot(one_query, one_key.T, preferred_element_type=jnp.float32) / math.sqrt(HEAD)
            weights = jnp.exp(scores)
            totals = lax.optimization_barrier(jnp.sum(weights, axis=-1, keepdims=True))
            result = jnp.dot(weights.astype(jnp.bfloat16), one_value, preferred_element_type=jnp.float32) / totals
            return result.astype(jnp.bfloat16)
        attended = lax.map(attend_head, (queries, key_rows, value_rows))
        merged = attended.transpose(1, 0, 2).reshape(LEN, HEADS * HEAD)
        projected = jnp.dot(merged, w_out, preferred_element_type=jnp.float32)
        return jnp.dot(hidden + projected, final_wide, precision=lax.Precision.HIGHEST)
    initial = jnp.broadcast_to(start_latent[None], (STEPS, LEN, C)).astype(jnp.float32)
    noise_term = noise_coeff[:, None, None] * noise.astype(jnp.float32)
    step_inputs = initial
    previous = initial
    step_outputs = initial
    errors = jnp.zeros((STEPS,), jnp.float32)
    for iteration in range(ITERS):
        velocity = lax.map(velocity_of, (step_inputs.astype(jnp.bfloat16), temb_all))
        drifts = step_delta[:, None, None] * velocity + noise_term
        step_outputs = start_latent[None] + jnp.cumsum(drifts, axis=0)
        if iteration == ITERS - 1:
            errors = lax.optimization_barrier(jnp.mean((step_outputs - previous) ** 2, axis=(1, 2))) / noise_coeff ** 2
        previous = step_outputs
        step_inputs = step_outputs - drifts
    return (step_outputs, errors)
```

```python
import math

import jax
import jax.numpy as jnp
from jax import lax
from jax.experimental import pallas as pl
from jax.experimental.pallas import tpu as pltpu
from jax.sharding import PartitionSpec as P

NSCHED = 28
EPS = 1e-06
SHIFT = 3.0
ETA = 0.5
MESH = pl.DeviceIdType.MESH
F32 = jnp.float32
BF16 = jnp.bfloat16

D = 3072
C = 64
HEAD = 128
LEN = 1536
HALF = LEN // 2
STEPS = 16
ROWS = 48
SEQ = 32
COLS = 8
QBLK = 256
KBLK = 512


def sigma_of(index):
    fraction = 1.0 - index / NSCHED
    return SHIFT * fraction / (1.0 + (SHIFT - 1.0) * fraction)


def chunk_i(n):
    return 2 * lax.rem(n, 4) + lax.div(n, 8)


def chunk_p(n):
    return lax.rem(lax.div(n, 4), 2)


def seq_of(step, part):
    return 2 * step + lax.rem(step + part, 2)


def chunk_block(n):
    return 4 * lax.rem(n, 8) + lax.div(n, 8)


def split(x):
    hi = x.astype(BF16)
    rest = x - hi.astype(F32)
    mid = rest.astype(BF16)
    low = (rest - mid.astype(F32)).astype(BF16)
    return hi, mid, low


def mm(a, b):
    return jnp.dot(a, b, preferred_element_type=F32)


def kernel(
    ws_ref, start_hbm, noise_hbm, gain_hbm, qg_hbm, kg_hbm,
    wembed_hbm, wtime_hbm, wfinal_hbm, wq_hbm, wk_hbm, wv_hbm, wo_hbm,
    out_ref, err_ref,
    start_ref, noise_ref, gain_ref, qg_ref, kg_ref,
    wtime, wall, fold, left, right, wqkv, cdiag, crow,
    delta_ref, coeff_ref,
    zsrc, yin, slab, nsrc, nin, basesrc, basein,
    latents, heads, red, vsrc, mate, psend, gat, zsend, fin0, fin1, first_sums, esrc, ein,
    ztr, kbuf, qbuf, vbuf,
    wsem, ys, yr, zs, zr, cs, cr, ns, nr, bs, br, us, ur, gs, gr, ps, pr, fs, fr, es, er, ms, mr,
):
    i = lax.axis_index("step")
    j = lax.axis_index("seq")
    x = lax.div(i, 2)
    c = lax.rem(i, 2)
    z = lax.div(j, 4)
    y = lax.rem(j, 4)
    s = lax.div(j, 2)
    p = lax.rem(j + s, 2)
    pos = 4 * (2 * c + p) + x
    own_chunk = 8 * lax.rem(y, 2) + z
    half = lax.div(y, 2)
    source_i = chunk_i(own_chunk)
    source_p = chunk_p(own_chunk)
    first_block = chunk_block(pos)
    low_lanes = lax.broadcasted_iota(jnp.int32, (ROWS, 128), 1) < C

    def rows_of(n):
        return pl.ds(pl.multiple_of(n * ROWS, 16), ROWS)

    def push(src, dst, send, recv, to_i, to_j):
        pltpu.make_async_remote_copy(
            src_ref=src, dst_ref=dst, send_sem=send, recv_sem=recv,
            device_id=(to_i, to_j), device_id_type=MESH,
        ).start()

    def await_bytes(like, sem):
        pltpu.make_async_copy(like, like, sem).wait()

    def loop(low, high, fn):
        def body(k, carry):
            fn(k)
            return carry
        lax.fori_loop(low, high, body, 0)

    def each(low, high, fn):
        for k in range(low, high):
            fn(k)

    def group(fn):
        def one(k):
            n = lax.rem(pos + k, STEPS)
            fn(n, chunk_i(n), seq_of(s, chunk_p(n)))
        each(1, STEPS, one)

    zp = latents.at[0]
    zp2 = latents.at[1]

    head = pl.multiple_of(p * HEAD, HEAD)
    pairs = [
        (start_hbm, start_ref), (noise_hbm, noise_ref), (wtime_hbm, wtime), (wembed_hbm, left.at[0:64, :]),
        (gain_hbm, gain_ref), (wembed_hbm, right.at[128:192, :]), (wfinal_hbm, right.at[0:64, :]),
        (wfinal_hbm, right.at[64:128, :]), (wo_hbm.at[pl.ds(head, HEAD), :], left.at[112:240, :]),
        (qg_hbm, qg_ref), (kg_hbm, kg_ref),
    ] + [
        (w.at[:, pl.ds(head, HEAD)], wall.at[:, n * HEAD:(n + 1) * HEAD]) for n, w in enumerate((wq_hbm, wk_hbm, wv_hbm))
    ]
    local = [pltpu.make_async_copy(src, dst, wsem.at[n]) for n, (src, dst) in enumerate(pairs)]
    for copy in local:
        copy.start()

    barrier = pltpu.get_barrier_semaphore()

    def greet(to_i, to_j):
        pl.semaphore_signal(barrier, inc=1, device_id=(to_i, to_j), device_id_type=MESH)

    group(lambda n, ti, tj: greet(ti, tj))
    each(1, 4, lambda k: greet(i, 4 * z + lax.rem(y + k, 4)))
    each(1, 8, lambda k: greet(i, 4 * lax.rem(z + k, 8) + y))
    base_j = [seq_of(2 * i + n, source_p) for n in range(2)]
    base_mine = [jnp.logical_and(source_i == i, tj == j) for tj in base_j]
    from_j = [first_block + 2 * n for n in range(2)]
    from_i = lax.div(s, 2)
    from_mine = [jnp.logical_and(from_i == i, tj == j) for tj in from_j]
    for n in range(2):
        @pl.when(jnp.logical_not(from_mine[n]))
        def _():
            greet(from_i, from_j[n])

    local[0].wait()
    z0 = start_ref[...]
    start_dup = jnp.concatenate([z0, z0], axis=1)
    zsrc[...] = start_dup.astype(BF16)
    yin[y] = start_dup.astype(BF16)
    local[1].wait()
    packed_noise = jnp.concatenate([noise_ref[0], noise_ref[1]], axis=1)
    nsrc[...] = packed_noise
    nin[i] = packed_noise

    first = ws_ref[0]
    index = (lax.broadcasted_iota(jnp.int32, (STEPS, 128), 0) + first).astype(F32)
    sigma_now = sigma_of(index)
    delta = sigma_of(index + 1.0) - sigma_now
    coeff = ETA * jnp.sqrt(-delta)
    delta_ref[...] = delta
    coeff_ref[...] = coeff
    own = sigma_of((jnp.zeros((STEPS, 128), jnp.int32) + (first + s)).astype(F32))
    lane = lax.broadcasted_iota(jnp.int32, (STEPS, 128), 1).astype(F32)
    angle = 1000.0 * own * jnp.exp(-math.log(10000.0) * lane / 128)
    feats = jnp.concatenate([jnp.cos(angle), jnp.sin(angle)], axis=1)
    feats = (feats / (1.0 + jnp.exp(-feats))).astype(BF16)
    right[192:256] = jnp.zeros((64, D), BF16)
    for n in range(2):
        ztr[128 * n + 64:128 * n + 128] = jnp.where(
            lax.broadcasted_iota(jnp.int32, (64, LEN), 0) == 0, 1.0, 0.0).astype(BF16)
    vbuf[C:C + 16] = jnp.ones((16, LEN), BF16)

    for copy in local[3:5]:
        copy.wait()
    local[2].wait()
    temb = mm(feats, wtime[...])

    alone_count = base_mine[0].astype(jnp.int32) + base_mine[1].astype(jnp.int32)
    pl.semaphore_wait(barrier, 15 + 3 + 7 + 2 - alone_count)

    each(1, 4, lambda k: push(zsrc, yin.at[y], ys, yr, i, 4 * z + lax.rem(y + k, 4)))
    each(1, COLS, lambda k: push(nsrc, nin.at[i], ns, nr, lax.rem(i + k, COLS), j))

    emb = left[0:64].astype(F32)
    gain = gain_ref[...]
    for n, part in enumerate(split(jnp.concatenate([emb * gain, temb * gain], axis=0))):
        fold[n * 80:(n + 1) * 80] = part
    for n, part in enumerate(split(temb)):
        left[64 + 16 * n:80 + 16 * n] = part
    t_row = temb[0:1]
    twice_et = 2.0 * jnp.sum(emb * t_row, axis=1, keepdims=True)
    t_square = jnp.sum(t_row * t_row, axis=1, keepdims=True)

    await_bytes(yin.at[0:3], yr)
    slab_now = jnp.where(low_lanes, yin[c].astype(F32), yin[c + 2].astype(F32)).astype(BF16)
    slab[...] = slab_now
    slab_rows = rows_of(8 * c + z)
    zp[slab_rows, :] = slab_now
    each(1, 8, lambda k: push(slab, zp.at[slab_rows, :], zs, zr, i, 4 * lax.rem(z + k, 8) + y))

    for copy in local[5:]:
        copy.wait()
    folded = mm(fold[...], wall[...])
    folded = folded[0:80] + folded[80:160] + folded[160:240]
    both = lax.dot_general(left[...], right[...], (((1,), (1,)), ((), ())), preferred_element_type=F32)
    cdup = both[0:64, 0:128]
    gram = both[0:64, 128:256]
    mout = both[112:240, 0:128]
    lanes64 = lax.broadcasted_iota(jnp.int32, (64, 128), 1)
    diag = jnp.concatenate([jnp.where(lanes64 < C, cdup, 0.0), jnp.where(lanes64 < C, 0.0, cdup)], axis=0)
    for n, part in enumerate(split(diag)):
        cdiag[n * 128:(n + 1) * 128] = part
    crow[...] = (both[64:72, 0:128] + both[80:88, 0:128] + both[96:104, 0:128])

    await_bytes(zp.at[0:7 * ROWS, :], zr)
    core_rows = pl.ds(pl.multiple_of(8 * ROWS * c, 16), 8 * ROWS)
    push(zp.at[core_rows, :], zp.at[core_rows, :], cs, cr, i + 1 - 2 * c, j)

    value_fold = jnp.dot(folded[:, 256:384], mout, precision=lax.Precision.HIGHEST, preferred_element_type=F32)
    wide = jnp.concatenate([folded[:, 0:256], value_fold], axis=1)
    wide = jnp.concatenate([wide, jnp.zeros((48, 384), F32)], axis=0).T
    wide = jnp.concatenate([wide[0:320], jnp.where(lanes64 == C, twice_et, gram)], axis=0)
    whi = wide.astype(BF16)
    wqkv[:, 0:128] = whi
    wqkv[:, 128:256] = (wide - whi.astype(F32)).astype(BF16)
    scale_row = qg_ref[...] * kg_ref[...] * (math.log2(math.e) / math.sqrt(HEAD))
    scale_col = jnp.broadcast_to(scale_row, (128, 128)).T[:, 0:1]

    step_row = lax.broadcasted_iota(jnp.int32, (STEPS, 128), 0)
    coeff_even = jnp.sum(jnp.where(step_row == 2 * i, coeff, 0.0), axis=0, keepdims=True)
    coeff_odd = jnp.sum(jnp.where(step_row == 2 * i + 1, coeff, 0.0), axis=0, keepdims=True)

    def send_base():
        await_bytes(nin.at[0:COLS - 1], nr)

        def noise_of(step_pair):
            both = nin[step_pair].astype(F32)
            turned = pltpu.roll(both, C, 1)
            return jnp.where(low_lanes, both, turned), jnp.where(low_lanes, turned, both)

        base = start_dup
        for pair in range(COLS):
            even, odd = noise_of(pair)
            pair_sum = coeff_ref[2 * pair:2 * pair + 1] * even + coeff_ref[2 * pair + 1:2 * pair + 2] * odd
            base = base + jnp.where(pair < i, pair_sum, 0.0)
        own_even, own_odd = noise_of(i)
        after_even = base + coeff_even * own_even
        after_odd = after_even + coeff_odd * own_odd
        basesrc[0] = base
        basesrc[1] = after_even
        basesrc[2] = after_odd
        for n in range(2):
            @pl.when(base_mine[n])
            def _():
                basein[half] = basesrc[n]

            @pl.when(jnp.logical_not(base_mine[n]))
            def _():
                push(basesrc.at[n], basein.at[half], bs.at[n], br.at[half], source_i, base_j[n])

    def attend(lap):
        packed = latents[lap].T
        zb = jnp.concatenate([packed[0:64], packed[64:128]], axis=1)
        ztr[0:64] = zb
        ztr[128:192] = zb

        def project(n):
            cols = pl.ds(pl.multiple_of(n * KBLK, KBLK), KBLK)
            out = mm(wqkv[...], ztr[:, cols])
            yq, yk, yv, yg = out[0:128], out[128:256], out[256:320], out[320:384]
            mean_square = (jnp.sum(ztr[0:64, cols].astype(F32) * yg, axis=0, keepdims=True) + t_square) * (1.0 / D)
            square = jnp.maximum(mean_square, 0.0) + EPS
            aq = lax.rsqrt(jnp.mean(yq * yq, axis=0, keepdims=True) + EPS * square)
            ak = lax.rsqrt(jnp.mean(yk * yk, axis=0, keepdims=True) + EPS * square)
            qbuf[:, cols] = (yq * aq * scale_col).astype(BF16)
            kbuf[cols, :] = (yk * ak).astype(BF16).T
            vbuf[0:C, cols] = (yv * lax.rsqrt(square)).astype(BF16)

        loop(0, LEN // KBLK, project)

        def send(n):
            @pl.when(n != pos)
            def _():
                push(heads.at[lap, rows_of(n), :], red.at[lap, pos], us.at[lap], ur.at[lap], chunk_i(n), seq_of(s, chunk_p(n)))

        def block_of(block):
            outs = []
            for side in range(2):
                q = qbuf[:, pl.ds(pl.multiple_of(side * HALF + block * QBLK, QBLK), QBLK)]
                acc = jnp.zeros((C + 16, QBLK), F32)
                for m in range(LEN // KBLK):
                    weights = jnp.exp2(mm(kbuf[m * KBLK:(m + 1) * KBLK], q))
                    acc = acc + mm(vbuf[:, m * KBLK:(m + 1) * KBLK], weights.astype(BF16))
                outs.append(acc[0:C] / acc[C:C + 1])
            done = pl.ds(pl.multiple_of(block * QBLK, QBLK), QBLK)
            heads[lap, done, :] = jnp.concatenate(outs, axis=0).astype(BF16).T
            each(0, 5, lambda m: send(5 * block + m))

            @pl.when(block == 2)
            def _():
                send(15)

        loop(0, 3, block_of)

    def reduce_heads(lap):
        chunk = rows_of(pos)
        red[lap, pos] = heads[lap, chunk, :]
        latent = latents[lap, chunk, :]
        total = mm(jnp.concatenate([latent, latent, latent], axis=1), cdiag[...]) + crow[0:1]
        await_bytes(red.at[lap, 0:STEPS - 1], ur.at[lap])
        for h in range(STEPS):
            total = total + red[lap, h].astype(F32)
        total = total.astype(BF16)
        vsrc[lap] = total
        return total

    first_i = lax.div(s, 2)

    def owner_case(k):
        to_i = k // 2
        to_j = first_block + 2 * (k % 2)
        mine = jnp.logical_and(to_i == i, to_j == j)
        wanted = to_i >= first_i
        return to_i, to_j, jnp.logical_and(wanted, mine), jnp.logical_and(wanted, jnp.logical_not(mine))

    def to_owners(src, dst, n):
        def one(k):
            to_i, to_j, here, there = owner_case(k)

            @pl.when(here)
            def _():
                dst[s] = src[...]

            @pl.when(there)
            def _():
                push(src, dst.at[s], fs.at[n, k], fr.at[n], to_i, to_j)
        each(0, 16, one)

    def owners_sent(src, n):
        def one(k):
            @pl.when(owner_case(k)[3])
            def _():
                await_bytes(src, fs.at[n, k])
        each(0, 16, one)

    alone = jnp.logical_and(own_chunk == pos, first_i <= i)

    def owner_sums(dst, n):
        for pair in range(COLS):
            for own in range(2):
                @pl.when(jnp.logical_and(i == pair, alone == (own == 1)))
                def _():
                    await_bytes(dst.at[0:2 * pair + 2 - own], fr.at[n])
        even = jnp.zeros((ROWS, 128), F32)
        odd = even
        for k in range(STEPS):
            later = delta_ref[k:k + 1] * dst[k].astype(F32)
            even = even + jnp.where(k <= 2 * i, later, 0.0)
            odd = odd + jnp.where(k == 2 * i + 1, later, 0.0)
        return even, even + odd

    chunk = rows_of(pos)
    await_bytes(zp.at[0:8 * ROWS, :], cr)

    def iteration(lap):
        attend(lap)

        @pl.when(lap == 0)
        def _():
            send_base()

        @pl.when(lap == 1)
        def _():
            first_sums[0], first_sums[1] = owner_sums(fin0, 0)

        velocity = reduce_heads(lap)

        @pl.when(lap == 0)
        def _():
            even = lax.rem(s, 2) == 0
            partner = seq_of(s + 1 - 2 * lax.rem(s, 2), p)
            push(vsrc.at[0], mate, ms, mr, i, partner)
            delta_low = jnp.sum(jnp.where(step_row == 2 * z, delta, 0.0), axis=0, keepdims=True)
            delta_high = jnp.sum(jnp.where(step_row == 2 * z + 1, delta, 0.0), axis=0, keepdims=True)
            mine = vsrc[0].astype(F32)
            await_bytes(mate, mr)
            other = mate[...].astype(F32)
            low = delta_low * jnp.where(even, mine, other)
            pair = (low + delta_high * jnp.where(even, other, mine)).astype(BF16)
            gat[z] = pair
            psend[...] = pair
            each(1, 8, lambda k: push(psend, gat.at[z], gs, gr, i, 4 * lax.rem(z + k, 8) + y))
            for n in range(2):
                @pl.when(jnp.logical_not(from_mine[n]))
                def _():
                    await_bytes(basein.at[n], br.at[n])
            latent = jnp.where(low_lanes, basein[0], basein[1]) + jnp.where(even, 0.0, low)
            await_bytes(gat.at[0:7], gr)
            for n in range(8):
                latent = latent + jnp.where(n < z, gat[n].astype(F32), 0.0)
            latent = latent.astype(BF16)
            zsend[...] = latent
            zp2[chunk, :] = latent
            group(lambda n, ti, tj: push(zsend, zp2.at[chunk, :], ps, pr, ti, tj))
            to_owners(vsrc.at[0], fin0, 0)
            await_bytes(zp2.at[0:15 * ROWS, :], pr)

    loop(0, 2, iteration)
    to_owners(vsrc.at[1], fin1, 1)

    keep = low_lanes == (half == 0)
    even, odd = owner_sums(fin1, 1)
    change_even = even - first_sums[0]
    change_odd = odd - first_sums[1]
    row = lax.broadcasted_iota(jnp.int32, (2, 128), 0)
    sum_even = jnp.sum(jnp.where(keep, change_even * change_even, 0.0), axis=0, keepdims=True)
    sum_odd = jnp.sum(jnp.where(keep, change_odd * change_odd, 0.0), axis=0, keepdims=True)
    partial = jnp.where(row == 0, sum_even, sum_odd)
    esrc[0] = partial
    ein[z] = partial
    each(1, 8, lambda k: push(esrc.at[0], ein.at[z], es.at[0], er.at[0], i, 4 * lax.rem(z + k, 8) + y))
    for n, total in enumerate((basesrc[1] + even, basesrc[2] + odd)):
        out_ref[n] = jnp.where(half == 0, total, pltpu.roll(total, C, 1))[:, 0:C]
    await_bytes(ein.at[0:7], er.at[0])
    total = ein[0]
    for n in range(1, 8):
        total = total + ein[n]
    esrc[1] = total
    ein[8 + y] = total
    each(1, 4, lambda k: push(esrc.at[1], ein.at[8 + y], es.at[1], er.at[1], i, 4 * z + lax.rem(y + k, 4)))
    await_bytes(ein.at[8:11], er.at[1])
    total = (ein[8] + ein[9]) + (ein[10] + ein[11])
    total = total * (1.0 / (LEN * C))
    err_ref[0] = jnp.sum(total[0:1] / (coeff_even * coeff_even))
    err_ref[1] = jnp.sum(total[1:2] / (coeff_odd * coeff_odd))

    await_bytes(ein.at[0:7], es.at[0])
    await_bytes(ein.at[8:11], es.at[1])
    await_bytes(mate, ms)
    await_bytes(red.at[0, 0:STEPS - 1], us.at[0])
    await_bytes(red.at[1, 0:STEPS - 1], us.at[1])
    await_bytes(gat.at[0:7], gs)
    await_bytes(zp2.at[0:15 * ROWS, :], ps)
    owners_sent(vsrc.at[0], 0)
    owners_sent(vsrc.at[1], 1)
    await_bytes(yin.at[0:3], ys)
    await_bytes(nin.at[0:COLS - 1], ns)
    await_bytes(zp.at[0:7 * ROWS, :], zs)
    await_bytes(zp.at[0:8 * ROWS, :], cs)
    for n in range(2):
        @pl.when(jnp.logical_not(base_mine[n]))
        def _():
            await_bytes(basesrc.at[n], bs.at[n])


def per_device(
    start_latent, noise, window_start, w_embed, w_time, norm_gain, w_query, w_key, w_value, query_gain, key_gain, w_out, w_final,
):
    vmem = pl.BlockSpec(memory_space=pltpu.VMEM)
    hbm = pl.BlockSpec(memory_space=pltpu.HBM)
    smem = pl.BlockSpec(memory_space=pltpu.SMEM)
    dma = pltpu.SemaphoreType.DMA
    out, errors = pl.pallas_call(
        kernel,
        out_shape=(
            pltpu.VMEM((2, ROWS, C), F32),
            pltpu.SMEM((2,), F32),
        ),
        in_specs=[smem] + [hbm] * 12,
        out_specs=(vmem, smem),
        scratch_shapes=[
            pltpu.VMEM((ROWS, C), F32),
            pltpu.VMEM((2, ROWS, C), BF16),
            pltpu.VMEM((1, D), F32),
            pltpu.VMEM((1, HEAD), F32),
            pltpu.VMEM((1, HEAD), F32),
            pltpu.VMEM((256, D), BF16),
            pltpu.VMEM((D, 3 * HEAD), BF16),
            pltpu.VMEM((240, D), BF16),
            pltpu.VMEM((240, D), BF16),
            pltpu.VMEM((256, D), BF16),
            pltpu.VMEM((384, 256), BF16),
            pltpu.VMEM((384, 128), BF16),
            pltpu.VMEM((8, 128), F32),
            pltpu.VMEM((STEPS, 128), F32),
            pltpu.VMEM((STEPS, 128), F32),
            pltpu.VMEM((ROWS, 128), BF16),
            pltpu.VMEM((4, ROWS, 128), BF16),
            pltpu.VMEM((ROWS, 128), BF16),
            pltpu.VMEM((ROWS, 128), BF16),
            pltpu.VMEM((COLS, ROWS, 128), BF16),
            pltpu.VMEM((3, ROWS, 128), F32),
            pltpu.VMEM((2, ROWS, 128), F32),
            pltpu.VMEM((2, HALF, 128), BF16),
            pltpu.VMEM((2, HALF, 128), BF16),
            pltpu.VMEM((2, STEPS, ROWS, 128), BF16),
            pltpu.VMEM((2, ROWS, 128), BF16),
            pltpu.VMEM((ROWS, 128), BF16),
            pltpu.VMEM((ROWS, 128), BF16),
            pltpu.VMEM((8, ROWS, 128), BF16),
            pltpu.VMEM((ROWS, 128), BF16),
            pltpu.VMEM((STEPS, ROWS, 128), BF16),
            pltpu.VMEM((STEPS, ROWS, 128), BF16),
            pltpu.VMEM((2, ROWS, 128), F32),
            pltpu.VMEM((2, 2, 128), F32),
            pltpu.VMEM((12, 2, 128), F32),
            pltpu.VMEM((256, LEN), BF16),
            pltpu.VMEM((LEN, HEAD), BF16),
            pltpu.VMEM((HEAD, LEN), BF16),
            pltpu.VMEM((C + 16, LEN), BF16),
            dma((14,)),
            dma, dma, dma, dma, dma, dma, dma, dma, dma((2,)), dma((2,)),
            dma((2,)), dma((2,)), dma, dma, dma, dma, dma((2, STEPS)), dma((2,)), dma((2,)), dma((2,)), dma, dma,
        ],
        compiler_params=pltpu.CompilerParams(
            collective_id=0, has_side_effects=True, vmem_limit_bytes=56 * 1024 * 1024),
    )(
        window_start, start_latent, noise, norm_gain.reshape(1, D), query_gain.reshape(1, HEAD), key_gain.reshape(1, HEAD),
        w_embed, w_time, w_final.T, w_query, w_key, w_value, w_out,
    )
    return out, errors


def solution(mesh):
    return jax.shard_map(
        per_device,
        mesh=mesh,
        in_specs=(
            P("seq", None), P("step", "seq", None), P(), P(), P(), P(),
            P(None, "step"), P(None, "step"), P(None, "step"), P(), P(), P("step", None), P(),
        ),
        out_specs=(P("step", "seq", None), P("step")),
        check_vma=False,
    )
```

```python
import math

import jax
import jax.numpy as jnp
from jax import lax
from jax.experimental import pallas as pl
from jax.experimental.pallas import tpu as pltpu
from jax.sharding import PartitionSpec as P

NSCHED = 28
EPS = 1e-06
SHIFT = 3.0
ETA = 0.5
MESH = pl.DeviceIdType.MESH
F32 = jnp.float32
BF16 = jnp.bfloat16

D = 3072
C = 64
HEAD = 128
LEN = 1536
HALF = LEN // 2
STEPS = 16
ROWS = 48
SEQ = 32
COLS = 8
QBLK = 256
KBLK = 512


def sigma_of(index):
    fraction = 1.0 - index / NSCHED
    return SHIFT * fraction / (1.0 + (SHIFT - 1.0) * fraction)


def chunk_i(n):
    return 2 * lax.rem(n, 4) + lax.div(n, 8)


def chunk_p(n):
    return lax.rem(lax.div(n, 4), 2)


def seq_of(step, part):
    return 2 * step + lax.rem(step + part, 2)


def chunk_block(n):
    return 4 * lax.rem(n, 8) + lax.div(n, 8)


def split(x):
    hi = x.astype(BF16)
    rest = x - hi.astype(F32)
    mid = rest.astype(BF16)
    low = (rest - mid.astype(F32)).astype(BF16)
    return hi, mid, low


def mm(a, b):
    return jnp.dot(a, b, preferred_element_type=F32)


def kernel(
    ws_ref, start_hbm, noise_hbm, gain_hbm, qg_hbm, kg_hbm,
    wembed_hbm, wtime_hbm, wfinal_hbm, wq_hbm, wk_hbm, wv_hbm, wo_hbm,
    out_ref, err_ref,
    start_ref, noise_ref, gain_ref, qg_ref, kg_ref,
    wtime, wall, fold, left, right, wqkv, cdiag, crow,
    delta_ref, coeff_ref,
    zsrc, yin, slab, nsrc, nin, basesrc, basein,
    latents, heads, red, vsrc, vpack, mate, psend, gat, zsend, fin0, fin1, first_sums, esrc, ein,
    ztr, kbuf, qbuf, vbuf,
    wsem, ys, yr, zs, zr, cs, cr, ns, nr, bs, br, us, ur, gs, gr, ps, pr, fs, fr, es, er, ms, mr,
):
    i = lax.axis_index("step")
    j = lax.axis_index("seq")
    x = lax.div(i, 2)
    c = lax.rem(i, 2)
    z = lax.div(j, 4)
    y = lax.rem(j, 4)
    s = lax.div(j, 2)
    p = lax.rem(j + s, 2)
    pos = 4 * (2 * c + p) + x
    own_chunk = 8 * lax.rem(y, 2) + z
    half = lax.div(y, 2)
    source_i = chunk_i(own_chunk)
    source_p = chunk_p(own_chunk)
    first_block = chunk_block(pos)
    low_lanes = lax.broadcasted_iota(jnp.int32, (ROWS, 128), 1) < C

    def rows_of(n):
        return pl.ds(pl.multiple_of(n * 16, 16), 16)

    def push(src, dst, send, recv, to_i, to_j):
        pltpu.make_async_remote_copy(
            src_ref=src, dst_ref=dst, send_sem=send, recv_sem=recv,
            device_id=(to_i, to_j), device_id_type=MESH,
        ).start()

    def await_bytes(like, sem):
        pltpu.make_async_copy(like, like, sem).wait()

    def loop(low, high, fn):
        def body(k, carry):
            fn(k)
            return carry
        lax.fori_loop(low, high, body, 0)

    def each(low, high, fn):
        for k in range(low, high):
            fn(k)

    def group(fn):
        def one(k):
            n = lax.rem(pos + k, STEPS)
            fn(n, chunk_i(n), seq_of(s, chunk_p(n)))
        each(1, STEPS, one)

    zp = latents.at[0]
    zp2 = latents.at[1]

    head = pl.multiple_of(p * HEAD, HEAD)
    pairs = [
        (start_hbm, start_ref), (noise_hbm, noise_ref), (wtime_hbm, wtime), (wembed_hbm, left.at[0:64, :]),
        (gain_hbm, gain_ref), (wembed_hbm, right.at[128:192, :]), (wfinal_hbm, right.at[0:64, :]),
        (wfinal_hbm, right.at[64:128, :]), (wo_hbm.at[pl.ds(head, HEAD), :], left.at[112:240, :]),
        (qg_hbm, qg_ref), (kg_hbm, kg_ref),
    ] + [
        (w.at[:, pl.ds(head, HEAD)], wall.at[:, n * HEAD:(n + 1) * HEAD]) for n, w in enumerate((wq_hbm, wk_hbm, wv_hbm))
    ]
    local = [pltpu.make_async_copy(src, dst, wsem.at[n]) for n, (src, dst) in enumerate(pairs)]
    for copy in local:
        copy.start()

    barrier = pltpu.get_barrier_semaphore()

    def greet(to_i, to_j):
        pl.semaphore_signal(barrier, inc=1, device_id=(to_i, to_j), device_id_type=MESH)

    group(lambda n, ti, tj: greet(ti, tj))
    each(1, 4, lambda k: greet(i, 4 * z + lax.rem(y + k, 4)))
    each(1, 8, lambda k: greet(i, 4 * lax.rem(z + k, 8) + y))
    base_j = [seq_of(2 * i + n, source_p) for n in range(2)]
    base_mine = [jnp.logical_and(source_i == i, tj == j) for tj in base_j]
    from_j = [first_block + 2 * n for n in range(2)]
    from_i = lax.div(s, 2)
    from_mine = [jnp.logical_and(from_i == i, tj == j) for tj in from_j]
    for n in range(2):
        @pl.when(jnp.logical_not(from_mine[n]))
        def _():
            greet(from_i, from_j[n])

    local[0].wait()
    z0 = start_ref[...]
    start_dup = jnp.concatenate([z0, z0], axis=1)
    zsrc[...] = start_dup.astype(BF16)
    yin[y] = start_dup.astype(BF16)
    local[1].wait()
    packed_noise = jnp.concatenate([noise_ref[0], noise_ref[1]], axis=1)
    nsrc[...] = packed_noise
    nin[i] = packed_noise

    first = ws_ref[0]
    index = (lax.broadcasted_iota(jnp.int32, (STEPS, 128), 0) + first).astype(F32)
    sigma_now = sigma_of(index)
    delta = sigma_of(index + 1.0) - sigma_now
    coeff = ETA * jnp.sqrt(-delta)
    delta_ref[...] = delta
    coeff_ref[...] = coeff
    own = sigma_of((jnp.zeros((STEPS, 128), jnp.int32) + (first + s)).astype(F32))
    lane = lax.broadcasted_iota(jnp.int32, (STEPS, 128), 1).astype(F32)
    angle = 1000.0 * own * jnp.exp(-math.log(10000.0) * lane / 128)
    feats = jnp.concatenate([jnp.cos(angle), jnp.sin(angle)], axis=1)
    feats = (feats / (1.0 + jnp.exp(-feats))).astype(BF16)
    right[192:256] = jnp.zeros((64, D), BF16)
    for n in range(2):
        ztr[128 * n + 64:128 * n + 128] = jnp.where(
            lax.broadcasted_iota(jnp.int32, (64, LEN), 0) == 0, 1.0, 0.0).astype(BF16)
    vbuf[C:C + 16] = jnp.ones((16, LEN), BF16)

    for copy in local[3:5]:
        copy.wait()
    local[2].wait()
    temb = mm(feats, wtime[...])

    alone_count = base_mine[0].astype(jnp.int32) + base_mine[1].astype(jnp.int32)
    pl.semaphore_wait(barrier, 15 + 3 + 7 + 2 - alone_count)

    each(1, 4, lambda k: push(zsrc, yin.at[y], ys, yr, i, 4 * z + lax.rem(y + k, 4)))

    emb = left[0:64].astype(F32)
    gain = gain_ref[...]
    for n, part in enumerate(split(jnp.concatenate([emb * gain, temb * gain], axis=0))):
        fold[n * 80:(n + 1) * 80] = part
    for n, part in enumerate(split(temb)):
        left[64 + 16 * n:80 + 16 * n] = part
    t_row = temb[0:1]
    twice_et = 2.0 * jnp.sum(emb * t_row, axis=1, keepdims=True)
    t_square = jnp.sum(t_row * t_row, axis=1, keepdims=True)

    await_bytes(yin.at[0:3], yr)
    slab_now = jnp.where(low_lanes, yin[c].astype(F32), yin[c + 2].astype(F32)).reshape(3, 16, 128).astype(BF16)
    slab[...] = slab_now
    slab_rows = rows_of(8 * c + z)
    zp[:, slab_rows, :] = slab_now
    each(1, 8, lambda k: push(slab, zp.at[:, slab_rows, :], zs, zr, i, 4 * lax.rem(z + k, 8) + y))

    each(1, COLS, lambda k: push(nsrc, nin.at[i], ns, nr, lax.rem(i + k, COLS), j))

    for copy in local[5:]:
        copy.wait()
    folded = mm(fold[...], wall[...])
    folded = folded[0:80] + folded[80:160] + folded[160:240]
    both = lax.dot_general(left[...], right[...], (((1,), (1,)), ((), ())), preferred_element_type=F32)
    cdup = both[0:64, 0:128]
    gram = both[0:64, 128:256]
    mout = both[112:240, 0:128]
    lanes64 = lax.broadcasted_iota(jnp.int32, (64, 128), 1)
    diag = jnp.concatenate([jnp.where(lanes64 < C, cdup, 0.0), jnp.where(lanes64 < C, 0.0, cdup)], axis=0)
    for n, part in enumerate(split(diag)):
        cdiag[n * 128:(n + 1) * 128] = part
    crow[...] = (both[64:72, 0:128] + both[80:88, 0:128] + both[96:104, 0:128])

    await_bytes(zp.at[:, 0:7 * 16, :], zr)
    core_rows = pl.ds(pl.multiple_of(128 * c, 128), 128)
    push(zp.at[:, core_rows, :], zp.at[:, core_rows, :], cs, cr, i + 1 - 2 * c, j)

    value_fold = jnp.dot(folded[:, 256:384], mout, precision=lax.Precision.HIGHEST, preferred_element_type=F32)
    wide = jnp.concatenate([folded[:, 0:256], value_fold], axis=1)
    wide = jnp.concatenate([wide, jnp.zeros((48, 384), F32)], axis=0).T
    wide = jnp.concatenate([wide[0:320], jnp.where(lanes64 == C, twice_et, gram)], axis=0)
    whi = wide.astype(BF16)
    wqkv[:, 0:128] = whi
    wqkv[:, 128:256] = (wide - whi.astype(F32)).astype(BF16)
    scale_row = qg_ref[...] * kg_ref[...] * (math.log2(math.e) / math.sqrt(HEAD))
    scale_col = jnp.broadcast_to(scale_row, (128, 128)).T[:, 0:1]

    step_row = lax.broadcasted_iota(jnp.int32, (STEPS, 128), 0)
    coeff_even = jnp.sum(jnp.where(step_row == 2 * i, coeff, 0.0), axis=0, keepdims=True)
    coeff_odd = jnp.sum(jnp.where(step_row == 2 * i + 1, coeff, 0.0), axis=0, keepdims=True)

    def send_base():
        await_bytes(nin.at[0:COLS - 1], nr)

        def noise_of(step_pair):
            both = nin[step_pair].astype(F32)
            turned = pltpu.roll(both, C, 1)
            return jnp.where(low_lanes, both, turned), jnp.where(low_lanes, turned, both)

        base = start_dup
        for pair in range(COLS):
            even, odd = noise_of(pair)
            pair_sum = coeff_ref[2 * pair:2 * pair + 1] * even + coeff_ref[2 * pair + 1:2 * pair + 2] * odd
            base = base + jnp.where(pair < i, pair_sum, 0.0)
        own_even, own_odd = noise_of(i)
        after_even = base + coeff_even * own_even
        after_odd = after_even + coeff_odd * own_odd
        basesrc[0] = base
        basesrc[1] = after_even
        basesrc[2] = after_odd
        for n in range(2):
            @pl.when(base_mine[n])
            def _():
                basein[half] = basesrc[n]

            @pl.when(jnp.logical_not(base_mine[n]))
            def _():
                push(basesrc.at[n], basein.at[half], bs.at[n], br.at[half], source_i, base_j[n])

    def attend(lap):
        packed = latents[lap].reshape(HALF, 128).T
        zb = jnp.concatenate([packed[0:64], packed[64:128]], axis=1)
        ztr[0:64] = zb
        ztr[128:192] = zb

        def project(n):
            cols = pl.ds(pl.multiple_of(n * KBLK, KBLK), KBLK)
            out = mm(wqkv[...], ztr[:, cols])
            yq, yk, yv, yg = out[0:128], out[128:256], out[256:320], out[320:384]
            mean_square = (jnp.sum(ztr[0:64, cols].astype(F32) * yg, axis=0, keepdims=True) + t_square) * (1.0 / D)
            square = jnp.maximum(mean_square, 0.0) + EPS
            aq = lax.rsqrt(jnp.mean(yq * yq, axis=0, keepdims=True) + EPS * square)
            ak = lax.rsqrt(jnp.mean(yk * yk, axis=0, keepdims=True) + EPS * square)
            qbuf[:, cols] = (yq * aq * scale_col).astype(BF16)
            kbuf[cols, :] = (yk * ak).astype(BF16).T
            vbuf[0:C, cols] = (yv * lax.rsqrt(square)).astype(BF16)

        loop(0, LEN // KBLK, project)

        def block_of(block):
            outs = []
            for side in range(2):
                q = qbuf[:, pl.ds(pl.multiple_of(side * HALF + block * QBLK, QBLK), QBLK)]
                acc = jnp.zeros((C + 16, QBLK), F32)
                for m in range(LEN // KBLK):
                    weights = jnp.exp2(mm(kbuf[m * KBLK:(m + 1) * KBLK], q))
                    acc = acc + mm(vbuf[:, m * KBLK:(m + 1) * KBLK], weights.astype(BF16))
                outs.append(acc[0:C] / acc[C:C + 1])
            heads[lap, block] = jnp.concatenate(outs, axis=0).astype(BF16).T
            group(lambda n, ti, tj: push(
                heads.at[lap, block, rows_of(n), :], red.at[lap, pos, block], us.at[lap], ur.at[lap], ti, tj))

        loop(0, 3, block_of)

    def reduce_heads(lap):
        chunk = rows_of(pos)
        red[lap, pos] = heads[lap, :, chunk, :]
        latent = latents[lap, :, chunk, :].reshape(ROWS, 128)
        total = mm(jnp.concatenate([latent, latent, latent], axis=1), cdiag[...]) + crow[0:1]
        await_bytes(red.at[lap, 0:STEPS - 1], ur.at[lap])
        for h in range(STEPS):
            total = total + red[lap, h].astype(F32).reshape(ROWS, 128)
        vsrc[lap] = total.astype(BF16)
        low = low_lanes[0:16]
        parts = [total[0:16], total[16:32], total[32:48]]
        turned = [pltpu.roll(part, C, 1) for part in parts]
        for side, (first_part, second_part, third_part) in enumerate((
            (parts[0], turned[1], parts[2]), (turned[0], parts[1], turned[2]),
        )):
            vpack[lap, side, 0:16] = jnp.where(low, first_part, second_part).astype(BF16)
            vpack[lap, side, 16:32] = jnp.where(low, third_part, 0.0).astype(BF16)

    first_i = lax.div(s, 2)

    def owner_case(k):
        to_i = k // 2
        to_j = first_block + 2 * (k % 2)
        mine = jnp.logical_and(to_i == i, to_j == j)
        wanted = to_i >= first_i
        return to_i, to_j, jnp.logical_and(wanted, mine), jnp.logical_and(wanted, jnp.logical_not(mine))

    def to_owners(src, dst, n):
        def one(k):
            to_i, to_j, here, there = owner_case(k)

            @pl.when(here)
            def _():
                dst[s] = src[k % 2]

            @pl.when(there)
            def _():
                push(src.at[k % 2], dst.at[s], fs.at[n, k], fr.at[n], to_i, to_j)
        each(0, 16, one)

    def owners_sent(src, n):
        def one(k):
            @pl.when(owner_case(k)[3])
            def _():
                await_bytes(src.at[k % 2], fs.at[n, k])
        each(0, 16, one)

    alone = jnp.logical_and(own_chunk == pos, first_i <= i)

    def owner_sums(dst, n):
        for pair in range(COLS):
            for own in range(2):
                @pl.when(jnp.logical_and(i == pair, alone == (own == 1)))
                def _():
                    await_bytes(dst.at[0:2 * pair + 2 - own], fr.at[n])
        even = jnp.zeros((32, 128), F32)
        odd = even
        for k in range(STEPS):
            later = delta_ref[k:k + 1] * dst[k].astype(F32)
            even = even + jnp.where(k <= 2 * i, later, 0.0)
            odd = odd + jnp.where(k == 2 * i + 1, later, 0.0)
        return even, even + odd

    chunk = rows_of(pos)
    await_bytes(zp.at[:, 0:128, :], cr)

    def iteration(lap):
        attend(lap)

        @pl.when(lap == 0)
        def _():
            send_base()

        @pl.when(lap == 1)
        def _():
            first_sums[0], first_sums[1] = owner_sums(fin0, 0)

        reduce_heads(lap)

        @pl.when(lap == 0)
        def _():
            even = lax.rem(s, 2) == 0
            partner = seq_of(s + 1 - 2 * lax.rem(s, 2), p)
            push(vsrc.at[0], mate, ms, mr, i, partner)
            delta_low = jnp.sum(jnp.where(step_row == 2 * z, delta, 0.0), axis=0, keepdims=True)
            delta_high = jnp.sum(jnp.where(step_row == 2 * z + 1, delta, 0.0), axis=0, keepdims=True)
            mine = vsrc[0].astype(F32)
            await_bytes(mate, mr)
            other = mate[...].astype(F32)
            low = delta_low * jnp.where(even, mine, other)
            pair = (low + delta_high * jnp.where(even, other, mine)).astype(BF16)
            gat[z] = pair
            psend[...] = pair
            each(1, 8, lambda k: push(psend, gat.at[z], gs, gr, i, 4 * lax.rem(z + k, 8) + y))
            for n in range(2):
                @pl.when(jnp.logical_not(from_mine[n]))
                def _():
                    await_bytes(basein.at[n], br.at[n])
            latent = jnp.where(low_lanes, basein[0], basein[1]) + jnp.where(even, 0.0, low)
            await_bytes(gat.at[0:7], gr)
            for n in range(8):
                latent = latent + jnp.where(n < z, gat[n].astype(F32), 0.0)
            latent = latent.reshape(3, 16, 128).astype(BF16)
            zsend[...] = latent
            zp2[:, chunk, :] = latent
            group(lambda n, ti, tj: push(zsend, zp2.at[:, chunk, :], ps, pr, ti, tj))
            to_owners(vpack.at[0], fin0, 0)
            await_bytes(zp2.at[:, 0:15 * 16, :], pr)

    loop(0, 2, iteration)
    to_owners(vpack.at[1], fin1, 1)

    even, odd = owner_sums(fin1, 1)
    change_even = even - first_sums[0]
    change_odd = odd - first_sums[1]

    def unpack(x):
        return jnp.concatenate([x[0:16], pltpu.roll(x[0:16], C, 1), x[16:32]], axis=0)

    row = lax.broadcasted_iota(jnp.int32, (2, 128), 0)
    sum_even = jnp.sum(change_even * change_even, axis=0, keepdims=True)
    sum_odd = jnp.sum(change_odd * change_odd, axis=0, keepdims=True)
    partial = jnp.where(row == 0, sum_even, sum_odd)
    esrc[0] = partial
    ein[z] = partial
    each(1, 8, lambda k: push(esrc.at[0], ein.at[z], es.at[0], er.at[0], i, 4 * lax.rem(z + k, 8) + y))
    for n, total in enumerate((basesrc[1] + unpack(even), basesrc[2] + unpack(odd))):
        out_ref[n] = total[:, 0:C]
    await_bytes(ein.at[0:7], er.at[0])
    total = ein[0]
    for n in range(1, 8):
        total = total + ein[n]
    esrc[1] = total
    ein[8 + y] = total
    each(1, 4, lambda k: push(esrc.at[1], ein.at[8 + y], es.at[1], er.at[1], i, 4 * z + lax.rem(y + k, 4)))
    await_bytes(ein.at[8:11], er.at[1])
    total = (ein[8] + ein[9]) + (ein[10] + ein[11])
    total = total * (1.0 / (LEN * C))
    err_ref[0] = jnp.sum(total[0:1] / (coeff_even * coeff_even))
    err_ref[1] = jnp.sum(total[1:2] / (coeff_odd * coeff_odd))

    await_bytes(ein.at[0:7], es.at[0])
    await_bytes(ein.at[8:11], es.at[1])
    await_bytes(mate, ms)
    await_bytes(red.at[0, 0:STEPS - 1], us.at[0])
    await_bytes(red.at[1, 0:STEPS - 1], us.at[1])
    await_bytes(gat.at[0:7], gs)
    await_bytes(zp2.at[:, 0:15 * 16, :], ps)
    owners_sent(vpack.at[0], 0)
    owners_sent(vpack.at[1], 1)
    await_bytes(yin.at[0:3], ys)
    await_bytes(nin.at[0:COLS - 1], ns)
    await_bytes(zp.at[:, 0:7 * 16, :], zs)
    await_bytes(zp.at[:, 0:128, :], cs)
    for n in range(2):
        @pl.when(jnp.logical_not(base_mine[n]))
        def _():
            await_bytes(basesrc.at[n], bs.at[n])


def per_device(
    start_latent, noise, window_start, w_embed, w_time, norm_gain, w_query, w_key, w_value, query_gain, key_gain, w_out, w_final,
):
    vmem = pl.BlockSpec(memory_space=pltpu.VMEM)
    hbm = pl.BlockSpec(memory_space=pltpu.HBM)
    smem = pl.BlockSpec(memory_space=pltpu.SMEM)
    dma = pltpu.SemaphoreType.DMA
    out, errors = pl.pallas_call(
        kernel,
        out_shape=(
            pltpu.VMEM((2, ROWS, C), F32),
            pltpu.SMEM((2,), F32),
        ),
        in_specs=[smem] + [hbm] * 12,
        out_specs=(vmem, smem),
        scratch_shapes=[
            pltpu.VMEM((ROWS, C), F32),
            pltpu.VMEM((2, ROWS, C), BF16),
            pltpu.VMEM((1, D), F32),
            pltpu.VMEM((1, HEAD), F32),
            pltpu.VMEM((1, HEAD), F32),
            pltpu.VMEM((256, D), BF16),
            pltpu.VMEM((D, 3 * HEAD), BF16),
            pltpu.VMEM((240, D), BF16),
            pltpu.VMEM((240, D), BF16),
            pltpu.VMEM((256, D), BF16),
            pltpu.VMEM((384, 256), BF16),
            pltpu.VMEM((384, 128), BF16),
            pltpu.VMEM((8, 128), F32),
            pltpu.VMEM((STEPS, 128), F32),
            pltpu.VMEM((STEPS, 128), F32),
            pltpu.VMEM((ROWS, 128), BF16),
            pltpu.VMEM((4, ROWS, 128), BF16),
            pltpu.VMEM((3, 16, 128), BF16),
            pltpu.VMEM((ROWS, 128), BF16),
            pltpu.VMEM((COLS, ROWS, 128), BF16),
            pltpu.VMEM((3, ROWS, 128), F32),
            pltpu.VMEM((2, ROWS, 128), F32),
            pltpu.VMEM((2, 3, QBLK, 128), BF16),
            pltpu.VMEM((2, 3, QBLK, 128), BF16),
            pltpu.VMEM((2, STEPS, 3, 16, 128), BF16),
            pltpu.VMEM((2, ROWS, 128), BF16),
            pltpu.VMEM((2, 2, 32, 128), BF16),
            pltpu.VMEM((ROWS, 128), BF16),
            pltpu.VMEM((ROWS, 128), BF16),
            pltpu.VMEM((8, ROWS, 128), BF16),
            pltpu.VMEM((3, 16, 128), BF16),
            pltpu.VMEM((STEPS, 32, 128), BF16),
            pltpu.VMEM((STEPS, 32, 128), BF16),
            pltpu.VMEM((2, 32, 128), F32),
            pltpu.VMEM((2, 2, 128), F32),
            pltpu.VMEM((12, 2, 128), F32),
            pltpu.VMEM((256, LEN), BF16),
            pltpu.VMEM((LEN, HEAD), BF16),
            pltpu.VMEM((HEAD, LEN), BF16),
            pltpu.VMEM((C + 16, LEN), BF16),
            dma((14,)),
            dma, dma, dma, dma, dma, dma, dma, dma, dma((2,)), dma((2,)),
            dma((2,)), dma((2,)), dma, dma, dma, dma, dma((2, STEPS)), dma((2,)), dma((2,)), dma((2,)), dma, dma,
        ],
        compiler_params=pltpu.CompilerParams(
            collective_id=0, has_side_effects=True, vmem_limit_bytes=56 * 1024 * 1024),
    )(
        window_start, start_latent, noise, norm_gain.reshape(1, D), query_gain.reshape(1, HEAD), key_gain.reshape(1, HEAD),
        w_embed, w_time, w_final.T, w_query, w_key, w_value, w_out,
    )
    return out, errors


def solution(mesh):
    return jax.shard_map(
        per_device,
        mesh=mesh,
        in_specs=(
            P("seq", None), P("step", "seq", None), P(), P(), P(), P(),
            P(None, "step"), P(None, "step"), P(None, "step"), P(), P(), P("step", None), P(),
        ),
        out_specs=(P("step", "seq", None), P("step")),
        check_vma=False,
    )
```

```python
import math

import jax
import jax.numpy as jnp
from jax import lax
from jax.experimental import pallas as pl
from jax.experimental.pallas import tpu as pltpu
from jax.sharding import PartitionSpec as P

NSCHED = 28
EPS = 1e-06
SHIFT = 3.0
ETA = 0.5
MESH = pl.DeviceIdType.MESH
F32 = jnp.float32
BF16 = jnp.bfloat16

D = 3072
C = 64
HEAD = 128
LEN = 1536
HALF = LEN // 2
STEPS = 16
ROWS = 48
SEQ = 32
COLS = 8
QBLK = 256
KBLK = 512


def sigma_of(index):
    fraction = 1.0 - index / NSCHED
    return SHIFT * fraction / (1.0 + (SHIFT - 1.0) * fraction)


def chunk_i(n):
    return 2 * lax.rem(n, 4) + lax.div(n, 8)


def chunk_p(n):
    return lax.rem(lax.div(n, 4), 2)


def seq_of(step, part):
    return 2 * step + lax.rem(step + part, 2)


def chunk_block(n):
    return 4 * lax.rem(n, 8) + lax.div(n, 8)


def split(x):
    hi = x.astype(BF16)
    rest = x - hi.astype(F32)
    mid = rest.astype(BF16)
    low = (rest - mid.astype(F32)).astype(BF16)
    return hi, mid, low


def mm(a, b):
    return jnp.dot(a, b, preferred_element_type=F32)


def kernel(
    ws_ref, start_hbm, noise_hbm, gain_hbm, qg_hbm, kg_hbm,
    wembed_hbm, wtime_hbm, wfinal_hbm, wq_hbm, wk_hbm, wv_hbm, wo_hbm,
    out_ref, err_ref,
    start_ref, noise_ref, gain_ref, qg_ref, kg_ref,
    wtime, wall, fold, left, right, wqkv, cdiag, crow,
    delta_ref, coeff_ref,
    zsrc, yin, slab, nsrc, nin, basesrc, basein,
    latents, heads, red, vsrc, vpack, mate, psend, gat, zsend, fin0, fin1, first_sums, esrc, ein,
    ztr, kbuf, qbuf, vbuf,
    wsem, ys, yr, zs, zr, cs, cr, ns, nr, bs, br, us, ur, gs, gr, ps, pr, fs, fr, es, er, ms, mr,
):
    i = lax.axis_index("step")
    j = lax.axis_index("seq")
    x = lax.div(i, 2)
    c = lax.rem(i, 2)
    z = lax.div(j, 4)
    y = lax.rem(j, 4)
    s = lax.div(j, 2)
    p = lax.rem(j + s, 2)
    pos = 4 * (2 * c + p) + x
    own_chunk = 8 * lax.rem(y, 2) + z
    half = lax.div(y, 2)
    source_i = chunk_i(own_chunk)
    source_p = chunk_p(own_chunk)
    first_block = chunk_block(pos)
    low_lanes = lax.broadcasted_iota(jnp.int32, (ROWS, 128), 1) < C

    def rows_of(n):
        return pl.ds(pl.multiple_of(n * 16, 16), 16)

    def push(src, dst, send, recv, to_i, to_j):
        pltpu.make_async_remote_copy(
            src_ref=src, dst_ref=dst, send_sem=send, recv_sem=recv,
            device_id=(to_i, to_j), device_id_type=MESH,
        ).start()

    def await_bytes(like, sem):
        pltpu.make_async_copy(like, like, sem).wait()

    def each(low, high, fn):
        for k in range(low, high):
            fn(k)

    def group(fn):
        def one(k):
            n = lax.rem(pos + k, STEPS)
            fn(n, chunk_i(n), seq_of(s, chunk_p(n)))
        each(1, STEPS, one)

    zp = latents.at[0]

    head = pl.multiple_of(p * HEAD, HEAD)
    pairs = [
        (start_hbm, start_ref), (noise_hbm, noise_ref), (wtime_hbm, wtime), (wembed_hbm, left.at[0:64, :]),
        (gain_hbm, gain_ref), (wembed_hbm, right.at[128:192, :]), (wfinal_hbm, right.at[0:64, :]),
        (wfinal_hbm, right.at[64:128, :]), (wo_hbm.at[pl.ds(head, HEAD), :], left.at[112:240, :]),
        (qg_hbm, qg_ref), (kg_hbm, kg_ref),
    ] + [
        (w.at[:, pl.ds(head, HEAD)], wall.at[:, n * HEAD:(n + 1) * HEAD]) for n, w in enumerate((wq_hbm, wk_hbm, wv_hbm))
    ]
    local = [pltpu.make_async_copy(src, dst, wsem.at[n]) for n, (src, dst) in enumerate(pairs)]
    for copy in local:
        copy.start()

    barrier = pltpu.get_barrier_semaphore()

    def greet(to_i, to_j):
        pl.semaphore_signal(barrier, inc=1, device_id=(to_i, to_j), device_id_type=MESH)

    group(lambda n, ti, tj: greet(ti, tj))
    each(1, 4, lambda k: greet(i, 4 * z + lax.rem(y + k, 4)))
    each(1, 8, lambda k: greet(i, 4 * lax.rem(z + k, 8) + y))
    base_j = [seq_of(2 * i + n, source_p) for n in range(2)]
    base_mine = [jnp.logical_and(source_i == i, tj == j) for tj in base_j]
    from_j = [first_block + 2 * n for n in range(2)]
    from_i = lax.div(s, 2)
    from_mine = [jnp.logical_and(from_i == i, tj == j) for tj in from_j]
    for n in range(2):
        @pl.when(jnp.logical_not(from_mine[n]))
        def _():
            greet(from_i, from_j[n])

    local[0].wait()
    z0 = start_ref[...]
    start_dup = jnp.concatenate([z0, z0], axis=1)
    zsrc[...] = start_dup.astype(BF16)
    yin[y] = start_dup.astype(BF16)
    local[1].wait()
    packed_noise = jnp.concatenate([noise_ref[0], noise_ref[1]], axis=1)
    nsrc[...] = packed_noise
    nin[i] = packed_noise

    alone_count = base_mine[0].astype(jnp.int32) + base_mine[1].astype(jnp.int32)
    pl.semaphore_wait(barrier, 15 + 3 + 7 + 2 - alone_count)

    each(1, 4, lambda k: push(zsrc, yin.at[y], ys, yr, i, 4 * z + lax.rem(y + k, 4)))

    first = ws_ref[0]
    index = (lax.broadcasted_iota(jnp.int32, (STEPS, 128), 0) + first).astype(F32)
    sigma_now = sigma_of(index)
    delta = sigma_of(index + 1.0) - sigma_now
    coeff = ETA * jnp.sqrt(-delta)
    delta_ref[...] = delta
    coeff_ref[...] = coeff
    own = sigma_of((jnp.zeros((STEPS, 128), jnp.int32) + (first + s)).astype(F32))
    lane = lax.broadcasted_iota(jnp.int32, (STEPS, 128), 1).astype(F32)
    angle = 1000.0 * own * jnp.exp(-math.log(10000.0) * lane / 128)
    feats = jnp.concatenate([jnp.cos(angle), jnp.sin(angle)], axis=1)
    feats = (feats / (1.0 + jnp.exp(-feats))).astype(BF16)
    right[192:256] = jnp.zeros((64, D), BF16)
    for n in range(2):
        ztr[128 * n + 64:128 * n + 128] = jnp.where(
            lax.broadcasted_iota(jnp.int32, (64, KBLK), 0) == 0, 1.0, 0.0).astype(BF16)
    vbuf[C:C + 16] = jnp.ones((16, LEN), BF16)

    for copy in local[3:5]:
        copy.wait()
    local[2].wait()
    temb = mm(feats, wtime[...])

    emb = left[0:64].astype(F32)
    gain = gain_ref[...]
    for n, part in enumerate(split(jnp.concatenate([emb * gain, temb * gain], axis=0))):
        fold[n * 80:(n + 1) * 80] = part
    for n, part in enumerate(split(temb)):
        left[64 + 16 * n:80 + 16 * n] = part
    t_row = temb[0:1]
    twice_et = 2.0 * jnp.sum(emb * t_row, axis=1, keepdims=True)
    t_square = jnp.sum(t_row * t_row, axis=1, keepdims=True)

    await_bytes(yin.at[0:3], yr)
    slab_now = jnp.where(low_lanes, yin[c].astype(F32), yin[c + 2].astype(F32)).reshape(3, 16, 128).astype(BF16)
    slab[...] = slab_now
    slab_rows = rows_of(8 * c + z)
    zp[:, slab_rows, :] = slab_now
    each(1, 8, lambda k: push(slab, zp.at[:, slab_rows, :], zs, zr, i, 4 * lax.rem(z + k, 8) + y))

    each(1, COLS, lambda k: push(nsrc, nin.at[i], ns, nr, lax.rem(i + k, COLS), j))

    for copy in local[5:]:
        copy.wait()
    folded = mm(fold[...], wall[...])
    folded = folded[0:80] + folded[80:160] + folded[160:240]
    both = lax.dot_general(left[...], right[...], (((1,), (1,)), ((), ())), preferred_element_type=F32)
    cdup = both[0:64, 0:128]
    gram = both[0:64, 128:256]
    mout = both[112:240, 0:128]
    lanes64 = lax.broadcasted_iota(jnp.int32, (64, 128), 1)
    diag = jnp.concatenate([jnp.where(lanes64 < C, cdup, 0.0), jnp.where(lanes64 < C, 0.0, cdup)], axis=0)
    for n, part in enumerate(split(diag)):
        cdiag[n * 128:(n + 1) * 128] = part
    crow[...] = (both[64:72, 0:128] + both[80:88, 0:128] + both[96:104, 0:128])

    await_bytes(zp.at[:, 0:7 * 16, :], zr)
    core_rows = pl.ds(pl.multiple_of(128 * c, 128), 128)
    push(zp.at[:, core_rows, :], zp.at[:, core_rows, :], cs, cr, i + 1 - 2 * c, j)

    value_fold = jnp.dot(folded[:, 256:384], mout, precision=lax.Precision.HIGHEST, preferred_element_type=F32)
    wide = jnp.concatenate([folded[:, 0:256], value_fold], axis=1)
    wide = jnp.concatenate([wide, jnp.zeros((48, 384), F32)], axis=0).T
    wide = jnp.concatenate([wide[0:320], jnp.where(lanes64 == C, twice_et, gram)], axis=0)
    whi = wide.astype(BF16)
    wqkv[:, 0:128] = whi
    wqkv[:, 128:256] = (wide - whi.astype(F32)).astype(BF16)
    scale_row = qg_ref[...] * kg_ref[...] * (math.log2(math.e) / math.sqrt(HEAD))
    scale_col = jnp.broadcast_to(scale_row, (128, 128)).T[:, 0:1]

    step_row = lax.broadcasted_iota(jnp.int32, (STEPS, 128), 0)
    coeff_even = jnp.sum(jnp.where(step_row == 2 * i, coeff, 0.0), axis=0, keepdims=True)
    coeff_odd = jnp.sum(jnp.where(step_row == 2 * i + 1, coeff, 0.0), axis=0, keepdims=True)

    def send_base():
        await_bytes(nin.at[0:COLS - 1], nr)

        def noise_of(step_pair):
            both = nin[step_pair].astype(F32)
            turned = pltpu.roll(both, C, 1)
            return jnp.where(low_lanes, both, turned), jnp.where(low_lanes, turned, both)

        base = start_dup
        for pair in range(COLS):
            even, odd = noise_of(pair)
            pair_sum = coeff_ref[2 * pair:2 * pair + 1] * even + coeff_ref[2 * pair + 1:2 * pair + 2] * odd
            base = base + jnp.where(pair < i, pair_sum, 0.0)
        own_even, own_odd = noise_of(i)
        after_even = base + coeff_even * own_even
        after_odd = after_even + coeff_odd * own_odd
        basesrc[0] = base
        basesrc[1] = after_even
        basesrc[2] = after_odd
        for n in range(2):
            @pl.when(base_mine[n])
            def _():
                basein[half] = basesrc[n]

            @pl.when(jnp.logical_not(base_mine[n]))
            def _():
                push(basesrc.at[n], basein.at[half], bs.at[n], br.at[half], source_i, base_j[n])

    chunk = rows_of(pos)
    low = low_lanes[0:16]

    def project(lap, n):
        packed = latents[lap, n].T
        zb = jnp.concatenate([packed[0:64], packed[64:128]], axis=1)
        ztr[0:64] = zb
        ztr[128:192] = zb
        cols = slice(n * KBLK, (n + 1) * KBLK)
        out = mm(wqkv[...], ztr[...])
        yq, yk, yv, yg = out[0:128], out[128:256], out[256:320], out[320:384]
        mean_square = (jnp.sum(zb.astype(F32) * yg, axis=0, keepdims=True) + t_square) * (1.0 / D)
        square = jnp.maximum(mean_square, 0.0) + EPS
        aq = lax.rsqrt(jnp.mean(yq * yq, axis=0, keepdims=True) + EPS * square)
        ak = lax.rsqrt(jnp.mean(yk * yk, axis=0, keepdims=True) + EPS * square)
        qbuf[:, cols] = (yq * aq * scale_col).astype(BF16)
        kbuf[cols, :] = (yk * ak).astype(BF16).T
        vbuf[0:C, cols] = (yv * lax.rsqrt(square)).astype(BF16)

    def attend(block, keys, accs):
        out = []
        for side in range(2):
            q = qbuf[:, block * KBLK + side * QBLK:block * KBLK + (side + 1) * QBLK]
            acc = accs[side]
            for m in keys:
                weights = jnp.exp2(mm(kbuf[m * KBLK:(m + 1) * KBLK], q))
                part = mm(vbuf[:, m * KBLK:(m + 1) * KBLK], weights.astype(BF16))
                acc = part if acc is None else acc + part
            out.append(acc)
        return out

    def finish(lap, block, accs):
        outs = [acc[0:C] / acc[C:C + 1] for acc in accs]
        heads[lap, block] = jnp.concatenate(outs, axis=0).astype(BF16).T
        group(lambda n, ti, tj: push(
            heads.at[lap, block, rows_of(n), :], red.at[lap, block, pos], us.at[lap], ur.at[lap, block], ti, tj))

    def reduce_heads(lap, block):
        red[lap, block, pos] = heads[lap, block, chunk, :]
        latent = latents[lap, block, chunk, :]
        total = mm(jnp.concatenate([latent, latent, latent], axis=1), cdiag[...]) + crow[0:1]
        await_bytes(red.at[lap, block, 0:STEPS - 1], ur.at[lap, block])
        for h in range(STEPS):
            total = total + red[lap, block, h].astype(F32)
        return total

    def pack_first(lap, first_part, second_part):
        vpack[lap, 0, 0:16] = jnp.where(low, first_part, pltpu.roll(second_part, C, 1)).astype(BF16)
        vpack[lap, 1, 0:16] = jnp.where(low, pltpu.roll(first_part, C, 1), second_part).astype(BF16)

    def pack_last(lap, part):
        vpack[lap, 0, 16:32] = jnp.where(low, part, 0.0).astype(BF16)
        vpack[lap, 1, 16:32] = jnp.where(low, pltpu.roll(part, C, 1), 0.0).astype(BF16)

    first_i = lax.div(s, 2)

    def owner_case(k):
        to_i = k // 2
        to_j = first_block + 2 * (k % 2)
        mine = jnp.logical_and(to_i == i, to_j == j)
        wanted = to_i >= first_i
        return to_i, to_j, jnp.logical_and(wanted, mine), jnp.logical_and(wanted, jnp.logical_not(mine))

    def to_owners(src, dst, rows, n):
        def one(k):
            to_i, to_j, here, there = owner_case(k)

            @pl.when(here)
            def _():
                dst[s, rows] = src[k % 2, rows]

            @pl.when(there)
            def _():
                push(src.at[k % 2, rows], dst.at[s, rows], fs.at[n, k], fr.at[n], to_i, to_j)
        each(0, 16, one)

    def owners_sent(src, rows, n):
        def one(k):
            @pl.when(owner_case(k)[3])
            def _():
                await_bytes(src.at[k % 2, rows], fs.at[n, k])
        each(0, 16, one)

    alone = jnp.logical_and(own_chunk == pos, first_i <= i)

    def owner_sums(dst, rows, n):
        for pair in range(COLS):
            for own in range(2):
                @pl.when(jnp.logical_and(i == pair, alone == (own == 1)))
                def _():
                    await_bytes(dst.at[0:2 * pair + 2 - own, rows], fr.at[n])
        even = jnp.zeros((rows.stop - rows.start, 128), F32)
        odd = even
        for k in range(STEPS):
            later = delta_ref[k:k + 1] * dst[k, rows].astype(F32)
            even = even + jnp.where(k <= 2 * i, later, 0.0)
            odd = odd + jnp.where(k == 2 * i + 1, later, 0.0)
        return even, even + odd

    all_rows, early_rows, late_rows = slice(0, 32), slice(0, 16), slice(16, 32)
    blocks = range(3)
    even_step = lax.rem(s, 2) == 0
    partner = seq_of(s + 1 - 2 * lax.rem(s, 2), p)
    delta_low = jnp.sum(jnp.where(step_row == 2 * z, delta, 0.0), axis=0, keepdims=True)
    delta_high = jnp.sum(jnp.where(step_row == 2 * z + 1, delta, 0.0), axis=0, keepdims=True)
    velocities = {}
    lows = {}

    def sum_heads(block):
        velocities[block] = reduce_heads(0, block)
        vsrc[block] = velocities[block].astype(BF16)
        push(vsrc.at[block], mate.at[block], ms.at[block], mr.at[block], i, partner)

    def sum_pair(block):
        mine = vsrc[block].astype(F32)
        await_bytes(mate.at[block], mr.at[block])
        other = mate[block].astype(F32)
        lows[block] = delta_low * jnp.where(even_step, mine, other)
        pair = (lows[block] + delta_high * jnp.where(even_step, other, mine)).astype(BF16)
        gat[block, z] = pair
        psend[block] = pair
        each(1, 8, lambda k: push(
            psend.at[block], gat.at[block, z], gs.at[block], gr.at[block], i, 4 * lax.rem(z + k, 8) + y))

    def next_latent(block):
        rows = slice(block * 16, (block + 1) * 16)
        latent = jnp.where(low, basein[0, rows], basein[1, rows]) + jnp.where(even_step, 0.0, lows[block])
        await_bytes(gat.at[block, 0:7], gr.at[block])
        for n in range(8):
            latent = latent + jnp.where(n < z, gat[block, n].astype(F32), 0.0)
        latent = latent.astype(BF16)
        zsend[block] = latent
        latents[1, block, chunk, :] = latent
        group(lambda n, ti, tj: push(
            zsend.at[block], latents.at[1, block, chunk, :], ps.at[block], pr.at[block], ti, tj))

    def await_latents(block):
        await_bytes(latents.at[1, block, 0:15 * 16, :], pr.at[block])

    await_bytes(zp.at[:, 0:128, :], cr)
    for block in blocks:
        project(0, block)
    for block in blocks:
        finish(0, block, attend(block, blocks, (None, None)))
        if block:
            sum_heads(block - 1)
    sum_pair(0)
    send_base()
    sum_heads(2)
    sum_pair(1)
    for n in range(2):
        @pl.when(jnp.logical_not(from_mine[n]))
        def _():
            await_bytes(basein.at[n], br.at[n])
    next_latent(0)
    sum_pair(2)
    next_latent(1)
    pack_first(0, velocities[0], velocities[1])
    pack_last(0, velocities[2])

    await_latents(0)
    project(1, 0)
    next_latent(2)
    to_owners(vpack.at[0], fin0, all_rows, 0)
    await_latents(1)
    project(1, 1)
    early = [attend(block, (0, 1), (None, None)) for block in (0, 1)]
    await_latents(2)
    project(1, 2)
    for block in (0, 1):
        finish(1, block, attend(block, (2,), early[block]))
    finish(1, 2, attend(2, blocks, (None, None)))
    pack_first(1, reduce_heads(1, 0), reduce_heads(1, 1))
    to_owners(vpack.at[1], fin1, early_rows, 1)
    first_sums[0], first_sums[1] = owner_sums(fin0, all_rows, 0)
    pack_last(1, reduce_heads(1, 2))
    to_owners(vpack.at[1], fin1, late_rows, 2)

    even, odd = (
        jnp.concatenate(parts, axis=0) for parts in zip(owner_sums(fin1, early_rows, 1), owner_sums(fin1, late_rows, 2)))
    change_even = even - first_sums[0]
    change_odd = odd - first_sums[1]

    def unpack(x):
        return jnp.concatenate([x[0:16], pltpu.roll(x[0:16], C, 1), x[16:32]], axis=0)

    row = lax.broadcasted_iota(jnp.int32, (2, 128), 0)
    sum_even = jnp.sum(change_even * change_even, axis=0, keepdims=True)
    sum_odd = jnp.sum(change_odd * change_odd, axis=0, keepdims=True)
    partial = jnp.where(row == 0, sum_even, sum_odd)
    esrc[0] = partial
    ein[z] = partial
    each(1, 8, lambda k: push(esrc.at[0], ein.at[z], es.at[0], er.at[0], i, 4 * lax.rem(z + k, 8) + y))
    for n, total in enumerate((basesrc[1] + unpack(even), basesrc[2] + unpack(odd))):
        out_ref[n] = total[:, 0:C]
    await_bytes(ein.at[0:7], er.at[0])
    total = ein[0]
    for n in range(1, 8):
        total = total + ein[n]
    esrc[1] = total
    ein[8 + y] = total
    each(1, 4, lambda k: push(esrc.at[1], ein.at[8 + y], es.at[1], er.at[1], i, 4 * z + lax.rem(y + k, 4)))
    await_bytes(ein.at[8:11], er.at[1])
    total = (ein[8] + ein[9]) + (ein[10] + ein[11])
    total = total * (1.0 / (LEN * C))
    err_ref[0] = jnp.sum(total[0:1] / (coeff_even * coeff_even))
    err_ref[1] = jnp.sum(total[1:2] / (coeff_odd * coeff_odd))

    await_bytes(ein.at[0:7], es.at[0])
    await_bytes(ein.at[8:11], es.at[1])
    for lap in range(2):
        await_bytes(red.at[lap, :, 0:STEPS - 1], us.at[lap])
    for block in blocks:
        await_bytes(gat.at[block, 0:7], gs.at[block])
        await_bytes(latents.at[1, block, 0:15 * 16, :], ps.at[block])
        await_bytes(mate.at[block], ms.at[block])
    owners_sent(vpack.at[0], all_rows, 0)
    owners_sent(vpack.at[1], early_rows, 1)
    owners_sent(vpack.at[1], late_rows, 2)
    await_bytes(yin.at[0:3], ys)
    await_bytes(nin.at[0:COLS - 1], ns)
    await_bytes(zp.at[:, 0:7 * 16, :], zs)
    await_bytes(zp.at[:, 0:128, :], cs)
    for n in range(2):
        @pl.when(jnp.logical_not(base_mine[n]))
        def _():
            await_bytes(basesrc.at[n], bs.at[n])


def per_device(
    start_latent, noise, window_start, w_embed, w_time, norm_gain, w_query, w_key, w_value, query_gain, key_gain, w_out, w_final,
):
    vmem = pl.BlockSpec(memory_space=pltpu.VMEM)
    hbm = pl.BlockSpec(memory_space=pltpu.HBM)
    smem = pl.BlockSpec(memory_space=pltpu.SMEM)
    dma = pltpu.SemaphoreType.DMA
    out, errors = pl.pallas_call(
        kernel,
        out_shape=(
            pltpu.VMEM((2, ROWS, C), F32),
            pltpu.SMEM((2,), F32),
        ),
        in_specs=[smem] + [hbm] * 12,
        out_specs=(vmem, smem),
        scratch_shapes=[
            pltpu.VMEM((ROWS, C), F32),
            pltpu.VMEM((2, ROWS, C), BF16),
            pltpu.VMEM((1, D), F32),
            pltpu.VMEM((1, HEAD), F32),
            pltpu.VMEM((1, HEAD), F32),
            pltpu.VMEM((256, D), BF16),
            pltpu.VMEM((D, 3 * HEAD), BF16),
            pltpu.VMEM((240, D), BF16),
            pltpu.VMEM((240, D), BF16),
            pltpu.VMEM((256, D), BF16),
            pltpu.VMEM((384, 256), BF16),
            pltpu.VMEM((384, 128), BF16),
            pltpu.VMEM((8, 128), F32),
            pltpu.VMEM((STEPS, 128), F32),
            pltpu.VMEM((STEPS, 128), F32),
            pltpu.VMEM((ROWS, 128), BF16),
            pltpu.VMEM((4, ROWS, 128), BF16),
            pltpu.VMEM((3, 16, 128), BF16),
            pltpu.VMEM((ROWS, 128), BF16),
            pltpu.VMEM((COLS, ROWS, 128), BF16),
            pltpu.VMEM((3, ROWS, 128), F32),
            pltpu.VMEM((2, ROWS, 128), F32),
            pltpu.VMEM((2, 3, QBLK, 128), BF16),
            pltpu.VMEM((2, 3, QBLK, 128), BF16),
            pltpu.VMEM((2, 3, STEPS, 16, 128), BF16),
            pltpu.VMEM((3, 16, 128), BF16),
            pltpu.VMEM((2, 2, 32, 128), BF16),
            pltpu.VMEM((3, 16, 128), BF16),
            pltpu.VMEM((3, 16, 128), BF16),
            pltpu.VMEM((3, 8, 16, 128), BF16),
            pltpu.VMEM((3, 16, 128), BF16),
            pltpu.VMEM((STEPS, 32, 128), BF16),
            pltpu.VMEM((STEPS, 32, 128), BF16),
            pltpu.VMEM((2, 32, 128), F32),
            pltpu.VMEM((2, 2, 128), F32),
            pltpu.VMEM((12, 2, 128), F32),
            pltpu.VMEM((256, KBLK), BF16),
            pltpu.VMEM((LEN, HEAD), BF16),
            pltpu.VMEM((HEAD, LEN), BF16),
            pltpu.VMEM((C + 16, LEN), BF16),
            dma((14,)),
            dma, dma, dma, dma, dma, dma, dma, dma, dma((2,)), dma((2,)),
            dma((2,)), dma((2, 3)), dma((3,)), dma((3,)), dma((3,)), dma((3,)), dma((3, STEPS)), dma((3,)), dma((2,)), dma((2,)),
            dma((3,)), dma((3,)),
        ],
        compiler_params=pltpu.CompilerParams(
            collective_id=0, has_side_effects=True, vmem_limit_bytes=56 * 1024 * 1024),
    )(
        window_start, start_latent, noise, norm_gain.reshape(1, D), query_gain.reshape(1, HEAD), key_gain.reshape(1, HEAD),
        w_embed, w_time, w_final.T, w_query, w_key, w_value, w_out,
    )
    return out, errors


def solution(mesh):
    return jax.shard_map(
        per_device,
        mesh=mesh,
        in_specs=(
            P("seq", None), P("step", "seq", None), P(), P(), P(), P(),
            P(None, "step"), P(None, "step"), P(None, "step"), P(), P(), P("step", None), P(),
        ),
        out_specs=(P("step", "seq", None), P("step")),
        check_vma=False,
    )
```

```python
import math

import jax
import jax.numpy as jnp
from jax import lax
from jax.experimental import pallas as pl
from jax.experimental.pallas import tpu as pltpu
from jax.sharding import PartitionSpec as P

NSCHED = 28
EPS = 1e-06
SHIFT = 3.0
ETA = 0.5
MESH = pl.DeviceIdType.MESH
F32 = jnp.float32
BF16 = jnp.bfloat16

D = 3072
C = 64
HEAD = 128
LEN = 1536
HALF = LEN // 2
STEPS = 16
ROWS = 48
SEQ = 32
COLS = 8
QBLK = 256
KBLK = 512


def sigma_of(index):
    fraction = 1.0 - index / NSCHED
    return SHIFT * fraction / (1.0 + (SHIFT - 1.0) * fraction)


def chunk_i(n):
    return 2 * lax.rem(n, 4) + lax.div(n, 8)


def chunk_p(n):
    return lax.rem(lax.div(n, 4), 2)


def seq_of(step, part):
    return 2 * step + lax.rem(step + part, 2)


def chunk_block(n):
    return 4 * lax.rem(n, 8) + lax.div(n, 8)


def split(x):
    hi = x.astype(BF16)
    return hi, (x - hi.astype(F32)).astype(BF16)


def mm(a, b):
    return jnp.dot(a, b, preferred_element_type=F32)


def kernel(
    ws_ref, start_hbm, noise_hbm, gain_hbm, qg_hbm, kg_hbm,
    wembed_hbm, wtime_hbm, wfinal_hbm, wq_hbm, wk_hbm, wv_hbm, wo_hbm,
    out_ref, err_ref,
    start_ref, noise_ref, gain_ref, qg_ref, kg_ref,
    wtime, wall, fold, left, right, wqkv, cdiag, crow,
    delta_ref, coeff_ref,
    zsrc, yin, slab, nsrc, nin, basesrc, basein,
    latents, heads, red, vsrc, vpack, mate, psend, gat, zsend, fin0, fin1, first_sums, esrc, ein,
    ztr, kbuf, qvbuf,
    wsem, ys, yr, zs, zr, cs, cr, ns, nr, bs, br, us, ur, gs, gr, ps, pr, fs, fr, es, er, ms, mr,
):
    i = lax.axis_index("step")
    j = lax.axis_index("seq")
    x = lax.div(i, 2)
    c = lax.rem(i, 2)
    z = lax.div(j, 4)
    y = lax.rem(j, 4)
    s = lax.div(j, 2)
    p = lax.rem(j + s, 2)
    pos = 4 * (2 * c + p) + x
    own_chunk = 8 * lax.rem(y, 2) + z
    half = lax.div(y, 2)
    source_i = chunk_i(own_chunk)
    source_p = chunk_p(own_chunk)
    first_block = chunk_block(pos)
    low_lanes = lax.broadcasted_iota(jnp.int32, (ROWS, 128), 1) < C

    def rows_of(n):
        return pl.ds(pl.multiple_of(n * 16, 16), 16)

    def push(src, dst, send, recv, to_i, to_j):
        pltpu.make_async_remote_copy(
            src_ref=src, dst_ref=dst, send_sem=send, recv_sem=recv,
            device_id=(to_i, to_j), device_id_type=MESH,
        ).start()

    def await_bytes(like, sem):
        pltpu.make_async_copy(like, like, sem).wait()

    def each(low, high, fn):
        for k in range(low, high):
            fn(k)

    def group(fn):
        def one(k):
            n = lax.rem(pos + k, STEPS)
            fn(n, chunk_i(n), seq_of(s, chunk_p(n)))
        each(1, STEPS, one)

    zp = latents.at[0]

    head = pl.multiple_of(p * HEAD, HEAD)
    pairs = [
        (start_hbm, start_ref), (noise_hbm, noise_ref), (wtime_hbm, wtime), (wembed_hbm, left.at[0:64, :]),
        (gain_hbm, gain_ref), (wembed_hbm, right.at[128:192, :]), (wfinal_hbm, right.at[0:64, :]),
        (wfinal_hbm, right.at[64:128, :]), (wo_hbm.at[pl.ds(head, HEAD), :], left.at[96:224, :]),
        (qg_hbm, qg_ref), (kg_hbm, kg_ref),
    ] + [
        (w.at[:, pl.ds(head, HEAD)], wall.at[:, n * HEAD:(n + 1) * HEAD]) for n, w in enumerate((wq_hbm, wk_hbm, wv_hbm))
    ]
    local = [pltpu.make_async_copy(src, dst, wsem.at[n]) for n, (src, dst) in enumerate(pairs)]
    for copy in local:
        copy.start()

    barrier = pltpu.get_barrier_semaphore()

    def greet(to_i, to_j):
        pl.semaphore_signal(barrier, inc=1, device_id=(to_i, to_j), device_id_type=MESH)

    group(lambda n, ti, tj: greet(ti, tj))
    each(1, 4, lambda k: greet(i, 4 * z + lax.rem(y + k, 4)))
    each(1, 8, lambda k: greet(i, 4 * lax.rem(z + k, 8) + y))
    base_j = [seq_of(2 * i + n, source_p) for n in range(2)]
    base_mine = [jnp.logical_and(source_i == i, tj == j) for tj in base_j]
    from_j = [first_block + 2 * n for n in range(2)]
    from_i = lax.div(s, 2)
    from_mine = [jnp.logical_and(from_i == i, tj == j) for tj in from_j]
    for n in range(2):
        @pl.when(jnp.logical_not(from_mine[n]))
        def _():
            greet(from_i, from_j[n])

    local[0].wait()
    z0 = start_ref[...]
    start_dup = jnp.concatenate([z0, z0], axis=1)
    zsrc[...] = start_dup.astype(BF16)
    yin[y] = start_dup.astype(BF16)
    local[1].wait()
    packed_noise = jnp.concatenate([noise_ref[0], noise_ref[1]], axis=1)
    nsrc[...] = packed_noise
    nin[i] = packed_noise

    alone_count = base_mine[0].astype(jnp.int32) + base_mine[1].astype(jnp.int32)
    pl.semaphore_wait(barrier, 15 + 3 + 7 + 2 - alone_count)

    each(1, 4, lambda k: push(zsrc, yin.at[y], ys, yr, i, 4 * z + lax.rem(y + k, 4)))

    first = ws_ref[0]
    index = (lax.broadcasted_iota(jnp.int32, (STEPS, 128), 0) + first).astype(F32)
    sigma_now = sigma_of(index)
    delta = sigma_of(index + 1.0) - sigma_now
    coeff = ETA * jnp.sqrt(-delta)
    delta_ref[...] = delta
    coeff_ref[...] = coeff
    own = sigma_of((jnp.zeros((STEPS, 128), jnp.int32) + (first + s)).astype(F32))
    lane = lax.broadcasted_iota(jnp.int32, (STEPS, 128), 1).astype(F32)
    angle = 1000.0 * own * jnp.exp(-math.log(10000.0) * lane / 128)
    feats = jnp.concatenate([jnp.cos(angle), jnp.sin(angle)], axis=1)
    feats = (feats / (1.0 + jnp.exp(-feats))).astype(BF16)
    right[192:256] = jnp.zeros((64, D), BF16)
    for n in range(2):
        ztr[128 * n + 64:128 * n + 128] = jnp.where(
            lax.broadcasted_iota(jnp.int32, (64, KBLK), 0) == 0, 1.0, 0.0).astype(BF16)

    for copy in local[3:5]:
        copy.wait()
    local[2].wait()
    temb = mm(feats, wtime[...])

    emb = left[0:64].astype(F32)
    gain = gain_ref[...]
    for n, part in enumerate(split(jnp.concatenate([emb * gain, temb * gain], axis=0))):
        fold[n * 80:(n + 1) * 80] = part
    for n, part in enumerate(split(temb)):
        left[64 + 16 * n:80 + 16 * n] = part
    t_row = temb[0:1]
    twice_et = 2.0 * jnp.sum(emb * t_row, axis=1, keepdims=True)
    t_square = jnp.sum(t_row * t_row, axis=1, keepdims=True)

    await_bytes(yin.at[0:3], yr)
    slab_now = jnp.where(low_lanes, yin[c].astype(F32), yin[c + 2].astype(F32)).reshape(3, 16, 128).astype(BF16)
    slab[...] = slab_now
    slab_rows = rows_of(8 * c + z)
    zp[:, slab_rows, :] = slab_now
    each(1, 8, lambda k: push(slab, zp.at[:, slab_rows, :], zs, zr, i, 4 * lax.rem(z + k, 8) + y))

    each(1, COLS, lambda k: push(nsrc, nin.at[i], ns, nr, lax.rem(i + k, COLS), j))

    for copy in local[5:]:
        copy.wait()
    folded = mm(fold[...], wall[...])
    folded = folded[0:80] + folded[80:160]
    both = lax.dot_general(left[...], right[...], (((1,), (1,)), ((), ())), preferred_element_type=F32)
    cdup = both[0:64, 0:128]
    gram = both[0:64, 128:256]
    mout = both[96:224, 0:128]
    lanes64 = lax.broadcasted_iota(jnp.int32, (64, 128), 1)
    diag = jnp.concatenate([jnp.where(lanes64 < C, cdup, 0.0), jnp.where(lanes64 < C, 0.0, cdup)], axis=0)
    for n, part in enumerate(split(diag)):
        cdiag[n * 128:(n + 1) * 128] = part
    crow[...] = both[64:72, 0:128] + both[80:88, 0:128]

    await_bytes(zp.at[:, 0:7 * 16, :], zr)
    core_rows = pl.ds(pl.multiple_of(128 * c, 128), 128)
    push(zp.at[:, core_rows, :], zp.at[:, core_rows, :], cs, cr, i + 1 - 2 * c, j)

    value_fold = jnp.dot(folded[:, 256:384], mout, precision=lax.Precision.HIGHEST, preferred_element_type=F32)
    wide = jnp.concatenate([folded[:, 0:256], value_fold], axis=1)
    wide = jnp.concatenate([wide, jnp.zeros((48, 384), F32)], axis=0).T
    wide = jnp.concatenate([wide[0:320], jnp.where(lanes64 == C, twice_et, gram)], axis=0)
    whi = wide.astype(BF16)
    wqkv[:, 0:128] = whi
    wqkv[:, 128:256] = (wide - whi.astype(F32)).astype(BF16)
    scale_row = qg_ref[...] * kg_ref[...] * (math.log2(math.e) / math.sqrt(HEAD))
    scale_col = jnp.broadcast_to(scale_row, (128, 128)).T[:, 0:1]

    step_row = lax.broadcasted_iota(jnp.int32, (STEPS, 128), 0)
    coeff_even = jnp.sum(jnp.where(step_row == 2 * i, coeff, 0.0), axis=0, keepdims=True)
    coeff_odd = jnp.sum(jnp.where(step_row == 2 * i + 1, coeff, 0.0), axis=0, keepdims=True)

    def send_base():
        await_bytes(nin.at[0:COLS - 1], nr)

        def noise_of(step_pair):
            both = nin[step_pair].astype(F32)
            turned = pltpu.roll(both, C, 1)
            return jnp.where(low_lanes, both, turned), jnp.where(low_lanes, turned, both)

        base = start_dup
        for pair in range(COLS):
            even, odd = noise_of(pair)
            pair_sum = coeff_ref[2 * pair:2 * pair + 1] * even + coeff_ref[2 * pair + 1:2 * pair + 2] * odd
            base = base + jnp.where(pair < i, pair_sum, 0.0)
        own_even, own_odd = noise_of(i)
        after_even = base + coeff_even * own_even
        after_odd = after_even + coeff_odd * own_odd
        basesrc[0] = base
        basesrc[1] = after_even
        basesrc[2] = after_odd
        for n in range(2):
            @pl.when(base_mine[n])
            def _():
                basein[half] = basesrc[n]

            @pl.when(jnp.logical_not(base_mine[n]))
            def _():
                push(basesrc.at[n], basein.at[half], bs.at[n], br.at[half], source_i, base_j[n])

    chunk = rows_of(pos)
    low = low_lanes[0:16]

    def project(lap, n):
        packed = latents[lap, n].T
        zb = jnp.concatenate([packed[0:64], packed[64:128]], axis=1)
        ztr[0:64] = zb
        ztr[128:192] = zb
        cols = slice(n * KBLK, (n + 1) * KBLK)
        out = mm(wqkv[...], ztr[...])
        yq, yk, yv, yg = out[0:128], out[128:256], out[256:320], out[320:384]
        mean_square = (jnp.sum(zb.astype(F32) * yg, axis=0, keepdims=True) + t_square) * (1.0 / D)
        square = jnp.maximum(mean_square, 0.0) + EPS
        aq = lax.rsqrt(jnp.mean(yq * yq, axis=0, keepdims=True) + EPS * square)
        ak = lax.rsqrt(jnp.mean(yk * yk, axis=0, keepdims=True) + EPS * square)
        kbuf[:, cols] = (yk * ak).astype(BF16)
        rows = jnp.concatenate([yq * aq * scale_col, yv * lax.rsqrt(square), jnp.ones((C, KBLK), F32)], axis=0)
        qvbuf[cols, :] = rows.astype(BF16).T

    def attend(block, keys, accs):
        out = []
        for side in range(2):
            q = qvbuf[block * KBLK + side * QBLK:block * KBLK + (side + 1) * QBLK, 0:HEAD]
            acc = accs[side]
            for m in keys:
                here = slice(m * KBLK, (m + 1) * KBLK)
                weights = jnp.exp2(mm(q, kbuf[:, here])).astype(BF16)
                part = mm(weights, qvbuf[here, HEAD:])
                acc = part if acc is None else acc + part
            out.append(acc)
        return out

    low_block = lax.broadcasted_iota(jnp.int32, (QBLK, 128), 1) < C

    def finish(lap, block, accs):
        first_acc, second_acc = accs
        heads[lap, block] = jnp.where(
            low_block, first_acc / pltpu.roll(first_acc, C, 1), pltpu.roll(second_acc, C, 1) / second_acc).astype(BF16)
        group(lambda n, ti, tj: push(
            heads.at[lap, block, rows_of(n), :], red.at[lap, block, pos], us.at[lap], ur.at[lap, block], ti, tj))

    def reduce_heads(lap, block):
        red[lap, block, pos] = heads[lap, block, chunk, :]
        latent = latents[lap, block, chunk, :]
        total = mm(jnp.concatenate([latent, latent], axis=1), cdiag[...]) + crow[0:1]
        await_bytes(red.at[lap, block, 0:STEPS - 1], ur.at[lap, block])
        for h in range(STEPS):
            total = total + red[lap, block, h].astype(F32)
        return total

    def pack_first(lap, first_part, second_part):
        vpack[lap, 0, 0:16] = jnp.where(low, first_part, pltpu.roll(second_part, C, 1)).astype(BF16)
        vpack[lap, 1, 0:16] = jnp.where(low, pltpu.roll(first_part, C, 1), second_part).astype(BF16)

    def pack_last(lap, part):
        vpack[lap, 0, 16:32] = jnp.where(low, part, 0.0).astype(BF16)
        vpack[lap, 1, 16:32] = jnp.where(low, pltpu.roll(part, C, 1), 0.0).astype(BF16)

    first_i = lax.div(s, 2)

    alone = jnp.logical_and(own_chunk == pos, first_i <= i)

    def to_owners(src, dst, rows, n):
        @pl.when(alone)
        def _():
            dst[s, rows] = src[half, rows]

        def one(k):
            to_i = k // 2
            to_j = first_block + 2 * (k % 2)
            mine = jnp.logical_and(to_i == i, to_j == j)

            @pl.when(jnp.logical_and(to_i >= first_i, jnp.logical_not(mine)))
            def _():
                push(src.at[k % 2, rows], dst.at[s, rows], fs.at[n], fr.at[n], to_i, to_j)
        each(0, 16, one)

    def owners_sent(dst, rows, n):
        for pair in range(COLS):
            for own in range(2):
                @pl.when(jnp.logical_and(first_i == pair, alone == (own == 1)))
                def _():
                    await_bytes(dst.at[0:2 * (COLS - pair) - own, rows], fs.at[n])

    def owner_sums(dst, rows, n):
        for pair in range(COLS):
            for own in range(2):
                @pl.when(jnp.logical_and(i == pair, alone == (own == 1)))
                def _():
                    await_bytes(dst.at[0:2 * pair + 2 - own, rows], fr.at[n])
        even = jnp.zeros((rows.stop - rows.start, 128), F32)
        odd = even
        for k in range(STEPS):
            later = delta_ref[k:k + 1] * dst[k, rows].astype(F32)
            even = even + jnp.where(k <= 2 * i, later, 0.0)
            odd = odd + jnp.where(k == 2 * i + 1, later, 0.0)
        return even, even + odd

    all_rows, early_rows, late_rows = slice(0, 32), slice(0, 16), slice(16, 32)
    blocks = range(3)
    even_step = lax.rem(s, 2) == 0
    partner = seq_of(s + 1 - 2 * lax.rem(s, 2), p)
    delta_low = jnp.sum(jnp.where(step_row == 2 * z, delta, 0.0), axis=0, keepdims=True)
    delta_high = jnp.sum(jnp.where(step_row == 2 * z + 1, delta, 0.0), axis=0, keepdims=True)
    velocities = {}
    lows = {}

    def sum_heads(block):
        velocities[block] = reduce_heads(0, block)
        vsrc[block] = velocities[block].astype(BF16)
        push(vsrc.at[block], mate.at[block], ms.at[block], mr.at[block], i, partner)

    def sum_pair(block):
        mine = vsrc[block].astype(F32)
        await_bytes(mate.at[block], mr.at[block])
        other = mate[block].astype(F32)
        lows[block] = delta_low * jnp.where(even_step, mine, other)
        pair = (lows[block] + delta_high * jnp.where(even_step, other, mine)).astype(BF16)
        gat[block, z] = pair
        psend[block] = pair
        each(1, 8, lambda k: push(
            psend.at[block], gat.at[block, z], gs.at[block], gr.at[block], i, 4 * lax.rem(z + k, 8) + y))

    def next_latent(block):
        rows = slice(block * 16, (block + 1) * 16)
        latent = jnp.where(low, basein[0, rows], basein[1, rows]) + jnp.where(even_step, 0.0, lows[block])
        await_bytes(gat.at[block, 0:7], gr.at[block])
        for n in range(8):
            latent = latent + jnp.where(n < z, gat[block, n].astype(F32), 0.0)
        latent = latent.astype(BF16)
        zsend[block] = latent
        latents[1, block, chunk, :] = latent
        group(lambda n, ti, tj: push(
            zsend.at[block], latents.at[1, block, chunk, :], ps.at[block], pr.at[block], ti, tj))

    def await_latents(block):
        await_bytes(latents.at[1, block, 0:15 * 16, :], pr.at[block])

    await_bytes(zp.at[:, 0:128, :], cr)
    for block in blocks:
        project(0, block)
    for block in blocks:
        finish(0, block, attend(block, blocks, (None, None)))
        if block:
            sum_heads(block - 1)
    sum_pair(0)
    send_base()
    sum_heads(2)
    sum_pair(1)
    for n in range(2):
        @pl.when(jnp.logical_not(from_mine[n]))
        def _():
            await_bytes(basein.at[n], br.at[n])
    next_latent(0)
    sum_pair(2)
    next_latent(1)
    pack_first(0, velocities[0], velocities[1])
    pack_last(0, velocities[2])

    await_latents(0)
    project(1, 0)
    next_latent(2)
    to_owners(vpack.at[0], fin0, all_rows, 0)
    await_latents(1)
    project(1, 1)
    early = [attend(block, (0, 1), (None, None)) for block in (0, 1)]
    await_latents(2)
    project(1, 2)
    for block in (0, 1):
        finish(1, block, attend(block, (2,), early[block]))
    finish(1, 2, attend(2, blocks, (None, None)))
    pack_first(1, reduce_heads(1, 0), reduce_heads(1, 1))
    to_owners(vpack.at[1], fin1, early_rows, 1)
    first_sums[0], first_sums[1] = owner_sums(fin0, all_rows, 0)
    pack_last(1, reduce_heads(1, 2))
    to_owners(vpack.at[1], fin1, late_rows, 2)

    even, odd = (
        jnp.concatenate(parts, axis=0) for parts in zip(owner_sums(fin1, early_rows, 1), owner_sums(fin1, late_rows, 2)))
    change_even = even - first_sums[0]
    change_odd = odd - first_sums[1]

    def unpack(x):
        return jnp.concatenate([x[0:16], pltpu.roll(x[0:16], C, 1), x[16:32]], axis=0)

    row = lax.broadcasted_iota(jnp.int32, (2, 128), 0)
    sum_even = jnp.sum(change_even * change_even, axis=0, keepdims=True)
    sum_odd = jnp.sum(change_odd * change_odd, axis=0, keepdims=True)
    partial = jnp.where(row == 0, sum_even, sum_odd)
    esrc[0] = partial
    ein[z] = partial
    each(1, 8, lambda k: push(esrc.at[0], ein.at[z], es.at[0], er.at[0], i, 4 * lax.rem(z + k, 8) + y))
    for n, total in enumerate((basesrc[1] + unpack(even), basesrc[2] + unpack(odd))):
        out_ref[n] = total[:, 0:C]
    for lap in range(2):
        await_bytes(red.at[lap, :, 0:STEPS - 1], us.at[lap])
    for block in blocks:
        await_bytes(gat.at[block, 0:7], gs.at[block])
        await_bytes(latents.at[1, block, 0:15 * 16, :], ps.at[block])
        await_bytes(mate.at[block], ms.at[block])
    owners_sent(fin0, all_rows, 0)
    owners_sent(fin1, early_rows, 1)
    owners_sent(fin1, late_rows, 2)
    await_bytes(yin.at[0:3], ys)
    await_bytes(nin.at[0:COLS - 1], ns)
    await_bytes(zp.at[:, 0:7 * 16, :], zs)
    await_bytes(zp.at[:, 0:128, :], cs)
    for n in range(2):
        @pl.when(jnp.logical_not(base_mine[n]))
        def _():
            await_bytes(basesrc.at[n], bs.at[n])

    await_bytes(ein.at[0:7], er.at[0])
    total = ein[0]
    for n in range(1, 8):
        total = total + ein[n]
    esrc[1] = total
    ein[8 + y] = total
    each(1, 4, lambda k: push(esrc.at[1], ein.at[8 + y], es.at[1], er.at[1], i, 4 * z + lax.rem(y + k, 4)))
    await_bytes(ein.at[8:11], er.at[1])
    total = (ein[8] + ein[9]) + (ein[10] + ein[11])
    total = total * (1.0 / (LEN * C))
    err_ref[0] = jnp.sum(total[0:1] / (coeff_even * coeff_even))
    err_ref[1] = jnp.sum(total[1:2] / (coeff_odd * coeff_odd))

    await_bytes(ein.at[0:7], es.at[0])
    await_bytes(ein.at[8:11], es.at[1])


def per_device(
    start_latent, noise, window_start, w_embed, w_time, norm_gain, w_query, w_key, w_value, query_gain, key_gain, w_out, w_final,
):
    vmem = pl.BlockSpec(memory_space=pltpu.VMEM)
    hbm = pl.BlockSpec(memory_space=pltpu.HBM)
    smem = pl.BlockSpec(memory_space=pltpu.SMEM)
    dma = pltpu.SemaphoreType.DMA
    out, errors = pl.pallas_call(
        kernel,
        out_shape=(
            pltpu.VMEM((2, ROWS, C), F32),
            pltpu.SMEM((2,), F32),
        ),
        in_specs=[smem] + [hbm] * 12,
        out_specs=(vmem, smem),
        scratch_shapes=[
            pltpu.VMEM((ROWS, C), F32),
            pltpu.VMEM((2, ROWS, C), BF16),
            pltpu.VMEM((1, D), F32),
            pltpu.VMEM((1, HEAD), F32),
            pltpu.VMEM((1, HEAD), F32),
            pltpu.VMEM((256, D), BF16),
            pltpu.VMEM((D, 3 * HEAD), BF16),
            pltpu.VMEM((160, D), BF16),
            pltpu.VMEM((224, D), BF16),
            pltpu.VMEM((256, D), BF16),
            pltpu.VMEM((384, 256), BF16),
            pltpu.VMEM((256, 128), BF16),
            pltpu.VMEM((8, 128), F32),
            pltpu.VMEM((STEPS, 128), F32),
            pltpu.VMEM((STEPS, 128), F32),
            pltpu.VMEM((ROWS, 128), BF16),
            pltpu.VMEM((4, ROWS, 128), BF16),
            pltpu.VMEM((3, 16, 128), BF16),
            pltpu.VMEM((ROWS, 128), BF16),
            pltpu.VMEM((COLS, ROWS, 128), BF16),
            pltpu.VMEM((3, ROWS, 128), F32),
            pltpu.VMEM((2, ROWS, 128), F32),
            pltpu.VMEM((2, 3, QBLK, 128), BF16),
            pltpu.VMEM((2, 3, QBLK, 128), BF16),
            pltpu.VMEM((2, 3, STEPS, 16, 128), BF16),
            pltpu.VMEM((3, 16, 128), BF16),
            pltpu.VMEM((2, 2, 32, 128), BF16),
            pltpu.VMEM((3, 16, 128), BF16),
            pltpu.VMEM((3, 16, 128), BF16),
            pltpu.VMEM((3, 8, 16, 128), BF16),
            pltpu.VMEM((3, 16, 128), BF16),
            pltpu.VMEM((STEPS, 32, 128), BF16),
            pltpu.VMEM((STEPS, 32, 128), BF16),
            pltpu.VMEM((2, 32, 128), F32),
            pltpu.VMEM((2, 2, 128), F32),
            pltpu.VMEM((12, 2, 128), F32),
            pltpu.VMEM((256, KBLK), BF16),
            pltpu.VMEM((HEAD, LEN), BF16),
            pltpu.VMEM((LEN, 2 * HEAD), BF16),
            dma((14,)),
            dma, dma, dma, dma, dma, dma, dma, dma, dma((2,)), dma((2,)),
            dma((2,)), dma((2, 3)), dma((3,)), dma((3,)), dma((3,)), dma((3,)), dma((3,)), dma((3,)), dma((2,)), dma((2,)),
            dma((3,)), dma((3,)),
        ],
        compiler_params=pltpu.CompilerParams(
            collective_id=0, has_side_effects=True, vmem_limit_bytes=56 * 1024 * 1024),
    )(
        window_start, start_latent, noise, norm_gain.reshape(1, D), query_gain.reshape(1, HEAD), key_gain.reshape(1, HEAD),
        w_embed, w_time, w_final.T, w_query, w_key, w_value, w_out,
    )
    return out, errors


def solution(mesh):
    return jax.shard_map(
        per_device,
        mesh=mesh,
        in_specs=(
            P("seq", None), P("step", "seq", None), P(), P(), P(), P(),
            P(None, "step"), P(None, "step"), P(None, "step"), P(), P(), P("step", None), P(),
        ),
        out_specs=(P("step", "seq", None), P("step")),
        check_vma=False,
    )
```

```python
import math

import jax
import jax.numpy as jnp
from jax import lax
from jax.experimental import pallas as pl
from jax.experimental.pallas import tpu as pltpu
from jax.sharding import PartitionSpec as P

NSCHED = 28
EPS = 1e-06
SHIFT = 3.0
ETA = 0.5
MESH = pl.DeviceIdType.MESH
F32 = jnp.float32
BF16 = jnp.bfloat16

D = 3072
C = 64
HEAD = 128
LEN = 1536
HALF = LEN // 2
STEPS = 16
ROWS = 48
SEQ = 32
COLS = 8
QBLK = 256
KBLK = 512


def sigma_of(index):
    fraction = 1.0 - index / NSCHED
    return SHIFT * fraction / (1.0 + (SHIFT - 1.0) * fraction)


def chunk_i(n):
    return 2 * lax.rem(n, 4) + lax.div(n, 8)


def chunk_p(n):
    return lax.rem(lax.div(n, 4), 2)


def seq_of(step, part):
    return 2 * step + lax.rem(step + part, 2)


def chunk_block(n):
    return 4 * lax.rem(n, 8) + lax.div(n, 8)


def split(x):
    hi = x.astype(BF16)
    return hi, (x - hi.astype(F32)).astype(BF16)


def mm(a, b):
    return jnp.dot(a, b, preferred_element_type=F32)


def kernel(
    ws_ref, start_hbm, noise_hbm, gain_hbm, qg_hbm, kg_hbm,
    wembed_hbm, wtime_hbm, wfinal_hbm, wq_hbm, wk_hbm, wv_hbm, wo_hbm,
    out_ref, err_ref,
    start_ref, noise_ref, gain_ref, qg_ref, kg_ref,
    wtime, wall, fold, left, right, wqkv, cdiag, crow,
    delta_ref, coeff_ref,
    zsrc, yin, nsrc, nin, basesrc, basein,
    latents, heads, red, vsrc, vpack, gat, zsend, fin0, fin1, first_sums, esrc, ein,
    ztr, kbuf, qvbuf,
    wsem, ys, yr, cs, cr, ns, nr, bs, br, us, ur, gs, gr, ps, pr, fs, fr, es, er,
):
    i = lax.axis_index("step")
    j = lax.axis_index("seq")
    x = lax.div(i, 2)
    c = lax.rem(i, 2)
    z = lax.div(j, 4)
    y = lax.rem(j, 4)
    s = lax.div(j, 2)
    p = lax.rem(j + s, 2)
    pos = 4 * (2 * c + p) + x
    own_chunk = 8 * lax.rem(y, 2) + z
    half = lax.div(y, 2)
    source_i = chunk_i(own_chunk)
    source_p = chunk_p(own_chunk)
    first_block = chunk_block(pos)
    low_lanes = lax.broadcasted_iota(jnp.int32, (ROWS, 128), 1) < C

    def rows_of(n):
        return pl.ds(pl.multiple_of(n * 16, 16), 16)

    def push(src, dst, send, recv, to_i, to_j):
        pltpu.make_async_remote_copy(
            src_ref=src, dst_ref=dst, send_sem=send, recv_sem=recv,
            device_id=(to_i, to_j), device_id_type=MESH,
        ).start()

    def await_bytes(like, sem):
        pltpu.make_async_copy(like, like, sem).wait()

    def each(low, high, fn):
        for k in range(low, high):
            fn(k)

    def group(fn):
        def one(k):
            n = lax.rem(pos + k, STEPS)
            fn(n, chunk_i(n), seq_of(s, chunk_p(n)))
        each(1, STEPS, one)

    zp = latents.at[0]

    def column(fn):
        each(1, SEQ, lambda k: fn(lax.rem(j + k, SEQ)))

    head = pl.multiple_of(p * HEAD, HEAD)
    pairs = [
        (start_hbm, start_ref), (noise_hbm, noise_ref), (wtime_hbm, wtime), (wembed_hbm, left.at[0:64, :]),
        (gain_hbm, gain_ref), (wembed_hbm, right.at[128:192, :]), (wfinal_hbm, right.at[0:64, :]),
        (wfinal_hbm, right.at[64:128, :]), (wo_hbm.at[pl.ds(head, HEAD), :], left.at[96:224, :]),
        (qg_hbm, qg_ref), (kg_hbm, kg_ref),
    ] + [
        (w.at[:, pl.ds(head, HEAD)], wall.at[:, n * HEAD:(n + 1) * HEAD]) for n, w in enumerate((wq_hbm, wk_hbm, wv_hbm))
    ]
    local = [pltpu.make_async_copy(src, dst, wsem.at[n]) for n, (src, dst) in enumerate(pairs)]
    for copy in local:
        copy.start()

    barrier = pltpu.get_barrier_semaphore()

    def greet(to_i, to_j):
        pl.semaphore_signal(barrier, inc=1, device_id=(to_i, to_j), device_id_type=MESH)

    group(lambda n, ti, tj: greet(ti, tj))
    column(lambda tj: greet(i, tj))
    base_j = [seq_of(2 * i + n, source_p) for n in range(2)]
    base_mine = [jnp.logical_and(source_i == i, tj == j) for tj in base_j]
    from_j = [first_block + 2 * n for n in range(2)]
    from_i = lax.div(s, 2)
    from_mine = [jnp.logical_and(from_i == i, tj == j) for tj in from_j]
    for n in range(2):
        @pl.when(jnp.logical_not(from_mine[n]))
        def _():
            greet(from_i, from_j[n])

    local[0].wait()
    z0 = start_ref[...]
    start_dup = jnp.concatenate([z0, z0], axis=1)
    low = low_lanes[0:16]
    own_half = lax.div(lax.broadcasted_iota(jnp.int32, (16, 128), 1), C) == half
    pieces = [start_dup[0:16], start_dup[16:32], start_dup[32:48]]
    packed_start = jnp.concatenate([
        jnp.where(own_half, pieces[0], pieces[1]), jnp.where(own_half, pieces[2], 0.0)], axis=0).astype(BF16)
    zsrc[...] = packed_start
    sends_start = lax.rem(y, 2) == c

    @pl.when(sends_start)
    def _():
        yin[8 * half + z] = packed_start

    local[1].wait()
    packed_noise = jnp.concatenate([noise_ref[0], noise_ref[1]], axis=1)
    nsrc[...] = packed_noise
    nin[i] = packed_noise

    alone_count = base_mine[0].astype(jnp.int32) + base_mine[1].astype(jnp.int32)
    pl.semaphore_wait(barrier, 15 + 31 + 2 - alone_count)

    @pl.when(sends_start)
    def _():
        column(lambda tj: push(zsrc, yin.at[8 * half + z], ys, yr, i, tj))


    first = ws_ref[0]
    index = (lax.broadcasted_iota(jnp.int32, (STEPS, 128), 0) + first).astype(F32)
    sigma_now = sigma_of(index)
    delta = sigma_of(index + 1.0) - sigma_now
    coeff = ETA * jnp.sqrt(-delta)
    delta_ref[...] = delta
    coeff_ref[...] = coeff
    own = sigma_of((jnp.zeros((STEPS, 128), jnp.int32) + (first + s)).astype(F32))
    lane = lax.broadcasted_iota(jnp.int32, (STEPS, 128), 1).astype(F32)
    angle = 1000.0 * own * jnp.exp(-math.log(10000.0) * lane / 128)
    feats = jnp.concatenate([jnp.cos(angle), jnp.sin(angle)], axis=1)
    feats = (feats / (1.0 + jnp.exp(-feats))).astype(BF16)
    right[192:256] = jnp.zeros((64, D), BF16)
    for n in range(2):
        ztr[128 * n + 64:128 * n + 128] = jnp.where(
            lax.broadcasted_iota(jnp.int32, (64, KBLK), 0) == 0, 1.0, 0.0).astype(BF16)

    for copy in local[3:5]:
        copy.wait()
    local[2].wait()
    temb = mm(feats, wtime[...])

    emb = left[0:64].astype(F32)
    gain = gain_ref[...]
    for n, part in enumerate(split(jnp.concatenate([emb * gain, temb * gain], axis=0))):
        fold[n * 80:(n + 1) * 80] = part
    for n, part in enumerate(split(temb)):
        left[64 + 16 * n:80 + 16 * n] = part
    t_row = temb[0:1]
    twice_et = 2.0 * jnp.sum(emb * t_row, axis=1, keepdims=True)
    t_square = jnp.sum(t_row * t_row, axis=1, keepdims=True)

    each(1, COLS, lambda k: push(nsrc, nin.at[i], ns, nr, lax.rem(i + k, COLS), j))

    for copy in local[5:]:
        copy.wait()
    folded = mm(fold[...], wall[...])
    folded = folded[0:80] + folded[80:160]
    @pl.when(sends_start)
    def _():
        await_bytes(yin.at[0:15], yr)

    @pl.when(jnp.logical_not(sends_start))
    def _():
        await_bytes(yin, yr)

    for n in range(8):
        below, above = yin[n].astype(F32), yin[8 + n].astype(F32)
        there = rows_of(8 * c + n)
        zp[0, there, :] = jnp.where(low, below[0:16], above[0:16]).astype(BF16)
        zp[1, there, :] = pltpu.roll(jnp.where(low, above[0:16], below[0:16]), C, 1).astype(BF16)
        zp[2, there, :] = jnp.where(low, below[16:32], above[16:32]).astype(BF16)
    core_rows = pl.ds(pl.multiple_of(128 * c, 128), 128)
    push(zp.at[:, core_rows, :], zp.at[:, core_rows, :], cs, cr, i + 1 - 2 * c, j)

    both = lax.dot_general(left[...], right[...], (((1,), (1,)), ((), ())), preferred_element_type=F32)
    cdup = both[0:64, 0:128]
    gram = both[0:64, 128:256]
    mout = both[96:224, 0:128]
    lanes64 = lax.broadcasted_iota(jnp.int32, (64, 128), 1)
    diag = jnp.concatenate([jnp.where(lanes64 < C, cdup, 0.0), jnp.where(lanes64 < C, 0.0, cdup)], axis=0)
    for n, part in enumerate(split(diag)):
        cdiag[n * 128:(n + 1) * 128] = part
    crow[...] = both[64:72, 0:128] + both[80:88, 0:128]

    value_fold = jnp.dot(folded[:, 256:384], mout, precision=lax.Precision.HIGHEST, preferred_element_type=F32)
    wide = jnp.concatenate([folded[:, 0:256], value_fold], axis=1)
    wide = jnp.concatenate([wide, jnp.zeros((48, 384), F32)], axis=0).T
    wide = jnp.concatenate([wide[0:320], jnp.where(lanes64 == C, twice_et, gram)], axis=0)
    whi = wide.astype(BF16)
    wqkv[:, 0:128] = whi
    wqkv[:, 128:256] = (wide - whi.astype(F32)).astype(BF16)
    scale_row = qg_ref[...] * kg_ref[...] * (math.log2(math.e) / math.sqrt(HEAD))
    scale_col = jnp.broadcast_to(scale_row, (128, 128)).T[:, 0:1]

    step_row = lax.broadcasted_iota(jnp.int32, (STEPS, 128), 0)
    coeff_even = jnp.sum(jnp.where(step_row == 2 * i, coeff, 0.0), axis=0, keepdims=True)
    coeff_odd = jnp.sum(jnp.where(step_row == 2 * i + 1, coeff, 0.0), axis=0, keepdims=True)

    def send_base():
        await_bytes(nin.at[0:COLS - 1], nr)

        def noise_of(step_pair):
            both = nin[step_pair].astype(F32)
            turned = pltpu.roll(both, C, 1)
            return jnp.where(low_lanes, both, turned), jnp.where(low_lanes, turned, both)

        base = start_dup
        for pair in range(COLS):
            even, odd = noise_of(pair)
            pair_sum = coeff_ref[2 * pair:2 * pair + 1] * even + coeff_ref[2 * pair + 1:2 * pair + 2] * odd
            base = base + jnp.where(pair < i, pair_sum, 0.0)
        own_even, own_odd = noise_of(i)
        after_even = base + coeff_even * own_even
        after_odd = after_even + coeff_odd * own_odd
        basesrc[0] = base
        basesrc[1] = after_even
        basesrc[2] = after_odd
        for n in range(2):
            @pl.when(base_mine[n])
            def _():
                basein[half] = basesrc[n]

            @pl.when(jnp.logical_not(base_mine[n]))
            def _():
                push(basesrc.at[n], basein.at[half], bs.at[n], br.at[half], source_i, base_j[n])

    chunk = rows_of(pos)
    low = low_lanes[0:16]

    def project(lap, n):
        packed = latents[lap, n].T
        zb = jnp.concatenate([packed[0:64], packed[64:128]], axis=1)
        ztr[0:64] = zb
        ztr[128:192] = zb
        cols = slice(n * KBLK, (n + 1) * KBLK)
        out = mm(wqkv[...], ztr[...])
        yq, yk, yv, yg = out[0:128], out[128:256], out[256:320], out[320:384]
        mean_square = (jnp.sum(zb.astype(F32) * yg, axis=0, keepdims=True) + t_square) * (1.0 / D)
        square = jnp.maximum(mean_square, 0.0) + EPS
        aq = lax.rsqrt(jnp.mean(yq * yq, axis=0, keepdims=True) + EPS * square)
        ak = lax.rsqrt(jnp.mean(yk * yk, axis=0, keepdims=True) + EPS * square)
        kbuf[:, cols] = (yk * ak).astype(BF16)
        rows = jnp.concatenate([yq * aq * scale_col, yv * lax.rsqrt(square), jnp.ones((C, KBLK), F32)], axis=0)
        qvbuf[cols, :] = rows.astype(BF16).T

    def attend(block, keys, accs):
        out = []
        for side in range(2):
            q = qvbuf[block * KBLK + side * QBLK:block * KBLK + (side + 1) * QBLK, 0:HEAD]
            acc = accs[side]
            for m in keys:
                here = slice(m * KBLK, (m + 1) * KBLK)
                weights = jnp.exp2(mm(q, kbuf[:, here])).astype(BF16)
                part = mm(weights, qvbuf[here, HEAD:])
                acc = part if acc is None else acc + part
            out.append(acc)
        return out

    low_block = lax.broadcasted_iota(jnp.int32, (QBLK, 128), 1) < C

    def finish(lap, block, accs):
        first_acc, second_acc = accs
        heads[lap, block] = jnp.where(
            low_block, first_acc / pltpu.roll(first_acc, C, 1), pltpu.roll(second_acc, C, 1) / second_acc).astype(BF16)
        group(lambda n, ti, tj: push(
            heads.at[lap, block, rows_of(n), :], red.at[lap, block, pos], us.at[lap], ur.at[lap, block], ti, tj))

    def reduce_heads(lap, block):
        red[lap, block, pos] = heads[lap, block, chunk, :]
        latent = latents[lap, block, chunk, :]
        total = mm(jnp.concatenate([latent, latent], axis=1), cdiag[...]) + crow[0:1]
        await_bytes(red.at[lap, block, 0:STEPS - 1], ur.at[lap, block])
        for h in range(STEPS):
            total = total + red[lap, block, h].astype(F32)
        return total

    def pack_first(lap, first_part, second_part):
        vpack[lap, 0, 0:16] = jnp.where(low, first_part, pltpu.roll(second_part, C, 1)).astype(BF16)
        vpack[lap, 1, 0:16] = jnp.where(low, pltpu.roll(first_part, C, 1), second_part).astype(BF16)

    def pack_last(lap, part):
        vpack[lap, 0, 16:32] = jnp.where(low, part, 0.0).astype(BF16)
        vpack[lap, 1, 16:32] = jnp.where(low, pltpu.roll(part, C, 1), 0.0).astype(BF16)

    first_i = lax.div(s, 2)

    alone = jnp.logical_and(own_chunk == pos, first_i <= i)

    def to_owners(src, dst, rows, n):
        @pl.when(alone)
        def _():
            dst[s, rows] = src[half, rows]

        def one(k):
            to_i = k // 2
            to_j = first_block + 2 * (k % 2)
            mine = jnp.logical_and(to_i == i, to_j == j)

            @pl.when(jnp.logical_and(to_i >= first_i, jnp.logical_not(mine)))
            def _():
                push(src.at[k % 2, rows], dst.at[s, rows], fs.at[n], fr.at[n], to_i, to_j)
        each(0, 16, one)

    def owners_sent(dst, rows, n):
        for pair in range(COLS):
            for own in range(2):
                @pl.when(jnp.logical_and(first_i == pair, alone == (own == 1)))
                def _():
                    await_bytes(dst.at[0:2 * (COLS - pair) - own, rows], fs.at[n])

    def owner_sums(dst, rows, n):
        for pair in range(COLS):
            for own in range(2):
                @pl.when(jnp.logical_and(i == pair, alone == (own == 1)))
                def _():
                    await_bytes(dst.at[0:2 * pair + 2 - own, rows], fr.at[n])
        even = jnp.zeros((rows.stop - rows.start, 128), F32)
        odd = even
        for k in range(STEPS):
            later = delta_ref[k:k + 1] * dst[k, rows].astype(F32)
            even = even + jnp.where(k <= 2 * i, later, 0.0)
            odd = odd + jnp.where(k == 2 * i + 1, later, 0.0)
        return even, even + odd

    all_rows, early_rows, late_rows = slice(0, 32), slice(0, 16), slice(16, 32)
    blocks = range(3)
    velocities = {}

    def sum_heads(block):
        velocities[block] = reduce_heads(0, block)
        vsrc[block] = velocities[block].astype(BF16)
        gat[block, s] = velocities[block].astype(BF16)

        def send(k):
            to = lax.rem(s + k, STEPS)
            push(vsrc.at[block], gat.at[block, s], gs.at[block], gr.at[block], i, seq_of(to, p))
        each(1, STEPS, send)

    def next_latent(block):
        rows = slice(block * 16, (block + 1) * 16)
        latent = jnp.where(low, basein[0, rows], basein[1, rows])
        await_bytes(gat.at[block, 0:STEPS - 1], gr.at[block])
        for n in range(STEPS):
            latent = latent + jnp.where(n < s, delta_ref[n:n + 1] * gat[block, n].astype(F32), 0.0)
        latent = latent.astype(BF16)
        zsend[block] = latent
        latents[1, block, chunk, :] = latent
        group(lambda n, ti, tj: push(
            zsend.at[block], latents.at[1, block, chunk, :], ps.at[block], pr.at[block], ti, tj))

    def await_latents(block):
        await_bytes(latents.at[1, block, 0:15 * 16, :], pr.at[block])

    await_bytes(zp.at[:, 0:128, :], cr)
    for block in blocks:
        project(0, block)
    for block in blocks:
        finish(0, block, attend(block, blocks, (None, None)))
        if block:
            sum_heads(block - 1)
    send_base()
    sum_heads(2)
    for n in range(2):
        @pl.when(jnp.logical_not(from_mine[n]))
        def _():
            await_bytes(basein.at[n], br.at[n])
    next_latent(0)
    next_latent(1)
    pack_first(0, velocities[0], velocities[1])
    pack_last(0, velocities[2])

    await_latents(0)
    project(1, 0)
    next_latent(2)
    to_owners(vpack.at[0], fin0, all_rows, 0)
    await_latents(1)
    project(1, 1)
    early = [attend(block, (0, 1), (None, None)) for block in (0, 1)]
    await_latents(2)
    project(1, 2)
    for block in (0, 1):
        finish(1, block, attend(block, (2,), early[block]))
    finish(1, 2, attend(2, blocks, (None, None)))
    pack_first(1, reduce_heads(1, 0), reduce_heads(1, 1))
    to_owners(vpack.at[1], fin1, early_rows, 1)
    first_sums[0], first_sums[1] = owner_sums(fin0, all_rows, 0)
    pack_last(1, reduce_heads(1, 2))
    to_owners(vpack.at[1], fin1, late_rows, 2)

    even, odd = (
        jnp.concatenate(parts, axis=0) for parts in zip(owner_sums(fin1, early_rows, 1), owner_sums(fin1, late_rows, 2)))
    change_even = even - first_sums[0]
    change_odd = odd - first_sums[1]

    def unpack(x):
        return jnp.concatenate([x[0:16], pltpu.roll(x[0:16], C, 1), x[16:32]], axis=0)

    row = lax.broadcasted_iota(jnp.int32, (2, 128), 0)
    sum_even = jnp.sum(change_even * change_even, axis=0, keepdims=True)
    sum_odd = jnp.sum(change_odd * change_odd, axis=0, keepdims=True)
    partial = jnp.where(row == 0, sum_even, sum_odd)
    esrc[...] = partial
    ein[j] = partial
    column(lambda tj: push(esrc, ein.at[j], es, er, i, tj))
    for n, total in enumerate((basesrc[1] + unpack(even), basesrc[2] + unpack(odd))):
        out_ref[n] = total[:, 0:C]
    for lap in range(2):
        await_bytes(red.at[lap, :, 0:STEPS - 1], us.at[lap])
    for block in blocks:
        await_bytes(gat.at[block, 0:STEPS - 1], gs.at[block])
        await_bytes(latents.at[1, block, 0:15 * 16, :], ps.at[block])
    owners_sent(fin0, all_rows, 0)
    owners_sent(fin1, early_rows, 1)
    owners_sent(fin1, late_rows, 2)
    @pl.when(sends_start)
    def _():
        await_bytes(wall.at[0:31 * 32, 0:128], ys)

    await_bytes(nin.at[0:COLS - 1], ns)
    await_bytes(zp.at[:, 0:128, :], cs)
    for n in range(2):
        @pl.when(jnp.logical_not(base_mine[n]))
        def _():
            await_bytes(basesrc.at[n], bs.at[n])

    await_bytes(ein.at[0:SEQ - 1], er)
    total = ein[0]
    for n in range(1, SEQ):
        total = total + ein[n]
    total = total * (1.0 / (LEN * C))
    err_ref[0] = jnp.sum(total[0:1] / (coeff_even * coeff_even))
    err_ref[1] = jnp.sum(total[1:2] / (coeff_odd * coeff_odd))

    await_bytes(ein.at[0:SEQ - 1], es)


def per_device(
    start_latent, noise, window_start, w_embed, w_time, norm_gain, w_query, w_key, w_value, query_gain, key_gain, w_out, w_final,
):
    vmem = pl.BlockSpec(memory_space=pltpu.VMEM)
    hbm = pl.BlockSpec(memory_space=pltpu.HBM)
    smem = pl.BlockSpec(memory_space=pltpu.SMEM)
    dma = pltpu.SemaphoreType.DMA
    out, errors = pl.pallas_call(
        kernel,
        out_shape=(
            pltpu.VMEM((2, ROWS, C), F32),
            pltpu.SMEM((2,), F32),
        ),
        in_specs=[smem] + [hbm] * 12,
        out_specs=(vmem, smem),
        scratch_shapes=[
            pltpu.VMEM((ROWS, C), F32),
            pltpu.VMEM((2, ROWS, C), BF16),
            pltpu.VMEM((1, D), F32),
            pltpu.VMEM((1, HEAD), F32),
            pltpu.VMEM((1, HEAD), F32),
            pltpu.VMEM((256, D), BF16),
            pltpu.VMEM((D, 3 * HEAD), BF16),
            pltpu.VMEM((160, D), BF16),
            pltpu.VMEM((224, D), BF16),
            pltpu.VMEM((256, D), BF16),
            pltpu.VMEM((384, 256), BF16),
            pltpu.VMEM((256, 128), BF16),
            pltpu.VMEM((8, 128), F32),
            pltpu.VMEM((STEPS, 128), F32),
            pltpu.VMEM((STEPS, 128), F32),
            pltpu.VMEM((32, 128), BF16),
            pltpu.VMEM((16, 32, 128), BF16),
            pltpu.VMEM((ROWS, 128), BF16),
            pltpu.VMEM((COLS, ROWS, 128), BF16),
            pltpu.VMEM((3, ROWS, 128), F32),
            pltpu.VMEM((2, ROWS, 128), F32),
            pltpu.VMEM((2, 3, QBLK, 128), BF16),
            pltpu.VMEM((2, 3, QBLK, 128), BF16),
            pltpu.VMEM((2, 3, STEPS, 16, 128), BF16),
            pltpu.VMEM((3, 16, 128), BF16),
            pltpu.VMEM((2, 2, 32, 128), BF16),
            pltpu.VMEM((3, STEPS, 16, 128), BF16),
            pltpu.VMEM((3, 16, 128), BF16),
            pltpu.VMEM((STEPS, 32, 128), BF16),
            pltpu.VMEM((STEPS, 32, 128), BF16),
            pltpu.VMEM((2, 32, 128), F32),
            pltpu.VMEM((2, 128), F32),
            pltpu.VMEM((SEQ, 2, 128), F32),
            pltpu.VMEM((256, KBLK), BF16),
            pltpu.VMEM((HEAD, LEN), BF16),
            pltpu.VMEM((LEN, 2 * HEAD), BF16),
            dma((14,)),
            dma, dma, dma, dma, dma, dma, dma((2,)), dma((2,)),
            dma((2,)), dma((2, 3)), dma((3,)), dma((3,)), dma((3,)), dma((3,)), dma((3,)), dma((3,)), dma, dma,
        ],
        compiler_params=pltpu.CompilerParams(
            collective_id=0, has_side_effects=True, vmem_limit_bytes=56 * 1024 * 1024),
    )(
        window_start, start_latent, noise, norm_gain.reshape(1, D), query_gain.reshape(1, HEAD), key_gain.reshape(1, HEAD),
        w_embed, w_time, w_final.T, w_query, w_key, w_value, w_out,
    )
    return out, errors


def solution(mesh):
    return jax.shard_map(
        per_device,
        mesh=mesh,
        in_specs=(
            P("seq", None), P("step", "seq", None), P(), P(), P(), P(),
            P(None, "step"), P(None, "step"), P(None, "step"), P(), P(), P("step", None), P(),
        ),
        out_specs=(P("step", "seq", None), P("step")),
        check_vma=False,
    )
```

```python
import math

import jax
import jax.numpy as jnp
from jax import lax
from jax.experimental import pallas as pl
from jax.experimental.pallas import tpu as pltpu
from jax.sharding import PartitionSpec as P

NSCHED = 28
EPS = 1e-06
SHIFT = 3.0
ETA = 0.5
MESH = pl.DeviceIdType.MESH
F32 = jnp.float32
BF16 = jnp.bfloat16

D = 3072
C = 64
HEAD = 128
LEN = 1536
HALF = LEN // 2
STEPS = 16
ROWS = 48
SEQ = 32
COLS = 8
QBLK = 256
KBLK = 512


def sigma_of(index):
    fraction = 1.0 - index / NSCHED
    return SHIFT * fraction / (1.0 + (SHIFT - 1.0) * fraction)


def chunk_i(n):
    return 2 * lax.rem(n, 4) + lax.div(n, 8)


def chunk_p(n):
    return lax.rem(lax.div(n, 4), 2)


def seq_of(step, part):
    return 2 * step + lax.rem(step + part, 2)


def chunk_block(n):
    return 4 * lax.rem(n, 8) + lax.div(n, 8)


def split(x):
    hi = x.astype(BF16)
    return hi, (x - hi.astype(F32)).astype(BF16)


def mm(a, b):
    return jnp.dot(a, b, preferred_element_type=F32)


def kernel(
    ws_ref, start_hbm, noise_hbm, gain_hbm, qg_hbm, kg_hbm,
    wembed_hbm, wtime_hbm, wfinal_hbm, wq_hbm, wk_hbm, wv_hbm, wo_hbm,
    out_ref, err_ref,
    start_ref, noise_ref, gain_ref, qg_ref, kg_ref,
    wtime, wall, fold, left, right, wqkv, cdiag, crow,
    delta_ref, coeff_ref,
    zsrc, yin, nsrc, nin, basesrc, basein,
    latents, heads, red, vsrc, vpack, gat, zsend, fin0, fin1, first_sums, esrc, ein,
    ztr, kbuf, qvbuf,
    wsem, ys, yr, cs, cr, ns, nr, bs, br, us, ur, gs, gr, ps, pr, fs, fr, es, er,
):
    i = lax.axis_index("step")
    j = lax.axis_index("seq")
    x = lax.div(i, 2)
    c = lax.rem(i, 2)
    z = lax.div(j, 4)
    y = lax.rem(j, 4)
    s = lax.div(j, 2)
    p = lax.rem(j + s, 2)
    pos = 4 * (2 * c + p) + x
    own_chunk = 8 * lax.rem(y, 2) + z
    half = lax.div(y, 2)
    source_i = chunk_i(own_chunk)
    source_p = chunk_p(own_chunk)
    first_block = chunk_block(pos)
    low_lanes = lax.broadcasted_iota(jnp.int32, (ROWS, 128), 1) < C

    def rows_of(n):
        return pl.ds(pl.multiple_of(n * 16, 16), 16)

    def push(src, dst, send, recv, to_i, to_j):
        pltpu.make_async_remote_copy(
            src_ref=src, dst_ref=dst, send_sem=send, recv_sem=recv,
            device_id=(to_i, to_j), device_id_type=MESH,
        ).start()

    def await_bytes(like, sem):
        pltpu.make_async_copy(like, like, sem).wait()

    def each(low, high, fn):
        for k in range(low, high):
            fn(k)

    def group(fn):
        def one(k):
            n = lax.rem(pos + k, STEPS)
            fn(n, chunk_i(n), seq_of(s, chunk_p(n)))
        each(1, STEPS, one)

    zp = latents.at[0]

    def column(fn):
        each(1, SEQ, lambda k: fn(lax.rem(j + k, SEQ)))

    head = pl.multiple_of(p * HEAD, HEAD)
    pairs = [
        (start_hbm, start_ref), (noise_hbm, noise_ref), (wtime_hbm, wtime), (wembed_hbm, left.at[0:64, :]),
        (gain_hbm, gain_ref), (wembed_hbm, right.at[128:192, :]), (wfinal_hbm, right.at[0:64, :]),
        (wfinal_hbm, right.at[64:128, :]), (wo_hbm.at[pl.ds(head, HEAD), :], left.at[96:224, :]),
        (qg_hbm, qg_ref), (kg_hbm, kg_ref),
    ] + [
        (w.at[:, pl.ds(head, HEAD)], wall.at[:, n * HEAD:(n + 1) * HEAD]) for n, w in enumerate((wq_hbm, wk_hbm, wv_hbm))
    ]
    local = [pltpu.make_async_copy(src, dst, wsem.at[n]) for n, (src, dst) in enumerate(pairs)]
    for copy in local:
        copy.start()

    barrier = pltpu.get_barrier_semaphore()

    def greet(to_i, to_j):
        pl.semaphore_signal(barrier, inc=1, device_id=(to_i, to_j), device_id_type=MESH)

    group(lambda n, ti, tj: greet(ti, tj))
    column(lambda tj: greet(i, tj))
    base_j = [seq_of(2 * i + n, source_p) for n in range(2)]
    base_mine = [jnp.logical_and(source_i == i, tj == j) for tj in base_j]
    from_j = [first_block + 2 * n for n in range(2)]
    from_i = lax.div(s, 2)
    from_mine = [jnp.logical_and(from_i == i, tj == j) for tj in from_j]
    for n in range(2):
        @pl.when(jnp.logical_not(from_mine[n]))
        def _():
            greet(from_i, from_j[n])

    local[0].wait()
    z0 = start_ref[...]
    start_dup = jnp.concatenate([z0, z0], axis=1)
    low = low_lanes[0:16]
    own_half = lax.div(lax.broadcasted_iota(jnp.int32, (16, 128), 1), C) == half
    pieces = [start_dup[0:16], start_dup[16:32], start_dup[32:48]]
    packed_start = jnp.concatenate([
        jnp.where(own_half, pieces[0], pieces[1]), jnp.where(own_half, pieces[2], 0.0)], axis=0).astype(BF16)
    zsrc[...] = packed_start
    sends_start = lax.rem(y, 2) == c

    @pl.when(sends_start)
    def _():
        yin[8 * half + z] = packed_start

    local[1].wait()
    packed_noise = jnp.concatenate([noise_ref[0], noise_ref[1]], axis=1)
    nsrc[...] = packed_noise
    nin[i] = packed_noise

    alone_count = base_mine[0].astype(jnp.int32) + base_mine[1].astype(jnp.int32)
    pl.semaphore_wait(barrier, 15 + 31 + 2 - alone_count)

    @pl.when(sends_start)
    def _():
        column(lambda tj: push(zsrc, yin.at[8 * half + z], ys, yr, i, tj))


    first = ws_ref[0]
    index = (lax.broadcasted_iota(jnp.int32, (STEPS, 128), 0) + first).astype(F32)
    sigma_now = sigma_of(index)
    delta = sigma_of(index + 1.0) - sigma_now
    coeff = ETA * jnp.sqrt(-delta)
    delta_ref[...] = delta
    coeff_ref[...] = coeff
    own = sigma_of((jnp.zeros((STEPS, 128), jnp.int32) + (first + s)).astype(F32))
    lane = lax.broadcasted_iota(jnp.int32, (STEPS, 128), 1).astype(F32)
    angle = 1000.0 * own * jnp.exp(-math.log(10000.0) * lane / 128)
    feats = jnp.concatenate([jnp.cos(angle), jnp.sin(angle)], axis=1)
    feats = (feats / (1.0 + jnp.exp(-feats))).astype(BF16)
    right[192:256] = jnp.zeros((64, D), BF16)
    for n in range(2):
        ztr[128 * n + 64:128 * n + 128] = jnp.where(
            lax.broadcasted_iota(jnp.int32, (64, KBLK), 0) == 0, 1.0, 0.0).astype(BF16)

    for copy in local[3:5]:
        copy.wait()
    local[2].wait()
    temb = mm(feats, wtime[...])

    emb = left[0:64].astype(F32)
    gain = gain_ref[...]
    for n, part in enumerate(split(jnp.concatenate([emb * gain, temb * gain], axis=0))):
        fold[n * 80:(n + 1) * 80] = part
    for n, part in enumerate(split(temb)):
        left[64 + 16 * n:80 + 16 * n] = part
    t_row = temb[0:1]
    twice_et = 2.0 * jnp.sum(emb * t_row, axis=1, keepdims=True)
    t_square = jnp.sum(t_row * t_row, axis=1, keepdims=True)

    each(1, COLS, lambda k: push(nsrc, nin.at[i], ns, nr, lax.rem(i + k, COLS), j))

    for copy in local[5:]:
        copy.wait()
    folded = mm(fold[...], wall[...])
    folded = folded[0:80] + folded[80:160]
    @pl.when(sends_start)
    def _():
        await_bytes(yin.at[0:15], yr)

    @pl.when(jnp.logical_not(sends_start))
    def _():
        await_bytes(yin, yr)

    for n in range(8):
        below, above = yin[n].astype(F32), yin[8 + n].astype(F32)
        there = rows_of(8 * c + n)
        zp[0, there, :] = jnp.where(low, below[0:16], above[0:16]).astype(BF16)
        zp[1, there, :] = pltpu.roll(jnp.where(low, above[0:16], below[0:16]), C, 1).astype(BF16)
        zp[2, there, :] = jnp.where(low, below[16:32], above[16:32]).astype(BF16)
    core_rows = pl.ds(pl.multiple_of(128 * c, 128), 128)
    push(zp.at[:, core_rows, :], zp.at[:, core_rows, :], cs, cr, i + 1 - 2 * c, j)

    both = lax.dot_general(left[...], right[...], (((1,), (1,)), ((), ())), preferred_element_type=F32)
    cdup = both[0:64, 0:128]
    gram = both[0:64, 128:256]
    mout = both[96:224, 0:128]
    lanes64 = lax.broadcasted_iota(jnp.int32, (64, 128), 1)
    diag = jnp.concatenate([jnp.where(lanes64 < C, cdup, 0.0), jnp.where(lanes64 < C, 0.0, cdup)], axis=0)
    for n, part in enumerate(split(diag)):
        cdiag[n * 128:(n + 1) * 128] = part
    crow[...] = both[64:72, 0:128] + both[80:88, 0:128]

    value_fold = jnp.dot(folded[:, 256:384], mout, precision=lax.Precision.HIGHEST, preferred_element_type=F32)
    wide = jnp.concatenate([folded[:, 0:256], value_fold], axis=1)
    wide = jnp.concatenate([wide, jnp.zeros((48, 384), F32)], axis=0).T
    wide = jnp.concatenate([wide[0:320], jnp.where(lanes64 == C, twice_et, gram)], axis=0)
    whi = wide.astype(BF16)
    wqkv[:, 0:128] = whi
    wqkv[:, 128:256] = (wide - whi.astype(F32)).astype(BF16)
    scale_row = qg_ref[...] * kg_ref[...] * (math.log2(math.e) / math.sqrt(HEAD))
    scale_col = jnp.broadcast_to(scale_row, (128, 128)).T[:, 0:1]

    step_row = lax.broadcasted_iota(jnp.int32, (STEPS, 128), 0)
    coeff_even = jnp.sum(jnp.where(step_row == 2 * i, coeff, 0.0), axis=0, keepdims=True)
    coeff_odd = jnp.sum(jnp.where(step_row == 2 * i + 1, coeff, 0.0), axis=0, keepdims=True)

    def send_base():
        await_bytes(nin.at[0:COLS - 1], nr)

        def noise_of(step_pair):
            both = nin[step_pair].astype(F32)
            turned = pltpu.roll(both, C, 1)
            return jnp.where(low_lanes, both, turned), jnp.where(low_lanes, turned, both)

        base = start_dup
        for pair in range(COLS):
            even, odd = noise_of(pair)
            pair_sum = coeff_ref[2 * pair:2 * pair + 1] * even + coeff_ref[2 * pair + 1:2 * pair + 2] * odd
            base = base + jnp.where(pair < i, pair_sum, 0.0)
        own_even, own_odd = noise_of(i)
        after_even = base + coeff_even * own_even
        after_odd = after_even + coeff_odd * own_odd
        basesrc[0] = base
        basesrc[1] = after_even
        basesrc[2] = after_odd
        for n in range(2):
            @pl.when(base_mine[n])
            def _():
                basein[half] = basesrc[n]

            @pl.when(jnp.logical_not(base_mine[n]))
            def _():
                push(basesrc.at[n], basein.at[half], bs.at[n], br.at[half], source_i, base_j[n])

    chunk = rows_of(pos)
    low = low_lanes[0:16]

    def project(lap, n):
        packed = latents[lap, n].T
        zb = jnp.concatenate([packed[0:64], packed[64:128]], axis=1)
        ztr[0:64] = zb
        ztr[128:192] = zb
        cols = slice(n * KBLK, (n + 1) * KBLK)
        out = mm(wqkv[...], ztr[...])
        yq, yk, yv, yg = out[0:128], out[128:256], out[256:320], out[320:384]
        mean_square = (jnp.sum(zb.astype(F32) * yg, axis=0, keepdims=True) + t_square) * (1.0 / D)
        square = jnp.maximum(mean_square, 0.0) + EPS
        aq = lax.rsqrt(jnp.mean(yq * yq, axis=0, keepdims=True) + EPS * square)
        ak = lax.rsqrt(jnp.mean(yk * yk, axis=0, keepdims=True) + EPS * square)
        kbuf[:, cols] = (yk * ak).astype(BF16)
        rows = jnp.concatenate([yq * aq * scale_col, yv * lax.rsqrt(square), jnp.ones((C, KBLK), F32)], axis=0)
        qvbuf[cols, :] = rows.astype(BF16).T

    def attend(block, side, keys, acc=None):
        q = qvbuf[block * KBLK + side * QBLK:block * KBLK + (side + 1) * QBLK, 0:HEAD]
        for m in keys:
            here = slice(m * KBLK, (m + 1) * KBLK)
            weights = jnp.exp2(mm(q, kbuf[:, here])).astype(BF16)
            part = mm(weights, qvbuf[here, HEAD:])
            acc = part if acc is None else acc + part
        return acc

    low_block = lax.broadcasted_iota(jnp.int32, (QBLK, 128), 1) < C

    def finish(lap, block, first_acc, second_acc):
        heads[lap, block] = jnp.where(
            low_block, first_acc / pltpu.roll(first_acc, C, 1), pltpu.roll(second_acc, C, 1) / second_acc).astype(BF16)
        group(lambda n, ti, tj: push(
            heads.at[lap, block, rows_of(n), :], red.at[lap, block, pos], us.at[lap], ur.at[lap, block], ti, tj))

    def reduce_heads(lap, block):
        red[lap, block, pos] = heads[lap, block, chunk, :]
        latent = latents[lap, block, chunk, :]
        total = mm(jnp.concatenate([latent, latent], axis=1), cdiag[...]) + crow[0:1]
        await_bytes(red.at[lap, block, 0:STEPS - 1], ur.at[lap, block])
        for h in range(STEPS):
            total = total + red[lap, block, h].astype(F32)
        return total

    def pack_first(lap, first_part, second_part):
        vpack[lap, 0, 0:16] = jnp.where(low, first_part, pltpu.roll(second_part, C, 1)).astype(BF16)
        vpack[lap, 1, 0:16] = jnp.where(low, pltpu.roll(first_part, C, 1), second_part).astype(BF16)

    def pack_last(lap, part):
        vpack[lap, 0, 16:32] = jnp.where(low, part, 0.0).astype(BF16)
        vpack[lap, 1, 16:32] = jnp.where(low, pltpu.roll(part, C, 1), 0.0).astype(BF16)

    first_i = lax.div(s, 2)

    alone = jnp.logical_and(own_chunk == pos, first_i <= i)

    def to_owners(src, dst, rows, n):
        @pl.when(alone)
        def _():
            dst[s, rows] = src[half, rows]

        def one(k):
            to_i = k // 2
            to_j = first_block + 2 * (k % 2)
            mine = jnp.logical_and(to_i == i, to_j == j)

            @pl.when(jnp.logical_and(to_i >= first_i, jnp.logical_not(mine)))
            def _():
                push(src.at[k % 2, rows], dst.at[s, rows], fs.at[n], fr.at[n], to_i, to_j)
        each(0, 16, one)

    def owners_sent(dst, rows, n):
        for pair in range(COLS):
            for own in range(2):
                @pl.when(jnp.logical_and(first_i == pair, alone == (own == 1)))
                def _():
                    await_bytes(dst.at[0:2 * (COLS - pair) - own, rows], fs.at[n])

    def owner_sums(dst, rows, n):
        for pair in range(COLS):
            for own in range(2):
                @pl.when(jnp.logical_and(i == pair, alone == (own == 1)))
                def _():
                    await_bytes(dst.at[0:2 * pair + 2 - own, rows], fr.at[n])
        even = jnp.zeros((rows.stop - rows.start, 128), F32)
        odd = even
        for k in range(STEPS):
            later = delta_ref[k:k + 1] * dst[k, rows].astype(F32)
            even = even + jnp.where(k <= 2 * i, later, 0.0)
            odd = odd + jnp.where(k == 2 * i + 1, later, 0.0)
        return even, even + odd

    all_rows, early_rows, late_rows = slice(0, 32), slice(0, 16), slice(16, 32)
    blocks = range(3)
    velocities = {}

    def sum_heads(block):
        velocities[block] = reduce_heads(0, block)
        vsrc[block] = velocities[block].astype(BF16)
        gat[block, s] = velocities[block].astype(BF16)

        def send(k):
            to = lax.rem(s + k, STEPS)
            push(vsrc.at[block], gat.at[block, s], gs.at[block], gr.at[block], i, seq_of(to, p))
        each(1, STEPS, send)

    def next_latent(block):
        rows = slice(block * 16, (block + 1) * 16)
        latent = jnp.where(low, basein[0, rows], basein[1, rows])
        await_bytes(gat.at[block, 0:STEPS - 1], gr.at[block])
        for n in range(STEPS):
            latent = latent + jnp.where(n < s, delta_ref[n:n + 1] * gat[block, n].astype(F32), 0.0)
        latent = latent.astype(BF16)
        zsend[block] = latent
        latents[1, block, chunk, :] = latent
        group(lambda n, ti, tj: push(
            zsend.at[block], latents.at[1, block, chunk, :], ps.at[block], pr.at[block], ti, tj))

    def await_latents(block):
        await_bytes(latents.at[1, block, 0:15 * 16, :], pr.at[block])

    await_bytes(zp.at[:, 0:128, :], cr)
    for block in blocks:
        project(0, block)
    finish(0, 0, attend(0, 0, blocks), attend(0, 1, blocks))
    send_base()
    finish(0, 1, attend(1, 0, blocks), attend(1, 1, blocks))
    sum_heads(0)
    first_acc = attend(2, 0, blocks)
    sum_heads(1)
    for n in range(2):
        @pl.when(jnp.logical_not(from_mine[n]))
        def _():
            await_bytes(basein.at[n], br.at[n])
    next_latent(0)
    finish(0, 2, first_acc, attend(2, 1, blocks))
    next_latent(1)
    pack_first(0, velocities[0], velocities[1])

    await_latents(0)
    project(1, 0)
    early = {(0, 0): attend(0, 0, (0,))}
    sum_heads(2)
    pack_last(0, velocities[2])
    early[0, 1] = attend(0, 1, (0,))
    await_latents(1)
    project(1, 1)
    next_latent(2)
    for side in range(2):
        early[0, side] = attend(0, side, (1,), early[0, side])
        early[1, side] = attend(1, side, (0, 1))
    to_owners(vpack.at[0], fin0, all_rows, 0)
    await_latents(2)
    project(1, 2)
    for block in (0, 1):
        finish(1, block, *(attend(block, side, (2,), early[block, side]) for side in range(2)))
    first_acc = attend(2, 0, blocks)
    pack_first(1, reduce_heads(1, 0), reduce_heads(1, 1))
    to_owners(vpack.at[1], fin1, early_rows, 1)
    finish(1, 2, first_acc, attend(2, 1, blocks))
    first_sums[0], first_sums[1] = owner_sums(fin0, all_rows, 0)
    pack_last(1, reduce_heads(1, 2))
    to_owners(vpack.at[1], fin1, late_rows, 2)

    even, odd = (
        jnp.concatenate(parts, axis=0) for parts in zip(owner_sums(fin1, early_rows, 1), owner_sums(fin1, late_rows, 2)))
    change_even = even - first_sums[0]
    change_odd = odd - first_sums[1]

    def unpack(x):
        return jnp.concatenate([x[0:16], pltpu.roll(x[0:16], C, 1), x[16:32]], axis=0)

    row = lax.broadcasted_iota(jnp.int32, (2, 128), 0)
    sum_even = jnp.sum(change_even * change_even, axis=0, keepdims=True)
    sum_odd = jnp.sum(change_odd * change_odd, axis=0, keepdims=True)
    partial = jnp.where(row == 0, sum_even, sum_odd)
    esrc[...] = partial
    ein[j] = partial
    column(lambda tj: push(esrc, ein.at[j], es, er, i, tj))
    for n, total in enumerate((basesrc[1] + unpack(even), basesrc[2] + unpack(odd))):
        out_ref[n] = total[:, 0:C]
    for lap in range(2):
        await_bytes(red.at[lap, :, 0:STEPS - 1], us.at[lap])
    for block in blocks:
        await_bytes(gat.at[block, 0:STEPS - 1], gs.at[block])
        await_bytes(latents.at[1, block, 0:15 * 16, :], ps.at[block])
    owners_sent(fin0, all_rows, 0)
    owners_sent(fin1, early_rows, 1)
    owners_sent(fin1, late_rows, 2)
    @pl.when(sends_start)
    def _():
        await_bytes(wall.at[0:31 * 32, 0:128], ys)

    await_bytes(nin.at[0:COLS - 1], ns)
    await_bytes(zp.at[:, 0:128, :], cs)
    for n in range(2):
        @pl.when(jnp.logical_not(base_mine[n]))
        def _():
            await_bytes(basesrc.at[n], bs.at[n])

    await_bytes(ein.at[0:SEQ - 1], er)
    total = ein[0]
    for n in range(1, SEQ):
        total = total + ein[n]
    total = total * (1.0 / (LEN * C))
    err_ref[0] = jnp.sum(total[0:1] / (coeff_even * coeff_even))
    err_ref[1] = jnp.sum(total[1:2] / (coeff_odd * coeff_odd))

    await_bytes(ein.at[0:SEQ - 1], es)


def per_device(
    start_latent, noise, window_start, w_embed, w_time, norm_gain, w_query, w_key, w_value, query_gain, key_gain, w_out, w_final,
):
    vmem = pl.BlockSpec(memory_space=pltpu.VMEM)
    hbm = pl.BlockSpec(memory_space=pltpu.HBM)
    smem = pl.BlockSpec(memory_space=pltpu.SMEM)
    dma = pltpu.SemaphoreType.DMA
    out, errors = pl.pallas_call(
        kernel,
        out_shape=(
            pltpu.VMEM((2, ROWS, C), F32),
            pltpu.SMEM((2,), F32),
        ),
        in_specs=[smem] + [hbm] * 12,
        out_specs=(vmem, smem),
        scratch_shapes=[
            pltpu.VMEM((ROWS, C), F32),
            pltpu.VMEM((2, ROWS, C), BF16),
            pltpu.VMEM((1, D), F32),
            pltpu.VMEM((1, HEAD), F32),
            pltpu.VMEM((1, HEAD), F32),
            pltpu.VMEM((256, D), BF16),
            pltpu.VMEM((D, 3 * HEAD), BF16),
            pltpu.VMEM((160, D), BF16),
            pltpu.VMEM((224, D), BF16),
            pltpu.VMEM((256, D), BF16),
            pltpu.VMEM((384, 256), BF16),
            pltpu.VMEM((256, 128), BF16),
            pltpu.VMEM((8, 128), F32),
            pltpu.VMEM((STEPS, 128), F32),
            pltpu.VMEM((STEPS, 128), F32),
            pltpu.VMEM((32, 128), BF16),
            pltpu.VMEM((16, 32, 128), BF16),
            pltpu.VMEM((ROWS, 128), BF16),
            pltpu.VMEM((COLS, ROWS, 128), BF16),
            pltpu.VMEM((3, ROWS, 128), F32),
            pltpu.VMEM((2, ROWS, 128), F32),
            pltpu.VMEM((2, 3, QBLK, 128), BF16),
            pltpu.VMEM((2, 3, QBLK, 128), BF16),
            pltpu.VMEM((2, 3, STEPS, 16, 128), BF16),
            pltpu.VMEM((3, 16, 128), BF16),
            pltpu.VMEM((2, 2, 32, 128), BF16),
            pltpu.VMEM((3, STEPS, 16, 128), BF16),
            pltpu.VMEM((3, 16, 128), BF16),
            pltpu.VMEM((STEPS, 32, 128), BF16),
            pltpu.VMEM((STEPS, 32, 128), BF16),
            pltpu.VMEM((2, 32, 128), F32),
            pltpu.VMEM((2, 128), F32),
            pltpu.VMEM((SEQ, 2, 128), F32),
            pltpu.VMEM((256, KBLK), BF16),
            pltpu.VMEM((HEAD, LEN), BF16),
            pltpu.VMEM((LEN, 2 * HEAD), BF16),
            dma((14,)),
            dma, dma, dma, dma, dma, dma, dma((2,)), dma((2,)),
            dma((2,)), dma((2, 3)), dma((3,)), dma((3,)), dma((3,)), dma((3,)), dma((3,)), dma((3,)), dma, dma,
        ],
        compiler_params=pltpu.CompilerParams(
            collective_id=0, has_side_effects=True, vmem_limit_bytes=56 * 1024 * 1024),
    )(
        window_start, start_latent, noise, norm_gain.reshape(1, D), query_gain.reshape(1, HEAD), key_gain.reshape(1, HEAD),
        w_embed, w_time, w_final.T, w_query, w_key, w_value, w_out,
    )
    return out, errors


def solution(mesh):
    return jax.shard_map(
        per_device,
        mesh=mesh,
        in_specs=(
            P("seq", None), P("step", "seq", None), P(), P(), P(), P(),
            P(None, "step"), P(None, "step"), P(None, "step"), P(), P(), P("step", None), P(),
        ),
        out_specs=(P("step", "seq", None), P("step")),
        check_vma=False,
    )
```

```python
import math

import jax
import jax.numpy as jnp
from jax import lax
from jax.experimental import pallas as pl
from jax.experimental.pallas import tpu as pltpu
from jax.sharding import PartitionSpec as P

NSCHED = 28
EPS = 1e-06
SHIFT = 3.0
ETA = 0.5
MESH = pl.DeviceIdType.MESH
F32 = jnp.float32
BF16 = jnp.bfloat16

D = 3072
C = 64
HEAD = 128
LEN = 1536
HALF = LEN // 2
STEPS = 16
ROWS = 48
SEQ = 32
COLS = 8
QBLK = 256
KBLK = 512


def sigma_of(index):
    fraction = 1.0 - index / NSCHED
    return SHIFT * fraction / (1.0 + (SHIFT - 1.0) * fraction)


def chunk_i(n):
    return 2 * lax.rem(n, 4) + lax.div(n, 8)


def chunk_p(n):
    return lax.rem(lax.div(n, 4), 2)


def seq_of(step, part):
    return 2 * step + lax.rem(step + part, 2)


def chunk_block(n):
    return 4 * lax.rem(n, 8) + lax.div(n, 8)


def split(x):
    hi = x.astype(BF16)
    return hi, (x - hi.astype(F32)).astype(BF16)


def mm(a, b):
    return jnp.dot(a, b, preferred_element_type=F32)


def kernel(
    ws_ref, start_hbm, noise_hbm, gain_hbm, qg_hbm, kg_hbm,
    wembed_hbm, wtime_hbm, wfinal_hbm, wq_hbm, wk_hbm, wv_hbm, wo_hbm,
    out_ref, err_ref,
    start_ref, noise_ref, gain_ref, qg_ref, kg_ref,
    wtime, wall, fold, left, right, wqkv, cdiag, crow,
    delta_ref, coeff_ref,
    zsrc, yin, nsrc, nin, basesrc, basein,
    latents, heads, red, vsrc, vpack, gat, zsend, fin0, fin1, first_sums, esrc, ein,
    ztr, kbuf, qbuf, vbuf,
    wsem, ys, yr, cs, cr, ns, nr, bs, br, us, ur, gs, gr, ps, pr, fs, fr, es, er,
):
    i = lax.axis_index("step")
    j = lax.axis_index("seq")
    x = lax.div(i, 2)
    c = lax.rem(i, 2)
    z = lax.div(j, 4)
    y = lax.rem(j, 4)
    s = lax.div(j, 2)
    p = lax.rem(j + s, 2)
    pos = 4 * (2 * c + p) + x
    own_chunk = 8 * lax.rem(y, 2) + z
    half = lax.div(y, 2)
    source_i = chunk_i(own_chunk)
    source_p = chunk_p(own_chunk)
    first_block = chunk_block(pos)
    low_lanes = lax.broadcasted_iota(jnp.int32, (ROWS, 128), 1) < C

    def rows_of(n):
        return pl.ds(pl.multiple_of(n * 16, 16), 16)

    def push(src, dst, send, recv, to_i, to_j):
        pltpu.make_async_remote_copy(
            src_ref=src, dst_ref=dst, send_sem=send, recv_sem=recv,
            device_id=(to_i, to_j), device_id_type=MESH,
        ).start()

    def await_bytes(like, sem):
        pltpu.make_async_copy(like, like, sem).wait()

    def each(low, high, fn):
        for k in range(low, high):
            fn(k)

    def group(fn):
        def one(k):
            n = lax.rem(pos + k, STEPS)
            fn(n, chunk_i(n), seq_of(s, chunk_p(n)))
        for k in sorted(range(1, STEPS), key=lambda k: -min(k % 4, -k % 4)):
            one(k)

    zp = latents.at[0]

    def column(fn):
        for k in sorted(range(1, SEQ), key=lambda k: abs(k - SEQ // 2)):
            fn(lax.rem(j + k, SEQ))

    barrier = pltpu.get_barrier_semaphore()

    def greet(to_i, to_j):
        pl.semaphore_signal(barrier, inc=1, device_id=(to_i, to_j), device_id_type=MESH)

    group(lambda n, ti, tj: greet(ti, tj))
    column(lambda tj: greet(i, tj))
    base_j = [seq_of(2 * i + n, source_p) for n in range(2)]
    base_mine = [jnp.logical_and(source_i == i, tj == j) for tj in base_j]
    from_j = [first_block + 2 * n for n in range(2)]
    from_i = lax.div(s, 2)
    from_mine = [jnp.logical_and(from_i == i, tj == j) for tj in from_j]
    for n in range(2):
        @pl.when(jnp.logical_not(from_mine[n]))
        def _():
            greet(from_i, from_j[n])

    head = pl.multiple_of(p * HEAD, HEAD)
    pairs = [
        (start_hbm, start_ref), (noise_hbm, noise_ref), (wtime_hbm, wtime), (wembed_hbm, left.at[0:64, :]),
        (gain_hbm, gain_ref), (wembed_hbm, right.at[128:192, :]), (wfinal_hbm, right.at[0:64, :]),
        (wfinal_hbm, right.at[64:128, :]), (wo_hbm.at[pl.ds(head, HEAD), :], left.at[96:224, :]),
        (qg_hbm, qg_ref), (kg_hbm, kg_ref),
    ] + [
        (w.at[:, pl.ds(head, HEAD)], wall.at[:, n * HEAD:(n + 1) * HEAD]) for n, w in enumerate((wq_hbm, wk_hbm, wv_hbm))
    ]
    local = [pltpu.make_async_copy(src, dst, wsem.at[n]) for n, (src, dst) in enumerate(pairs)]
    for copy in local:
        copy.start()

    local[0].wait()
    z0 = start_ref[...]
    start_dup = jnp.concatenate([z0, z0], axis=1)
    low = low_lanes[0:16]
    own_half = lax.div(lax.broadcasted_iota(jnp.int32, (16, 128), 1), C) == half
    pieces = [start_dup[0:16], start_dup[16:32], start_dup[32:48]]
    packed_start = jnp.concatenate([
        jnp.where(own_half, pieces[0], pieces[1]), jnp.where(own_half, pieces[2], 0.0)], axis=0).astype(BF16)
    zsrc[...] = packed_start
    sends_start = lax.rem(y, 2) == c

    @pl.when(sends_start)
    def _():
        yin[8 * half + z] = packed_start

    local[1].wait()
    packed_noise = jnp.concatenate([noise_ref[0], noise_ref[1]], axis=1)
    nsrc[...] = packed_noise
    nin[i] = packed_noise

    alone_count = base_mine[0].astype(jnp.int32) + base_mine[1].astype(jnp.int32)
    pl.semaphore_wait(barrier, 15 + 31 + 2 - alone_count)

    @pl.when(sends_start)
    def _():
        column(lambda tj: push(zsrc, yin.at[8 * half + z], ys, yr, i, tj))


    first = ws_ref[0]
    index = (lax.broadcasted_iota(jnp.int32, (STEPS, 128), 0) + first).astype(F32)
    sigma_now = sigma_of(index)
    delta = sigma_of(index + 1.0) - sigma_now
    coeff = ETA * jnp.sqrt(-delta)
    delta_ref[...] = delta
    coeff_ref[...] = coeff
    own = sigma_of((jnp.zeros((STEPS, 128), jnp.int32) + (first + s)).astype(F32))
    lane = lax.broadcasted_iota(jnp.int32, (STEPS, 128), 1).astype(F32)
    angle = 1000.0 * own * jnp.exp(-math.log(10000.0) * lane / 128)
    feats = jnp.concatenate([jnp.cos(angle), jnp.sin(angle)], axis=1)
    feats = (feats / (1.0 + jnp.exp(-feats))).astype(BF16)
    right[192:256] = jnp.zeros((64, D), BF16)
    vbuf[C:C + 16] = jnp.ones((16, LEN), BF16)
    for n in range(2):
        ztr[128 * n + 64:128 * n + 128] = jnp.where(
            lax.broadcasted_iota(jnp.int32, (64, KBLK), 0) == 0, 1.0, 0.0).astype(BF16)

    for copy in local[3:5]:
        copy.wait()
    local[2].wait()
    temb = mm(feats, wtime[...])

    emb = left[0:64].astype(F32)
    gain = gain_ref[...]
    for n, part in enumerate(split(jnp.concatenate([emb * gain, temb * gain], axis=0))):
        fold[n * 80:(n + 1) * 80] = part
    for n, part in enumerate(split(temb)):
        left[64 + 16 * n:80 + 16 * n] = part
    t_row = temb[0:1]
    twice_et = 2.0 * jnp.sum(emb * t_row, axis=1, keepdims=True)
    t_square = jnp.sum(t_row * t_row, axis=1, keepdims=True)

    each(1, COLS, lambda k: push(nsrc, nin.at[i], ns, nr, lax.rem(i + k, COLS), j))

    for copy in local[5:]:
        copy.wait()
    folded = mm(fold[...], wall[...])
    folded = folded[0:80] + folded[80:160]
    @pl.when(sends_start)
    def _():
        await_bytes(yin.at[0:15], yr)

    @pl.when(jnp.logical_not(sends_start))
    def _():
        await_bytes(yin, yr)

    for n in range(8):
        below, above = yin[n].astype(F32), yin[8 + n].astype(F32)
        there = rows_of(8 * c + n)
        zp[0, there, :] = jnp.where(low, below[0:16], above[0:16]).astype(BF16)
        zp[1, there, :] = pltpu.roll(jnp.where(low, above[0:16], below[0:16]), C, 1).astype(BF16)
        zp[2, there, :] = jnp.where(low, below[16:32], above[16:32]).astype(BF16)
    core_rows = pl.ds(pl.multiple_of(128 * c, 128), 128)
    push(zp.at[:, core_rows, :], zp.at[:, core_rows, :], cs, cr, i + 1 - 2 * c, j)

    both = lax.dot_general(left[...], right[...], (((1,), (1,)), ((), ())), preferred_element_type=F32)
    cdup = both[0:64, 0:128]
    gram = both[0:64, 128:256]
    mout = both[96:224, 0:128]
    lanes64 = lax.broadcasted_iota(jnp.int32, (64, 128), 1)
    diag = jnp.concatenate([jnp.where(lanes64 < C, cdup, 0.0), jnp.where(lanes64 < C, 0.0, cdup)], axis=0)
    for n, part in enumerate(split(diag)):
        cdiag[n * 128:(n + 1) * 128] = part
    crow[...] = both[64:72, 0:128] + both[80:88, 0:128]

    value_fold = jnp.dot(folded[:, 256:384], mout, precision=lax.Precision.HIGHEST, preferred_element_type=F32)
    wide = jnp.concatenate([folded[:, 0:256], value_fold], axis=1)
    wide = jnp.concatenate([wide, jnp.zeros((48, 384), F32)], axis=0).T
    wide = jnp.concatenate([wide[0:320], jnp.where(lanes64 == C, twice_et, gram)], axis=0)
    whi = wide.astype(BF16)
    wqkv[:, 0:128] = whi
    wqkv[:, 128:256] = (wide - whi.astype(F32)).astype(BF16)
    scale_row = qg_ref[...] * kg_ref[...] * (math.log2(math.e) / math.sqrt(HEAD))
    scale_col = jnp.broadcast_to(scale_row, (128, 128)).T[:, 0:1]

    step_row = lax.broadcasted_iota(jnp.int32, (STEPS, 128), 0)
    coeff_even = jnp.sum(jnp.where(step_row == 2 * i, coeff, 0.0), axis=0, keepdims=True)
    coeff_odd = jnp.sum(jnp.where(step_row == 2 * i + 1, coeff, 0.0), axis=0, keepdims=True)

    def send_base():
        await_bytes(nin.at[0:COLS - 1], nr)

        def noise_of(step_pair):
            both = nin[step_pair].astype(F32)
            turned = pltpu.roll(both, C, 1)
            return jnp.where(low_lanes, both, turned), jnp.where(low_lanes, turned, both)

        base = start_dup
        for pair in range(COLS):
            even, odd = noise_of(pair)
            pair_sum = coeff_ref[2 * pair:2 * pair + 1] * even + coeff_ref[2 * pair + 1:2 * pair + 2] * odd
            base = base + jnp.where(pair < i, pair_sum, 0.0)
        own_even, own_odd = noise_of(i)
        after_even = base + coeff_even * own_even
        after_odd = after_even + coeff_odd * own_odd
        basesrc[0] = base
        basesrc[1] = after_even
        basesrc[2] = after_odd
        for n in range(2):
            @pl.when(base_mine[n])
            def _():
                basein[half] = basesrc[n]

            @pl.when(jnp.logical_not(base_mine[n]))
            def _():
                push(basesrc.at[n], basein.at[half], bs.at[n], br.at[half], source_i, base_j[n])

    chunk = rows_of(pos)
    low = low_lanes[0:16]

    def project(lap, n):
        packed = latents[lap, n].T
        zb = jnp.concatenate([packed[0:64], packed[64:128]], axis=1)
        ztr[0:64] = zb
        ztr[128:192] = zb
        cols = slice(n * KBLK, (n + 1) * KBLK)
        out = mm(wqkv[...], ztr[...])
        yq, yk, yv, yg = out[0:128], out[128:256], out[256:320], out[320:384]
        mean_square = (jnp.sum(zb.astype(F32) * yg, axis=0, keepdims=True) + t_square) * (1.0 / D)
        square = jnp.maximum(mean_square, 0.0) + EPS
        aq = lax.rsqrt(jnp.mean(yq * yq, axis=0, keepdims=True) + EPS * square)
        ak = lax.rsqrt(jnp.mean(yk * yk, axis=0, keepdims=True) + EPS * square)
        qbuf[:, cols] = (yq * aq * scale_col).astype(BF16)
        kbuf[cols, :] = (yk * ak).astype(BF16).T
        vbuf[0:C, cols] = (yv * lax.rsqrt(square)).astype(BF16)

    def attend(block, keys, accs):
        out = []
        for side in range(2):
            q = qbuf[:, block * KBLK + side * QBLK:block * KBLK + (side + 1) * QBLK]
            acc = accs[side]
            for m in keys:
                here = slice(m * KBLK, (m + 1) * KBLK)
                weights = jnp.exp2(mm(kbuf[here], q)).astype(BF16)
                part = mm(vbuf[:, here], weights)
                acc = part if acc is None else acc + part
            out.append(acc)
        return out

    def finish(lap, block, accs):
        outs = [acc[0:C] / acc[C:C + 1] for acc in accs]
        heads[lap, block] = jnp.concatenate(outs, axis=0).astype(BF16).T
        group(lambda n, ti, tj: push(
            heads.at[lap, block, rows_of(n), :], red.at[lap, block, pos], us.at[lap], ur.at[lap, block], ti, tj))

    def reduce_heads(lap, block):
        red[lap, block, pos] = heads[lap, block, chunk, :]
        latent = latents[lap, block, chunk, :]
        total = mm(jnp.concatenate([latent, latent], axis=1), cdiag[...]) + crow[0:1]
        await_bytes(red.at[lap, block, 0:STEPS - 1], ur.at[lap, block])
        for h in range(STEPS):
            total = total + red[lap, block, h].astype(F32)
        return total

    def pack_first(lap, first_part, second_part):
        vpack[lap, 0, 0:16] = jnp.where(low, first_part, pltpu.roll(second_part, C, 1)).astype(BF16)
        vpack[lap, 1, 0:16] = jnp.where(low, pltpu.roll(first_part, C, 1), second_part).astype(BF16)

    def pack_last(lap, part):
        vpack[lap, 0, 16:32] = jnp.where(low, part, 0.0).astype(BF16)
        vpack[lap, 1, 16:32] = jnp.where(low, pltpu.roll(part, C, 1), 0.0).astype(BF16)

    first_i = lax.div(s, 2)

    alone = jnp.logical_and(own_chunk == pos, first_i <= i)

    def to_owners(src, dst, rows, n):
        @pl.when(alone)
        def _():
            dst[s, rows] = src[half, rows]

        def one(k):
            to_i = k // 2
            to_j = first_block + 2 * (k % 2)
            mine = jnp.logical_and(to_i == i, to_j == j)

            @pl.when(jnp.logical_and(to_i >= first_i, jnp.logical_not(mine)))
            def _():
                push(src.at[k % 2, rows], dst.at[s, rows], fs.at[n], fr.at[n], to_i, to_j)
        each(0, 16, one)

    def owners_sent(dst, rows, n):
        for pair in range(COLS):
            for own in range(2):
                @pl.when(jnp.logical_and(first_i == pair, alone == (own == 1)))
                def _():
                    await_bytes(dst.at[0:2 * (COLS - pair) - own, rows], fs.at[n])

    def owner_sums(dst, rows, n):
        for pair in range(COLS):
            for own in range(2):
                @pl.when(jnp.logical_and(i == pair, alone == (own == 1)))
                def _():
                    await_bytes(dst.at[0:2 * pair + 2 - own, rows], fr.at[n])
        even = jnp.zeros((rows.stop - rows.start, 128), F32)
        odd = even
        for k in range(STEPS):
            later = delta_ref[k:k + 1] * dst[k, rows].astype(F32)
            even = even + jnp.where(k <= 2 * i, later, 0.0)
            odd = odd + jnp.where(k == 2 * i + 1, later, 0.0)
        return even, even + odd

    all_rows, early_rows, late_rows = slice(0, 32), slice(0, 16), slice(16, 32)
    blocks = range(3)
    velocities = {}

    def sum_heads(block):
        velocities[block] = reduce_heads(0, block)
        vsrc[block] = velocities[block].astype(BF16)
        gat[block, s] = velocities[block].astype(BF16)

        def send(k):
            to = lax.rem(s + k, STEPS)
            push(vsrc.at[block], gat.at[block, s], gs.at[block], gr.at[block], i, seq_of(to, p))
        for k in sorted(range(1, STEPS), key=lambda k: abs(k - STEPS // 2)):
            send(k)

    def next_latent(block):
        rows = slice(block * 16, (block + 1) * 16)
        latent = jnp.where(low, basein[0, rows], basein[1, rows])
        await_bytes(gat.at[block, 0:STEPS - 1], gr.at[block])
        for n in range(STEPS):
            latent = latent + jnp.where(n < s, delta_ref[n:n + 1] * gat[block, n].astype(F32), 0.0)
        latent = latent.astype(BF16)
        zsend[block] = latent
        latents[1, block, chunk, :] = latent
        group(lambda n, ti, tj: push(
            zsend.at[block], latents.at[1, block, chunk, :], ps.at[block], pr.at[block], ti, tj))

    def await_latents(block):
        await_bytes(latents.at[1, block, 0:15 * 16, :], pr.at[block])

    await_bytes(zp.at[:, 0:128, :], cr)
    for block in blocks:
        project(0, block)
    for block in blocks:
        finish(0, block, attend(block, blocks, (None, None)))
        if block:
            sum_heads(block - 1)
    send_base()
    sum_heads(2)
    for n in range(2):
        @pl.when(jnp.logical_not(from_mine[n]))
        def _():
            await_bytes(basein.at[n], br.at[n])
    next_latent(0)
    next_latent(1)
    pack_first(0, velocities[0], velocities[1])
    pack_last(0, velocities[2])

    await_latents(0)
    project(1, 0)
    next_latent(2)
    to_owners(vpack.at[0], fin0, all_rows, 0)
    await_latents(1)
    project(1, 1)
    early = [attend(block, (0, 1), (None, None)) for block in (0, 1)]
    await_latents(2)
    project(1, 2)
    for block in (0, 1):
        finish(1, block, attend(block, (2,), early[block]))
    finish(1, 2, attend(2, blocks, (None, None)))
    pack_first(1, reduce_heads(1, 0), reduce_heads(1, 1))
    to_owners(vpack.at[1], fin1, early_rows, 1)
    first_sums[0], first_sums[1] = owner_sums(fin0, all_rows, 0)
    pack_last(1, reduce_heads(1, 2))
    to_owners(vpack.at[1], fin1, late_rows, 2)

    even, odd = (
        jnp.concatenate(parts, axis=0) for parts in zip(owner_sums(fin1, early_rows, 1), owner_sums(fin1, late_rows, 2)))
    change_even = even - first_sums[0]
    change_odd = odd - first_sums[1]

    def unpack(x):
        return jnp.concatenate([x[0:16], pltpu.roll(x[0:16], C, 1), x[16:32]], axis=0)

    row = lax.broadcasted_iota(jnp.int32, (2, 128), 0)
    sum_even = jnp.sum(change_even * change_even, axis=0, keepdims=True)
    sum_odd = jnp.sum(change_odd * change_odd, axis=0, keepdims=True)
    partial = jnp.where(row == 0, sum_even, sum_odd)
    esrc[...] = partial
    ein[j] = partial
    column(lambda tj: push(esrc, ein.at[j], es, er, i, tj))
    for n, total in enumerate((basesrc[1] + unpack(even), basesrc[2] + unpack(odd))):
        out_ref[n] = total[:, 0:C]
    for lap in range(2):
        await_bytes(red.at[lap, :, 0:STEPS - 1], us.at[lap])
    for block in blocks:
        await_bytes(gat.at[block, 0:STEPS - 1], gs.at[block])
        await_bytes(latents.at[1, block, 0:15 * 16, :], ps.at[block])
    owners_sent(fin0, all_rows, 0)
    owners_sent(fin1, early_rows, 1)
    owners_sent(fin1, late_rows, 2)
    @pl.when(sends_start)
    def _():
        await_bytes(wall.at[0:31 * 32, 0:128], ys)

    await_bytes(nin.at[0:COLS - 1], ns)
    await_bytes(zp.at[:, 0:128, :], cs)
    for n in range(2):
        @pl.when(jnp.logical_not(base_mine[n]))
        def _():
            await_bytes(basesrc.at[n], bs.at[n])

    await_bytes(ein.at[0:SEQ - 1], er)
    total = ein[0]
    for n in range(1, SEQ):
        total = total + ein[n]
    total = total * (1.0 / (LEN * C))
    err_ref[0] = jnp.sum(total[0:1] / (coeff_even * coeff_even))
    err_ref[1] = jnp.sum(total[1:2] / (coeff_odd * coeff_odd))

    await_bytes(ein.at[0:SEQ - 1], es)


def per_device(
    start_latent, noise, window_start, w_embed, w_time, norm_gain, w_query, w_key, w_value, query_gain, key_gain, w_out, w_final,
):
    vmem = pl.BlockSpec(memory_space=pltpu.VMEM)
    hbm = pl.BlockSpec(memory_space=pltpu.HBM)
    smem = pl.BlockSpec(memory_space=pltpu.SMEM)
    dma = pltpu.SemaphoreType.DMA
    out, errors = pl.pallas_call(
        kernel,
        out_shape=(
            pltpu.VMEM((2, ROWS, C), F32),
            pltpu.SMEM((2,), F32),
        ),
        in_specs=[smem] + [hbm] * 12,
        out_specs=(vmem, smem),
        scratch_shapes=[
            pltpu.VMEM((ROWS, C), F32),
            pltpu.VMEM((2, ROWS, C), BF16),
            pltpu.VMEM((1, D), F32),
            pltpu.VMEM((1, HEAD), F32),
            pltpu.VMEM((1, HEAD), F32),
            pltpu.VMEM((256, D), BF16),
            pltpu.VMEM((D, 3 * HEAD), BF16),
            pltpu.VMEM((160, D), BF16),
            pltpu.VMEM((224, D), BF16),
            pltpu.VMEM((256, D), BF16),
            pltpu.VMEM((384, 256), BF16),
            pltpu.VMEM((256, 128), BF16),
            pltpu.VMEM((8, 128), F32),
            pltpu.VMEM((STEPS, 128), F32),
            pltpu.VMEM((STEPS, 128), F32),
            pltpu.VMEM((32, 128), BF16),
            pltpu.VMEM((16, 32, 128), BF16),
            pltpu.VMEM((ROWS, 128), BF16),
            pltpu.VMEM((COLS, ROWS, 128), BF16),
            pltpu.VMEM((3, ROWS, 128), F32),
            pltpu.VMEM((2, ROWS, 128), F32),
            pltpu.VMEM((2, 3, QBLK, 128), BF16),
            pltpu.VMEM((2, 3, QBLK, 128), BF16),
            pltpu.VMEM((2, 3, STEPS, 16, 128), BF16),
            pltpu.VMEM((3, 16, 128), BF16),
            pltpu.VMEM((2, 2, 32, 128), BF16),
            pltpu.VMEM((3, STEPS, 16, 128), BF16),
            pltpu.VMEM((3, 16, 128), BF16),
            pltpu.VMEM((STEPS, 32, 128), BF16),
            pltpu.VMEM((STEPS, 32, 128), BF16),
            pltpu.VMEM((2, 32, 128), F32),
            pltpu.VMEM((2, 128), F32),
            pltpu.VMEM((SEQ, 2, 128), F32),
            pltpu.VMEM((256, KBLK), BF16),
            pltpu.VMEM((LEN, HEAD), BF16),
            pltpu.VMEM((HEAD, LEN), BF16),
            pltpu.VMEM((C + 16, LEN), BF16),
            dma((14,)),
            dma, dma, dma, dma, dma, dma, dma((2,)), dma((2,)),
            dma((2,)), dma((2, 3)), dma((3,)), dma((3,)), dma((3,)), dma((3,)), dma((3,)), dma((3,)), dma, dma,
        ],
        compiler_params=pltpu.CompilerParams(
            collective_id=0, has_side_effects=True, vmem_limit_bytes=56 * 1024 * 1024),
    )(
        window_start, start_latent, noise, norm_gain.reshape(1, D), query_gain.reshape(1, HEAD), key_gain.reshape(1, HEAD),
        w_embed, w_time, w_final.T, w_query, w_key, w_value, w_out,
    )
    return out, errors


def solution(mesh):
    return jax.shard_map(
        per_device,
        mesh=mesh,
        in_specs=(
            P("seq", None), P("step", "seq", None), P(), P(), P(), P(),
            P(None, "step"), P(None, "step"), P(None, "step"), P(), P(), P("step", None), P(),
        ),
        out_specs=(P("step", "seq", None), P("step")),
        check_vma=False,
    )
```

```python
import math

import jax
import jax.numpy as jnp
from jax import lax
from jax.experimental import pallas as pl
from jax.experimental.pallas import tpu as pltpu
from jax.sharding import PartitionSpec as P

NSCHED = 28
EPS = 1e-06
SHIFT = 3.0
ETA = 0.5
MESH = pl.DeviceIdType.MESH
F32 = jnp.float32
BF16 = jnp.bfloat16

D = 3072
C = 64
HEAD = 128
LEN = 1536
HALF = LEN // 2
STEPS = 16
ROWS = 48
SEQ = 32
COLS = 8
QBLK = 256
KBLK = 512


def sigma_of(index):
    fraction = 1.0 - index / NSCHED
    return SHIFT * fraction / (1.0 + (SHIFT - 1.0) * fraction)


def chunk_i(n):
    return 2 * lax.rem(n, 4) + lax.div(n, 8)


def chunk_p(n):
    return lax.rem(lax.div(n, 4), 2)


def seq_of(step, part):
    return 2 * step + lax.rem(step + part, 2)


def chunk_block(n):
    return 4 * lax.rem(n, 8) + lax.div(n, 8)


def split(x):
    hi = x.astype(BF16)
    return hi, (x - hi.astype(F32)).astype(BF16)


def mm(a, b):
    return jnp.dot(a, b, preferred_element_type=F32)


def kernel(
    ws_ref, start_hbm, noise_hbm, gain_hbm, qg_hbm, kg_hbm,
    wembed_hbm, wtime_hbm, wfinal_hbm, wq_hbm, wk_hbm, wv_hbm, wo_hbm,
    out_ref, err_ref,
    start_ref, noise_ref, gain_ref, qg_ref, kg_ref,
    wtime, wall, fold, left, right, wqkv, cdiag, crow,
    delta_ref, coeff_ref,
    zsrc, yin, nsrc, nin, basesrc, basein,
    latents, heads, red, vsrc, vpack, gat, zsend, fin0, fin1, first_sums, esrc, ein,
    ztr, kbuf, qbuf, vbuf,
    wsem, ys, yr, cs, cr, ns, nr, bs, br, us, ur, gs, gr, ps, pr, fs, fr, es, er,
):
    i = lax.axis_index("step")
    j = lax.axis_index("seq")
    x = lax.div(i, 2)
    c = lax.rem(i, 2)
    z = lax.div(j, 4)
    y = lax.rem(j, 4)
    s = lax.div(j, 2)
    p = lax.rem(j + s, 2)
    pos = 4 * (2 * c + p) + x
    own_chunk = 8 * lax.rem(y, 2) + z
    half = lax.div(y, 2)
    source_i = chunk_i(own_chunk)
    source_p = chunk_p(own_chunk)
    first_block = chunk_block(pos)
    low_lanes = lax.broadcasted_iota(jnp.int32, (ROWS, 128), 1) < C

    def rows_of(n):
        return pl.ds(pl.multiple_of(n * 16, 16), 16)

    def push(src, dst, send, recv, to_i, to_j):
        pltpu.make_async_remote_copy(
            src_ref=src, dst_ref=dst, send_sem=send, recv_sem=recv,
            device_id=(to_i, to_j), device_id_type=MESH,
        ).start()

    def await_bytes(like, sem):
        pltpu.make_async_copy(like, like, sem).wait()

    def each(low, high, fn):
        for k in range(low, high):
            fn(k)

    def group(fn):
        def one(k):
            n = lax.rem(pos + k, STEPS)
            fn(n, chunk_i(n), seq_of(s, chunk_p(n)))
        for k in sorted(range(1, STEPS), key=lambda k: -min(k % 4, -k % 4)):
            one(k)

    zp = latents.at[0]

    def column(fn):
        for k in sorted(range(1, SEQ), key=lambda k: abs(k - SEQ // 2)):
            fn(lax.rem(j + k, SEQ))

    barrier = pltpu.get_barrier_semaphore()

    def greet(to_i, to_j):
        pl.semaphore_signal(barrier, inc=1, device_id=(to_i, to_j), device_id_type=MESH)

    group(lambda n, ti, tj: greet(ti, tj))
    column(lambda tj: greet(i, tj))
    base_j = [seq_of(2 * i + n, source_p) for n in range(2)]
    base_mine = [jnp.logical_and(source_i == i, tj == j) for tj in base_j]
    from_j = [first_block + 2 * n for n in range(2)]
    from_i = lax.div(s, 2)
    from_mine = [jnp.logical_and(from_i == i, tj == j) for tj in from_j]
    for n in range(2):
        @pl.when(jnp.logical_not(from_mine[n]))
        def _():
            greet(from_i, from_j[n])

    head = pl.multiple_of(p * HEAD, HEAD)
    pairs = [
        (start_hbm, start_ref), (noise_hbm, noise_ref), (wtime_hbm, wtime), (wembed_hbm, left.at[0:64, :]),
        (gain_hbm, gain_ref), (wembed_hbm, right.at[128:192, :]), (wfinal_hbm, right.at[0:64, :]),
        (wfinal_hbm, right.at[64:128, :]), (wo_hbm.at[pl.ds(head, HEAD), :], left.at[96:224, :]),
        (qg_hbm, qg_ref), (kg_hbm, kg_ref),
    ] + [
        (w.at[:, pl.ds(head, HEAD)], wall.at[:, n * HEAD:(n + 1) * HEAD]) for n, w in enumerate((wq_hbm, wk_hbm, wv_hbm))
    ]
    local = [pltpu.make_async_copy(src, dst, wsem.at[n]) for n, (src, dst) in enumerate(pairs)]
    for copy in local:
        copy.start()

    local[0].wait()
    z0 = start_ref[...]
    start_dup = jnp.concatenate([z0, z0], axis=1)
    low = low_lanes[0:16]
    own_half = lax.div(lax.broadcasted_iota(jnp.int32, (16, 128), 1), C) == half
    pieces = [start_dup[0:16], start_dup[16:32], start_dup[32:48]]
    packed_start = jnp.concatenate([
        jnp.where(own_half, pieces[0], pieces[1]), jnp.where(own_half, pieces[2], 0.0)], axis=0).astype(BF16)
    zsrc[...] = packed_start
    sends_start = lax.rem(y, 2) == c

    @pl.when(sends_start)
    def _():
        yin[8 * half + z] = packed_start

    local[1].wait()
    packed_noise = jnp.concatenate([noise_ref[0], noise_ref[1]], axis=1)
    nsrc[...] = packed_noise
    nin[i] = packed_noise

    alone_count = base_mine[0].astype(jnp.int32) + base_mine[1].astype(jnp.int32)
    pl.semaphore_wait(barrier, 15 + 31 + 2 - alone_count)

    @pl.when(sends_start)
    def _():
        column(lambda tj: push(zsrc, yin.at[8 * half + z], ys, yr, i, tj))


    first = ws_ref[0]
    index = (lax.broadcasted_iota(jnp.int32, (STEPS, 128), 0) + first).astype(F32)
    sigma_now = sigma_of(index)
    delta = sigma_of(index + 1.0) - sigma_now
    coeff = ETA * jnp.sqrt(-delta)
    delta_ref[...] = delta
    coeff_ref[...] = coeff
    own = sigma_of((jnp.zeros((STEPS, 128), jnp.int32) + (first + s)).astype(F32))
    lane = lax.broadcasted_iota(jnp.int32, (STEPS, 128), 1).astype(F32)
    angle = 1000.0 * own * jnp.exp(-math.log(10000.0) * lane / 128)
    feats = jnp.concatenate([jnp.cos(angle), jnp.sin(angle)], axis=1)
    feats = (feats / (1.0 + jnp.exp(-feats))).astype(BF16)
    right[192:256] = jnp.zeros((64, D), BF16)
    vbuf[C:C + 16] = jnp.ones((16, LEN), BF16)
    for n in range(2):
        ztr[128 * n + 64:128 * n + 128] = jnp.where(
            lax.broadcasted_iota(jnp.int32, (64, KBLK), 0) == 0, 1.0, 0.0).astype(BF16)

    for copy in local[3:5]:
        copy.wait()
    local[2].wait()
    temb = mm(feats, wtime[...])

    emb = left[0:64].astype(F32)
    gain = gain_ref[...]
    for n, part in enumerate(split(jnp.concatenate([emb * gain, temb * gain], axis=0))):
        fold[n * 80:(n + 1) * 80] = part
    for n, part in enumerate(split(temb)):
        left[64 + 16 * n:80 + 16 * n] = part
    t_row = temb[0:1]
    twice_et = 2.0 * jnp.sum(emb * t_row, axis=1, keepdims=True)
    t_square = jnp.sum(t_row * t_row, axis=1, keepdims=True)

    each(1, COLS, lambda k: push(nsrc, nin.at[i], ns, nr, lax.rem(i + k, COLS), j))

    for copy in local[5:]:
        copy.wait()
    folded = mm(fold[...], wall[...])
    folded = folded[0:80] + folded[80:160]
    @pl.when(sends_start)
    def _():
        await_bytes(yin.at[0:15], yr)

    @pl.when(jnp.logical_not(sends_start))
    def _():
        await_bytes(yin, yr)

    for n in range(8):
        below, above = yin[n].astype(F32), yin[8 + n].astype(F32)
        there = rows_of(8 * c + n)
        zp[0, there, :] = jnp.where(low, below[0:16], above[0:16]).astype(BF16)
        zp[1, there, :] = pltpu.roll(jnp.where(low, above[0:16], below[0:16]), C, 1).astype(BF16)
        zp[2, there, :] = jnp.where(low, below[16:32], above[16:32]).astype(BF16)
    core_rows = pl.ds(pl.multiple_of(128 * c, 128), 128)
    push(zp.at[:, core_rows, :], zp.at[:, core_rows, :], cs, cr, i + 1 - 2 * c, j)

    both = lax.dot_general(left[...], right[...], (((1,), (1,)), ((), ())), preferred_element_type=F32)
    cdup = both[0:64, 0:128]
    gram = both[0:64, 128:256]
    mout = both[96:224, 0:128]
    lanes64 = lax.broadcasted_iota(jnp.int32, (64, 128), 1)
    diag = jnp.concatenate([jnp.where(lanes64 < C, cdup, 0.0), jnp.where(lanes64 < C, 0.0, cdup)], axis=0)
    for n, part in enumerate(split(diag)):
        cdiag[n * 128:(n + 1) * 128] = part
    crow[...] = both[64:72, 0:128] + both[80:88, 0:128]

    value_fold = jnp.dot(folded[:, 256:384], mout, precision=lax.Precision.HIGHEST, preferred_element_type=F32)
    wide = jnp.concatenate([folded[:, 0:256], value_fold], axis=1)
    wide = jnp.concatenate([wide, jnp.zeros((48, 384), F32)], axis=0).T
    wide = jnp.concatenate([wide[0:320], jnp.where(lanes64 == C, twice_et, gram)], axis=0)
    whi = wide.astype(BF16)
    wqkv[:, 0:128] = whi
    wqkv[:, 128:256] = (wide - whi.astype(F32)).astype(BF16)
    scale_row = qg_ref[...] * kg_ref[...] * (math.log2(math.e) / math.sqrt(HEAD))
    scale_col = jnp.broadcast_to(scale_row, (128, 128)).T[:, 0:1]

    step_row = lax.broadcasted_iota(jnp.int32, (STEPS, 128), 0)
    coeff_even = jnp.sum(jnp.where(step_row == 2 * i, coeff, 0.0), axis=0, keepdims=True)
    coeff_odd = jnp.sum(jnp.where(step_row == 2 * i + 1, coeff, 0.0), axis=0, keepdims=True)

    def send_base():
        await_bytes(nin.at[0:COLS - 1], nr)

        def noise_of(step_pair):
            both = nin[step_pair].astype(F32)
            turned = pltpu.roll(both, C, 1)
            return jnp.where(low_lanes, both, turned), jnp.where(low_lanes, turned, both)

        base = start_dup
        for pair in range(COLS):
            even, odd = noise_of(pair)
            pair_sum = coeff_ref[2 * pair:2 * pair + 1] * even + coeff_ref[2 * pair + 1:2 * pair + 2] * odd
            base = base + jnp.where(pair < i, pair_sum, 0.0)
        own_even, own_odd = noise_of(i)
        after_even = base + coeff_even * own_even
        after_odd = after_even + coeff_odd * own_odd
        basesrc[0] = base
        basesrc[1] = after_even
        basesrc[2] = after_odd
        for n in range(2):
            @pl.when(base_mine[n])
            def _():
                basein[half] = basesrc[n]

            @pl.when(jnp.logical_not(base_mine[n]))
            def _():
                push(basesrc.at[n], basein.at[half], bs.at[n], br.at[half], source_i, base_j[n])

    chunk = rows_of(pos)
    low = low_lanes[0:16]

    def project(lap, n):
        packed = latents[lap, n].T
        zb = jnp.concatenate([packed[0:64], packed[64:128]], axis=1)
        ztr[0:64] = zb
        ztr[128:192] = zb
        cols = slice(n * KBLK, (n + 1) * KBLK)
        out = mm(wqkv[...], ztr[...])
        yq, yk, yv, yg = out[0:128], out[128:256], out[256:320], out[320:384]
        mean_square = (jnp.sum(zb.astype(F32) * yg, axis=0, keepdims=True) + t_square) * (1.0 / D)
        square = jnp.maximum(mean_square, 0.0) + EPS
        aq = lax.rsqrt(jnp.mean(yq * yq, axis=0, keepdims=True) + EPS * square)
        ak = lax.rsqrt(jnp.mean(yk * yk, axis=0, keepdims=True) + EPS * square)
        qbuf[:, cols] = (yq * aq * scale_col).astype(BF16)
        kbuf[cols, :] = (yk * ak).astype(BF16).T
        vbuf[0:C, cols] = (yv * lax.rsqrt(square)).astype(BF16)

    def attend(block, keys, accs):
        here = slice(keys[0] * KBLK, (keys[-1] + 1) * KBLK)
        scores = [
            mm(kbuf[here], qbuf[:, block * KBLK + side * QBLK:block * KBLK + (side + 1) * QBLK]) for side in range(2)]
        parts = [mm(vbuf[:, here], jnp.exp2(score).astype(BF16)) for score in scores]
        return [part if acc is None else acc + part for part, acc in zip(parts, accs)]

    def finish(lap, block, accs):
        outs = [acc[0:C] / acc[C:C + 1] for acc in accs]
        heads[lap, block] = jnp.concatenate(outs, axis=0).astype(BF16).T
        group(lambda n, ti, tj: push(
            heads.at[lap, block, rows_of(n), :], red.at[lap, block, pos], us.at[lap], ur.at[lap, block], ti, tj))

    def reduce_heads(lap, block):
        red[lap, block, pos] = heads[lap, block, chunk, :]
        latent = latents[lap, block, chunk, :]
        total = mm(jnp.concatenate([latent, latent], axis=1), cdiag[...]) + crow[0:1]
        await_bytes(red.at[lap, block, 0:STEPS - 1], ur.at[lap, block])
        for h in range(STEPS):
            total = total + red[lap, block, h].astype(F32)
        return total

    def pack_first(lap, first_part, second_part):
        vpack[lap, 0, 0:16] = jnp.where(low, first_part, pltpu.roll(second_part, C, 1)).astype(BF16)
        vpack[lap, 1, 0:16] = jnp.where(low, pltpu.roll(first_part, C, 1), second_part).astype(BF16)

    def pack_last(lap, part):
        vpack[lap, 0, 16:32] = jnp.where(low, part, 0.0).astype(BF16)
        vpack[lap, 1, 16:32] = jnp.where(low, pltpu.roll(part, C, 1), 0.0).astype(BF16)

    first_i = lax.div(s, 2)

    alone = jnp.logical_and(own_chunk == pos, first_i <= i)

    def to_owners(src, dst, rows, n):
        @pl.when(alone)
        def _():
            dst[s, rows] = src[half, rows]

        def one(k):
            to_i = k // 2
            to_j = first_block + 2 * (k % 2)
            mine = jnp.logical_and(to_i == i, to_j == j)

            @pl.when(jnp.logical_and(to_i >= first_i, jnp.logical_not(mine)))
            def _():
                push(src.at[k % 2, rows], dst.at[s, rows], fs.at[n], fr.at[n], to_i, to_j)
        each(0, 16, one)

    def owners_sent(dst, rows, n):
        for pair in range(COLS):
            for own in range(2):
                @pl.when(jnp.logical_and(first_i == pair, alone == (own == 1)))
                def _():
                    await_bytes(dst.at[0:2 * (COLS - pair) - own, rows], fs.at[n])

    def owner_sums(dst, rows, n):
        for pair in range(COLS):
            for own in range(2):
                @pl.when(jnp.logical_and(i == pair, alone == (own == 1)))
                def _():
                    await_bytes(dst.at[0:2 * pair + 2 - own, rows], fr.at[n])
        even = jnp.zeros((rows.stop - rows.start, 128), F32)
        odd = even
        for k in range(STEPS):
            later = delta_ref[k:k + 1] * dst[k, rows].astype(F32)
            even = even + jnp.where(k <= 2 * i, later, 0.0)
            odd = odd + jnp.where(k == 2 * i + 1, later, 0.0)
        return even, even + odd

    all_rows, early_rows, late_rows = slice(0, 32), slice(0, 16), slice(16, 32)
    blocks = range(3)
    velocities = {}

    def sum_heads(block):
        velocities[block] = reduce_heads(0, block)
        vsrc[block] = velocities[block].astype(BF16)
        gat[block, s] = velocities[block].astype(BF16)

        def send(k):
            to = lax.rem(s + k, STEPS)
            push(vsrc.at[block], gat.at[block, s], gs.at[block], gr.at[block], i, seq_of(to, p))
        for k in sorted(range(1, STEPS), key=lambda k: abs(k - STEPS // 2)):
            send(k)

    def next_latent(block):
        rows = slice(block * 16, (block + 1) * 16)
        latent = jnp.where(low, basein[0, rows], basein[1, rows])
        await_bytes(gat.at[block, 0:STEPS - 1], gr.at[block])
        for n in range(STEPS):
            latent = latent + jnp.where(n < s, delta_ref[n:n + 1] * gat[block, n].astype(F32), 0.0)
        latent = latent.astype(BF16)
        zsend[block] = latent
        latents[1, block, chunk, :] = latent
        group(lambda n, ti, tj: push(
            zsend.at[block], latents.at[1, block, chunk, :], ps.at[block], pr.at[block], ti, tj))

    def await_latents(block):
        await_bytes(latents.at[1, block, 0:15 * 16, :], pr.at[block])

    await_bytes(zp.at[:, 0:128, :], cr)
    for block in blocks:
        project(0, block)
    for block in blocks:
        finish(0, block, attend(block, blocks, (None, None)))
        if block:
            sum_heads(block - 1)
    send_base()
    sum_heads(2)
    for n in range(2):
        @pl.when(jnp.logical_not(from_mine[n]))
        def _():
            await_bytes(basein.at[n], br.at[n])
    next_latent(0)
    next_latent(1)
    pack_first(0, velocities[0], velocities[1])
    pack_last(0, velocities[2])

    await_latents(0)
    project(1, 0)
    next_latent(2)
    to_owners(vpack.at[0], fin0, all_rows, 0)
    await_latents(1)
    project(1, 1)
    early = [attend(block, (0, 1), (None, None)) for block in (0, 1)]
    await_latents(2)
    project(1, 2)
    for block in (0, 1):
        finish(1, block, attend(block, (2,), early[block]))
    finish(1, 2, attend(2, blocks, (None, None)))
    pack_first(1, reduce_heads(1, 0), reduce_heads(1, 1))
    to_owners(vpack.at[1], fin1, early_rows, 1)
    first_sums[0], first_sums[1] = owner_sums(fin0, all_rows, 0)
    pack_last(1, reduce_heads(1, 2))
    to_owners(vpack.at[1], fin1, late_rows, 2)

    even, odd = (
        jnp.concatenate(parts, axis=0) for parts in zip(owner_sums(fin1, early_rows, 1), owner_sums(fin1, late_rows, 2)))
    change_even = even - first_sums[0]
    change_odd = odd - first_sums[1]

    def unpack(x):
        return jnp.concatenate([x[0:16], pltpu.roll(x[0:16], C, 1), x[16:32]], axis=0)

    row = lax.broadcasted_iota(jnp.int32, (2, 128), 0)
    sum_even = jnp.sum(change_even * change_even, axis=0, keepdims=True)
    sum_odd = jnp.sum(change_odd * change_odd, axis=0, keepdims=True)
    partial = jnp.where(row == 0, sum_even, sum_odd)
    esrc[...] = partial
    ein[j] = partial
    column(lambda tj: push(esrc, ein.at[j], es, er, i, tj))
    for n, total in enumerate((basesrc[1] + unpack(even), basesrc[2] + unpack(odd))):
        out_ref[n] = total[:, 0:C]
    for lap in range(2):
        await_bytes(red.at[lap, :, 0:STEPS - 1], us.at[lap])
    for block in blocks:
        await_bytes(gat.at[block, 0:STEPS - 1], gs.at[block])
        await_bytes(latents.at[1, block, 0:15 * 16, :], ps.at[block])
    owners_sent(fin0, all_rows, 0)
    owners_sent(fin1, early_rows, 1)
    owners_sent(fin1, late_rows, 2)
    @pl.when(sends_start)
    def _():
        await_bytes(wall.at[0:31 * 32, 0:128], ys)

    await_bytes(nin.at[0:COLS - 1], ns)
    await_bytes(zp.at[:, 0:128, :], cs)
    for n in range(2):
        @pl.when(jnp.logical_not(base_mine[n]))
        def _():
            await_bytes(basesrc.at[n], bs.at[n])

    await_bytes(ein.at[0:SEQ - 1], er)
    total = ein[0]
    for n in range(1, SEQ):
        total = total + ein[n]
    total = total * (1.0 / (LEN * C))
    err_ref[0] = jnp.sum(total[0:1] / (coeff_even * coeff_even))
    err_ref[1] = jnp.sum(total[1:2] / (coeff_odd * coeff_odd))

    await_bytes(ein.at[0:SEQ - 1], es)


def per_device(
    start_latent, noise, window_start, w_embed, w_time, norm_gain, w_query, w_key, w_value, query_gain, key_gain, w_out, w_final,
):
    vmem = pl.BlockSpec(memory_space=pltpu.VMEM)
    hbm = pl.BlockSpec(memory_space=pltpu.HBM)
    smem = pl.BlockSpec(memory_space=pltpu.SMEM)
    dma = pltpu.SemaphoreType.DMA
    out, errors = pl.pallas_call(
        kernel,
        out_shape=(
            pltpu.VMEM((2, ROWS, C), F32),
            pltpu.SMEM((2,), F32),
        ),
        in_specs=[smem] + [hbm] * 12,
        out_specs=(vmem, smem),
        scratch_shapes=[
            pltpu.VMEM((ROWS, C), F32),
            pltpu.VMEM((2, ROWS, C), BF16),
            pltpu.VMEM((1, D), F32),
            pltpu.VMEM((1, HEAD), F32),
            pltpu.VMEM((1, HEAD), F32),
            pltpu.VMEM((256, D), BF16),
            pltpu.VMEM((D, 3 * HEAD), BF16),
            pltpu.VMEM((160, D), BF16),
            pltpu.VMEM((224, D), BF16),
            pltpu.VMEM((256, D), BF16),
            pltpu.VMEM((384, 256), BF16),
            pltpu.VMEM((256, 128), BF16),
            pltpu.VMEM((8, 128), F32),
            pltpu.VMEM((STEPS, 128), F32),
            pltpu.VMEM((STEPS, 128), F32),
            pltpu.VMEM((32, 128), BF16),
            pltpu.VMEM((16, 32, 128), BF16),
            pltpu.VMEM((ROWS, 128), BF16),
            pltpu.VMEM((COLS, ROWS, 128), BF16),
            pltpu.VMEM((3, ROWS, 128), F32),
            pltpu.VMEM((2, ROWS, 128), F32),
            pltpu.VMEM((2, 3, QBLK, 128), BF16),
            pltpu.VMEM((2, 3, QBLK, 128), BF16),
            pltpu.VMEM((2, 3, STEPS, 16, 128), BF16),
            pltpu.VMEM((3, 16, 128), BF16),
            pltpu.VMEM((2, 2, 32, 128), BF16),
            pltpu.VMEM((3, STEPS, 16, 128), BF16),
            pltpu.VMEM((3, 16, 128), BF16),
            pltpu.VMEM((STEPS, 32, 128), BF16),
            pltpu.VMEM((STEPS, 32, 128), BF16),
            pltpu.VMEM((2, 32, 128), F32),
            pltpu.VMEM((2, 128), F32),
            pltpu.VMEM((SEQ, 2, 128), F32),
            pltpu.VMEM((256, KBLK), BF16),
            pltpu.VMEM((LEN, HEAD), BF16),
            pltpu.VMEM((HEAD, LEN), BF16),
            pltpu.VMEM((C + 16, LEN), BF16),
            dma((14,)),
            dma, dma, dma, dma, dma, dma, dma((2,)), dma((2,)),
            dma((2,)), dma((2, 3)), dma((3,)), dma((3,)), dma((3,)), dma((3,)), dma((3,)), dma((3,)), dma, dma,
        ],
        compiler_params=pltpu.CompilerParams(
            collective_id=0, has_side_effects=True, vmem_limit_bytes=56 * 1024 * 1024),
    )(
        window_start, start_latent, noise, norm_gain.reshape(1, D), query_gain.reshape(1, HEAD), key_gain.reshape(1, HEAD),
        w_embed, w_time, w_final.T, w_query, w_key, w_value, w_out,
    )
    return out, errors


def solution(mesh):
    return jax.shard_map(
        per_device,
        mesh=mesh,
        in_specs=(
            P("seq", None), P("step", "seq", None), P(), P(), P(), P(),
            P(None, "step"), P(None, "step"), P(None, "step"), P(), P(), P("step", None), P(),
        ),
        out_specs=(P("step", "seq", None), P("step")),
        check_vma=False,
    )
```

```python
import math

import jax
import jax.numpy as jnp
from jax import lax
from jax.experimental import pallas as pl
from jax.experimental.pallas import tpu as pltpu
from jax.sharding import PartitionSpec as P

NSCHED = 28
EPS = 1e-06
SHIFT = 3.0
ETA = 0.5
MESH = pl.DeviceIdType.MESH
F32 = jnp.float32
BF16 = jnp.bfloat16

D = 3072
C = 64
HEAD = 128
LEN = 1536
HALF = LEN // 2
STEPS = 16
ROWS = 48
SEQ = 32
COLS = 8
QBLK = 256
KBLK = 512
PARTS = 4
DBLK = D // PARTS


def sigma_of(index):
    fraction = 1.0 - index / NSCHED
    return SHIFT * fraction / (1.0 + (SHIFT - 1.0) * fraction)


def chunk_i(n):
    return 2 * lax.rem(n, 4) + lax.div(n, 8)


def chunk_p(n):
    return lax.rem(lax.div(n, 4), 2)


def seq_of(step, part):
    return 2 * step + lax.rem(step + part, 2)


def chunk_block(n):
    return 4 * lax.rem(n, 8) + lax.div(n, 8)


def split(x):
    hi = x.astype(BF16)
    return hi, (x - hi.astype(F32)).astype(BF16)


def mm(a, b):
    return jnp.dot(a, b, preferred_element_type=F32)


def kernel(
    ws_ref, start_hbm, noise_hbm, gain_hbm, qg_hbm, kg_hbm,
    wembed_hbm, wtime_hbm, wfinal_hbm, wq_hbm, wk_hbm, wv_hbm, wo_hbm,
    out_ref, err_ref,
    start_ref, noise_ref, gain_ref, qg_ref, kg_ref,
    wtime, wall, fold, left, right, wqkv, cdiag, crow,
    delta_ref, coeff_ref,
    zsrc, yin, nsrc, nin, basesrc, basein,
    latents, heads, red, vsrc, vpack, gat, zsend, fin0, fin1, first_sums, esrc, ein,
    ztr, kbuf, qbuf, vbuf,
    wsem, ys, yr, cs, cr, ns, nr, bs, br, us, ur, gs, gr, ps, pr, fs, fr, es, er,
):
    i = lax.axis_index("step")
    j = lax.axis_index("seq")
    x = lax.div(i, 2)
    c = lax.rem(i, 2)
    z = lax.div(j, 4)
    y = lax.rem(j, 4)
    s = lax.div(j, 2)
    p = lax.rem(j + s, 2)
    pos = 4 * (2 * c + p) + x
    own_chunk = 8 * lax.rem(y, 2) + z
    half = lax.div(y, 2)
    source_i = chunk_i(own_chunk)
    source_p = chunk_p(own_chunk)
    first_block = chunk_block(pos)
    low_lanes = lax.broadcasted_iota(jnp.int32, (ROWS, 128), 1) < C

    def rows_of(n):
        return pl.ds(pl.multiple_of(n * 16, 16), 16)

    def push(src, dst, send, recv, to_i, to_j):
        pltpu.make_async_remote_copy(
            src_ref=src, dst_ref=dst, send_sem=send, recv_sem=recv,
            device_id=(to_i, to_j), device_id_type=MESH,
        ).start()

    def await_bytes(like, sem):
        pltpu.make_async_copy(like, like, sem).wait()

    def each(low, high, fn):
        for k in range(low, high):
            fn(k)

    def group(fn):
        def one(k):
            n = lax.rem(pos + k, STEPS)
            fn(n, chunk_i(n), seq_of(s, chunk_p(n)))
        for k in sorted(range(1, STEPS), key=lambda k: -min(k % 4, -k % 4)):
            one(k)

    zp = latents.at[0]

    def column(fn):
        for k in sorted(range(1, SEQ), key=lambda k: abs(k - SEQ // 2)):
            fn(lax.rem(j + k, SEQ))

    barrier = pltpu.get_barrier_semaphore()

    def greet(to_i, to_j):
        pl.semaphore_signal(barrier, inc=1, device_id=(to_i, to_j), device_id_type=MESH)

    group(lambda n, ti, tj: greet(ti, tj))
    column(lambda tj: greet(i, tj))
    base_j = [seq_of(2 * i + n, source_p) for n in range(2)]
    base_mine = [jnp.logical_and(source_i == i, tj == j) for tj in base_j]
    from_j = [first_block + 2 * n for n in range(2)]
    from_i = lax.div(s, 2)
    from_mine = [jnp.logical_and(from_i == i, tj == j) for tj in from_j]
    for n in range(2):
        @pl.when(jnp.logical_not(from_mine[n]))
        def _():
            greet(from_i, from_j[n])

    head = pl.multiple_of(p * HEAD, HEAD)
    widths = [slice(n * DBLK, (n + 1) * DBLK) for n in range(PARTS)]
    pairs = [(start_hbm, start_ref), (noise_hbm, noise_ref), (gain_hbm, gain_ref), (qg_hbm, qg_ref), (kg_hbm, kg_ref)]
    for part in widths:
        pairs += [(wtime_hbm.at[:, part], wtime.at[:, part]), (wembed_hbm.at[:, part], left.at[0:64, part])]
        pairs += [
            (w.at[part, pl.ds(head, HEAD)], wall.at[part, n * HEAD:(n + 1) * HEAD]) for n, w in enumerate((wq_hbm, wk_hbm, wv_hbm))
        ]
        pairs += [
            (wfinal_hbm.at[:, part], right.at[0:64, part]),
            (wo_hbm.at[pl.ds(head, HEAD), part], left.at[96:224, part]),
        ]
    local = [pltpu.make_async_copy(src, dst, wsem.at[n]) for n, (src, dst) in enumerate(pairs)]
    for copy in local:
        copy.start()

    local[0].wait()
    z0 = start_ref[...]
    start_dup = jnp.concatenate([z0, z0], axis=1)
    low = low_lanes[0:16]
    own_half = lax.div(lax.broadcasted_iota(jnp.int32, (16, 128), 1), C) == half
    pieces = [start_dup[0:16], start_dup[16:32], start_dup[32:48]]
    packed_start = jnp.concatenate([
        jnp.where(own_half, pieces[0], pieces[1]), jnp.where(own_half, pieces[2], 0.0)], axis=0).astype(BF16)
    zsrc[...] = packed_start
    sends_start = lax.rem(y, 2) == c

    @pl.when(sends_start)
    def _():
        yin[8 * half + z] = packed_start

    local[1].wait()
    packed_noise = jnp.concatenate([noise_ref[0], noise_ref[1]], axis=1)
    nsrc[...] = packed_noise
    nin[i] = packed_noise

    alone_count = base_mine[0].astype(jnp.int32) + base_mine[1].astype(jnp.int32)
    pl.semaphore_wait(barrier, 15 + 31 + 2 - alone_count)

    @pl.when(sends_start)
    def _():
        column(lambda tj: push(zsrc, yin.at[8 * half + z], ys, yr, i, tj))


    first = ws_ref[0]
    index = (lax.broadcasted_iota(jnp.int32, (STEPS, 128), 0) + first).astype(F32)
    sigma_now = sigma_of(index)
    delta = sigma_of(index + 1.0) - sigma_now
    coeff = ETA * jnp.sqrt(-delta)
    delta_ref[...] = delta
    coeff_ref[...] = coeff
    own = sigma_of((jnp.zeros((STEPS, 128), jnp.int32) + (first + s)).astype(F32))
    lane = lax.broadcasted_iota(jnp.int32, (STEPS, 128), 1).astype(F32)
    angle = 1000.0 * own * jnp.exp(-math.log(10000.0) * lane / 128)
    feats = jnp.concatenate([jnp.cos(angle), jnp.sin(angle)], axis=1)
    feats = (feats / (1.0 + jnp.exp(-feats))).astype(BF16)
    right[192:256] = jnp.zeros((64, D), BF16)
    vbuf[C:C + 16] = jnp.ones((16, LEN), BF16)
    for n in range(2):
        ztr[128 * n + 64:128 * n + 128] = jnp.where(
            lax.broadcasted_iota(jnp.int32, (64, KBLK), 0) == 0, 1.0, 0.0).astype(BF16)

    each(1, COLS, lambda k: push(nsrc, nin.at[i], ns, nr, lax.rem(i + k, COLS), j))

    for copy in local[2:5]:
        copy.wait()
    sums = [0.0] * 4

    def fold_part(n):
        part = widths[n]
        for copy in local[5 + 7 * n:7 + 7 * n]:
            copy.wait()
        temb = mm(feats, wtime[:, part])
        embed = left[0:64, part]
        emb = embed.astype(F32)
        gain = gain_ref[:, part]
        for m, piece in enumerate(split(jnp.concatenate([emb * gain, temb * gain], axis=0))):
            fold[m * 80:(m + 1) * 80, part] = piece
        for m, piece in enumerate(split(temb)):
            left[64 + 16 * m:80 + 16 * m, part] = piece
        t_row = temb[0:1]
        right[128:192, part] = embed
        for copy in local[7 + 7 * n:12 + 7 * n]:
            copy.wait()
        right[64:128, part] = right[0:64, part]
        terms = (
            jnp.sum(emb * t_row, axis=1, keepdims=True),
            jnp.sum(t_row * t_row, axis=1, keepdims=True),
            mm(fold[:, part], wall[part]),
            lax.dot_general(left[:, part], right[:, part], (((1,), (1,)), ((), ())), preferred_element_type=F32),
        )
        for m, term in enumerate(terms):
            sums[m] = sums[m] + term

    each(0, PARTS - 1, fold_part)

    @pl.when(sends_start)
    def _():
        await_bytes(yin.at[0:15], yr)

    @pl.when(jnp.logical_not(sends_start))
    def _():
        await_bytes(yin, yr)

    for n in range(8):
        below, above = yin[n].astype(F32), yin[8 + n].astype(F32)
        there = rows_of(8 * c + n)
        zp[0, there, :] = jnp.where(low, below[0:16], above[0:16]).astype(BF16)
        zp[1, there, :] = pltpu.roll(jnp.where(low, above[0:16], below[0:16]), C, 1).astype(BF16)
        zp[2, there, :] = jnp.where(low, below[16:32], above[16:32]).astype(BF16)
    core_rows = pl.ds(pl.multiple_of(128 * c, 128), 128)
    push(zp.at[:, core_rows, :], zp.at[:, core_rows, :], cs, cr, i + 1 - 2 * c, j)

    fold_part(PARTS - 1)
    twice_et, t_square, folded, both = sums
    twice_et = 2.0 * twice_et
    folded = folded[0:80] + folded[80:160]
    cdup = both[0:64, 0:128]
    gram = both[0:64, 128:256]
    mout = both[96:224, 0:128]
    lanes64 = lax.broadcasted_iota(jnp.int32, (64, 128), 1)
    diag = jnp.concatenate([jnp.where(lanes64 < C, cdup, 0.0), jnp.where(lanes64 < C, 0.0, cdup)], axis=0)
    for n, part in enumerate(split(diag)):
        cdiag[n * 128:(n + 1) * 128] = part
    crow[...] = both[64:72, 0:128] + both[80:88, 0:128]

    value_fold = jnp.dot(folded[:, 256:384], mout, precision=lax.Precision.HIGHEST, preferred_element_type=F32)
    wide = jnp.concatenate([folded[:, 0:256], value_fold], axis=1)
    wide = jnp.concatenate([wide, jnp.zeros((48, 384), F32)], axis=0).T
    wide = jnp.concatenate([wide[0:320], jnp.where(lanes64 == C, twice_et, gram)], axis=0)
    whi = wide.astype(BF16)
    wqkv[:, 0:128] = whi
    wqkv[:, 128:256] = (wide - whi.astype(F32)).astype(BF16)
    scale_row = qg_ref[...] * kg_ref[...] * (math.log2(math.e) / math.sqrt(HEAD))
    scale_col = jnp.broadcast_to(scale_row, (128, 128)).T[:, 0:1]

    step_row = lax.broadcasted_iota(jnp.int32, (STEPS, 128), 0)
    coeff_even = jnp.sum(jnp.where(step_row == 2 * i, coeff, 0.0), axis=0, keepdims=True)
    coeff_odd = jnp.sum(jnp.where(step_row == 2 * i + 1, coeff, 0.0), axis=0, keepdims=True)

    def send_base():
        await_bytes(nin.at[0:COLS - 1], nr)

        def noise_of(step_pair):
            both = nin[step_pair].astype(F32)
            turned = pltpu.roll(both, C, 1)
            return jnp.where(low_lanes, both, turned), jnp.where(low_lanes, turned, both)

        base = start_dup
        for pair in range(COLS):
            even, odd = noise_of(pair)
            pair_sum = coeff_ref[2 * pair:2 * pair + 1] * even + coeff_ref[2 * pair + 1:2 * pair + 2] * odd
            base = base + jnp.where(pair < i, pair_sum, 0.0)
        own_even, own_odd = noise_of(i)
        after_even = base + coeff_even * own_even
        after_odd = after_even + coeff_odd * own_odd
        basesrc[0] = base
        basesrc[1] = after_even
        basesrc[2] = after_odd
        for n in range(2):
            @pl.when(base_mine[n])
            def _():
                basein[half] = basesrc[n]

            @pl.when(jnp.logical_not(base_mine[n]))
            def _():
                push(basesrc.at[n], basein.at[half], bs.at[n], br.at[half], source_i, base_j[n])

    chunk = rows_of(pos)
    low = low_lanes[0:16]

    def project(lap, n):
        packed = latents[lap, n].T
        zb = jnp.concatenate([packed[0:64], packed[64:128]], axis=1)
        ztr[0:64] = zb
        ztr[128:192] = zb
        cols = slice(n * KBLK, (n + 1) * KBLK)
        out = mm(wqkv[...], ztr[...])
        yq, yk, yv, yg = out[0:128], out[128:256], out[256:320], out[320:384]
        mean_square = (jnp.sum(zb.astype(F32) * yg, axis=0, keepdims=True) + t_square) * (1.0 / D)
        square = jnp.maximum(mean_square, 0.0) + EPS
        aq = lax.rsqrt(jnp.mean(yq * yq, axis=0, keepdims=True) + EPS * square)
        ak = lax.rsqrt(jnp.mean(yk * yk, axis=0, keepdims=True) + EPS * square)
        qbuf[:, cols] = (yq * aq * scale_col).astype(BF16)
        kbuf[cols, :] = (yk * ak).astype(BF16).T
        vbuf[0:C, cols] = (yv * lax.rsqrt(square)).astype(BF16)

    def attend(block, keys, accs):
        here = slice(keys[0] * KBLK, (keys[-1] + 1) * KBLK)
        scores = [
            mm(kbuf[here], qbuf[:, block * KBLK + side * QBLK:block * KBLK + (side + 1) * QBLK]) for side in range(2)]
        parts = [mm(vbuf[:, here], jnp.exp2(score).astype(BF16)) for score in scores]
        return [part if acc is None else acc + part for part, acc in zip(parts, accs)]

    def finish(lap, block, accs):
        outs = [acc[0:C] / acc[C:C + 1] for acc in accs]
        heads[lap, block] = jnp.concatenate(outs, axis=0).astype(BF16).T
        group(lambda n, ti, tj: push(
            heads.at[lap, block, rows_of(n), :], red.at[lap, block, pos], us.at[lap], ur.at[lap, block], ti, tj))

    def reduce_heads(lap, block):
        red[lap, block, pos] = heads[lap, block, chunk, :]
        latent = latents[lap, block, chunk, :]
        total = mm(jnp.concatenate([latent, latent], axis=1), cdiag[...]) + crow[0:1]
        await_bytes(red.at[lap, block, 0:STEPS - 1], ur.at[lap, block])
        for h in range(STEPS):
            total = total + red[lap, block, h].astype(F32)
        return total

    def pack_first(lap, first_part, second_part):
        vpack[lap, 0, 0:16] = jnp.where(low, first_part, pltpu.roll(second_part, C, 1)).astype(BF16)
        vpack[lap, 1, 0:16] = jnp.where(low, pltpu.roll(first_part, C, 1), second_part).astype(BF16)

    def pack_last(lap, part):
        vpack[lap, 0, 16:32] = jnp.where(low, part, 0.0).astype(BF16)
        vpack[lap, 1, 16:32] = jnp.where(low, pltpu.roll(part, C, 1), 0.0).astype(BF16)

    first_i = lax.div(s, 2)

    alone = jnp.logical_and(own_chunk == pos, first_i <= i)

    def to_owners(src, dst, rows, n):
        @pl.when(alone)
        def _():
            dst[s, rows] = src[half, rows]

        def one(k):
            to_i = k // 2
            to_j = first_block + 2 * (k % 2)
            mine = jnp.logical_and(to_i == i, to_j == j)

            @pl.when(jnp.logical_and(to_i >= first_i, jnp.logical_not(mine)))
            def _():
                push(src.at[k % 2, rows], dst.at[s, rows], fs.at[n], fr.at[n], to_i, to_j)
        each(0, 16, one)

    def owners_sent(dst, rows, n):
        for pair in range(COLS):
            for own in range(2):
                @pl.when(jnp.logical_and(first_i == pair, alone == (own == 1)))
                def _():
                    await_bytes(dst.at[0:2 * (COLS - pair) - own, rows], fs.at[n])

    def owner_sums(dst, rows, n):
        for pair in range(COLS):
            for own in range(2):
                @pl.when(jnp.logical_and(i == pair, alone == (own == 1)))
                def _():
                    await_bytes(dst.at[0:2 * pair + 2 - own, rows], fr.at[n])
        even = jnp.zeros((rows.stop - rows.start, 128), F32)
        odd = even
        for k in range(STEPS):
            later = delta_ref[k:k + 1] * dst[k, rows].astype(F32)
            even = even + jnp.where(k <= 2 * i, later, 0.0)
            odd = odd + jnp.where(k == 2 * i + 1, later, 0.0)
        return even, even + odd

    all_rows, early_rows, late_rows = slice(0, 32), slice(0, 16), slice(16, 32)
    blocks = range(3)
    velocities = {}

    def sum_heads(block):
        velocities[block] = reduce_heads(0, block)
        vsrc[block] = velocities[block].astype(BF16)
        gat[block, s] = velocities[block].astype(BF16)

        def send(k):
            to = lax.rem(s + k, STEPS)
            push(vsrc.at[block], gat.at[block, s], gs.at[block], gr.at[block], i, seq_of(to, p))
        for k in sorted(range(1, STEPS), key=lambda k: abs(k - STEPS // 2)):
            send(k)

    def next_latent(block):
        rows = slice(block * 16, (block + 1) * 16)
        latent = jnp.where(low, basein[0, rows], basein[1, rows])
        await_bytes(gat.at[block, 0:STEPS - 1], gr.at[block])
        for n in range(STEPS):
            latent = latent + jnp.where(n < s, delta_ref[n:n + 1] * gat[block, n].astype(F32), 0.0)
        latent = latent.astype(BF16)
        zsend[block] = latent
        latents[1, block, chunk, :] = latent
        group(lambda n, ti, tj: push(
            zsend.at[block], latents.at[1, block, chunk, :], ps.at[block], pr.at[block], ti, tj))

    def await_latents(block):
        await_bytes(latents.at[1, block, 0:15 * 16, :], pr.at[block])

    await_bytes(zp.at[:, 0:128, :], cr)
    for block in blocks:
        project(0, block)
    for block in blocks:
        finish(0, block, attend(block, blocks, (None, None)))
        if block:
            sum_heads(block - 1)
    send_base()
    sum_heads(2)
    for n in range(2):
        @pl.when(jnp.logical_not(from_mine[n]))
        def _():
            await_bytes(basein.at[n], br.at[n])
    next_latent(0)
    next_latent(1)
    pack_first(0, velocities[0], velocities[1])
    pack_last(0, velocities[2])

    await_latents(0)
    project(1, 0)
    next_latent(2)
    to_owners(vpack.at[0], fin0, all_rows, 0)
    await_latents(1)
    project(1, 1)
    early = [attend(block, (0, 1), (None, None)) for block in (0, 1)]
    await_latents(2)
    project(1, 2)
    for block in (0, 1):
        finish(1, block, attend(block, (2,), early[block]))
    finish(1, 2, attend(2, blocks, (None, None)))
    pack_first(1, reduce_heads(1, 0), reduce_heads(1, 1))
    to_owners(vpack.at[1], fin1, early_rows, 1)
    first_sums[0], first_sums[1] = owner_sums(fin0, all_rows, 0)
    pack_last(1, reduce_heads(1, 2))
    to_owners(vpack.at[1], fin1, late_rows, 2)

    even, odd = (
        jnp.concatenate(parts, axis=0) for parts in zip(owner_sums(fin1, early_rows, 1), owner_sums(fin1, late_rows, 2)))
    change_even = even - first_sums[0]
    change_odd = odd - first_sums[1]

    def unpack(x):
        return jnp.concatenate([x[0:16], pltpu.roll(x[0:16], C, 1), x[16:32]], axis=0)

    row = lax.broadcasted_iota(jnp.int32, (2, 128), 0)
    sum_even = jnp.sum(change_even * change_even, axis=0, keepdims=True)
    sum_odd = jnp.sum(change_odd * change_odd, axis=0, keepdims=True)
    partial = jnp.where(row == 0, sum_even, sum_odd)
    esrc[...] = partial
    ein[j] = partial
    column(lambda tj: push(esrc, ein.at[j], es, er, i, tj))
    for n, total in enumerate((basesrc[1] + unpack(even), basesrc[2] + unpack(odd))):
        out_ref[n] = total[:, 0:C]
    for lap in range(2):
        await_bytes(red.at[lap, :, 0:STEPS - 1], us.at[lap])
    for block in blocks:
        await_bytes(gat.at[block, 0:STEPS - 1], gs.at[block])
        await_bytes(latents.at[1, block, 0:15 * 16, :], ps.at[block])
    owners_sent(fin0, all_rows, 0)
    owners_sent(fin1, early_rows, 1)
    owners_sent(fin1, late_rows, 2)
    @pl.when(sends_start)
    def _():
        await_bytes(wall.at[0:31 * 32, 0:128], ys)

    await_bytes(nin.at[0:COLS - 1], ns)
    await_bytes(zp.at[:, 0:128, :], cs)
    for n in range(2):
        @pl.when(jnp.logical_not(base_mine[n]))
        def _():
            await_bytes(basesrc.at[n], bs.at[n])

    await_bytes(ein.at[0:SEQ - 1], er)
    total = ein[0]
    for n in range(1, SEQ):
        total = total + ein[n]
    total = total * (1.0 / (LEN * C))
    err_ref[0] = jnp.sum(total[0:1] / (coeff_even * coeff_even))
    err_ref[1] = jnp.sum(total[1:2] / (coeff_odd * coeff_odd))

    await_bytes(ein.at[0:SEQ - 1], es)


def per_device(
    start_latent, noise, window_start, w_embed, w_time, norm_gain, w_query, w_key, w_value, query_gain, key_gain, w_out, w_final,
):
    vmem = pl.BlockSpec(memory_space=pltpu.VMEM)
    hbm = pl.BlockSpec(memory_space=pltpu.HBM)
    smem = pl.BlockSpec(memory_space=pltpu.SMEM)
    dma = pltpu.SemaphoreType.DMA
    out, errors = pl.pallas_call(
        kernel,
        out_shape=(
            pltpu.VMEM((2, ROWS, C), F32),
            pltpu.SMEM((2,), F32),
        ),
        in_specs=[smem] + [hbm] * 12,
        out_specs=(vmem, smem),
        scratch_shapes=[
            pltpu.VMEM((ROWS, C), F32),
            pltpu.VMEM((2, ROWS, C), BF16),
            pltpu.VMEM((1, D), F32),
            pltpu.VMEM((1, HEAD), F32),
            pltpu.VMEM((1, HEAD), F32),
            pltpu.VMEM((256, D), BF16),
            pltpu.VMEM((D, 3 * HEAD), BF16),
            pltpu.VMEM((160, D), BF16),
            pltpu.VMEM((224, D), BF16),
            pltpu.VMEM((256, D), BF16),
            pltpu.VMEM((384, 256), BF16),
            pltpu.VMEM((256, 128), BF16),
            pltpu.VMEM((8, 128), F32),
            pltpu.VMEM((STEPS, 128), F32),
            pltpu.VMEM((STEPS, 128), F32),
            pltpu.VMEM((32, 128), BF16),
            pltpu.VMEM((16, 32, 128), BF16),
            pltpu.VMEM((ROWS, 128), BF16),
            pltpu.VMEM((COLS, ROWS, 128), BF16),
            pltpu.VMEM((3, ROWS, 128), F32),
            pltpu.VMEM((2, ROWS, 128), F32),
            pltpu.VMEM((2, 3, QBLK, 128), BF16),
            pltpu.VMEM((2, 3, QBLK, 128), BF16),
            pltpu.VMEM((2, 3, STEPS, 16, 128), BF16),
            pltpu.VMEM((3, 16, 128), BF16),
            pltpu.VMEM((2, 2, 32, 128), BF16),
            pltpu.VMEM((3, STEPS, 16, 128), BF16),
            pltpu.VMEM((3, 16, 128), BF16),
            pltpu.VMEM((STEPS, 32, 128), BF16),
            pltpu.VMEM((STEPS, 32, 128), BF16),
            pltpu.VMEM((2, 32, 128), F32),
            pltpu.VMEM((2, 128), F32),
            pltpu.VMEM((SEQ, 2, 128), F32),
            pltpu.VMEM((256, KBLK), BF16),
            pltpu.VMEM((LEN, HEAD), BF16),
            pltpu.VMEM((HEAD, LEN), BF16),
            pltpu.VMEM((C + 16, LEN), BF16),
            dma((5 + 7 * PARTS,)),
            dma, dma, dma, dma, dma, dma, dma((2,)), dma((2,)),
            dma((2,)), dma((2, 3)), dma((3,)), dma((3,)), dma((3,)), dma((3,)), dma((3,)), dma((3,)), dma, dma,
        ],
        compiler_params=pltpu.CompilerParams(
            collective_id=0, has_side_effects=True, vmem_limit_bytes=56 * 1024 * 1024),
    )(
        window_start, start_latent, noise, norm_gain.reshape(1, D), query_gain.reshape(1, HEAD), key_gain.reshape(1, HEAD),
        w_embed, w_time, w_final.T, w_query, w_key, w_value, w_out,
    )
    return out, errors


def solution(mesh):
    return jax.shard_map(
        per_device,
        mesh=mesh,
        in_specs=(
            P("seq", None), P("step", "seq", None), P(), P(), P(), P(),
            P(None, "step"), P(None, "step"), P(None, "step"), P(), P(), P("step", None), P(),
        ),
        out_specs=(P("step", "seq", None), P("step")),
        check_vma=False,
    )
```

```python
import math

import jax
import jax.numpy as jnp
from jax import lax
from jax.experimental import pallas as pl
from jax.experimental.pallas import tpu as pltpu
from jax.sharding import PartitionSpec as P

NSCHED = 28
EPS = 1e-06
SHIFT = 3.0
ETA = 0.5
MESH = pl.DeviceIdType.MESH
F32 = jnp.float32
BF16 = jnp.bfloat16

D = 3072
C = 64
HEAD = 128
LEN = 1536
HALF = LEN // 2
STEPS = 16
ROWS = 48
SEQ = 32
COLS = 8
QBLK = 256
KBLK = 512
PARTS = 4
DBLK = D // PARTS


def sigma_of(index):
    fraction = 1.0 - index / NSCHED
    return SHIFT * fraction / (1.0 + (SHIFT - 1.0) * fraction)


def chunk_i(n):
    return 2 * lax.rem(n, 4) + lax.div(n, 8)


def chunk_p(n):
    return lax.rem(lax.div(n, 4), 2)


def seq_of(step, part):
    return 2 * step + lax.rem(step + part, 2)


def chunk_block(n):
    return 4 * lax.rem(n, 8) + lax.div(n, 8)


def split(x):
    hi = x.astype(BF16)
    return hi, (x - hi.astype(F32)).astype(BF16)


def mm(a, b):
    return jnp.dot(a, b, preferred_element_type=F32)


def kernel(
    ws_ref, start_hbm, noise_hbm, gain_hbm, qg_hbm, kg_hbm,
    wembed_hbm, wtime_hbm, wfinal_hbm, wq_hbm, wk_hbm, wv_hbm, wo_hbm,
    out_ref, err_ref,
    start_ref, noise_ref, gain_ref, qg_ref, kg_ref,
    wtime, wall, fold, left, right, wqkv, cdiag, crow,
    delta_ref, coeff_ref,
    zsrc, yin, nsrc, nin, basesrc, basein,
    latents, heads, red, vsrc, vpack, gat, zsend, fin0, fin1, first_sums, esrc, ein,
    ztr, kbuf, qbuf, vbuf,
    wsem, ys, yr, cs, cr, ns, nr, bs, br, us, ur, gs, gr, ps, pr, fs, fr, es, er,
):
    i = lax.axis_index("step")
    j = lax.axis_index("seq")
    x = lax.div(i, 2)
    c = lax.rem(i, 2)
    z = lax.div(j, 4)
    y = lax.rem(j, 4)
    s = lax.div(j, 2)
    p = lax.rem(j + s, 2)
    pos = 4 * (2 * c + p) + x
    own_chunk = 8 * lax.rem(y, 2) + z
    half = lax.div(y, 2)
    source_i = chunk_i(own_chunk)
    source_p = chunk_p(own_chunk)
    first_block = chunk_block(pos)
    low_lanes = lax.broadcasted_iota(jnp.int32, (ROWS, 128), 1) < C

    def rows_of(n):
        return pl.ds(pl.multiple_of(n * 16, 16), 16)

    def push(src, dst, send, recv, to_i, to_j):
        pltpu.make_async_remote_copy(
            src_ref=src, dst_ref=dst, send_sem=send, recv_sem=recv,
            device_id=(to_i, to_j), device_id_type=MESH,
        ).start()

    def await_bytes(like, sem):
        pltpu.make_async_copy(like, like, sem).wait()

    def each(low, high, fn):
        for k in range(low, high):
            fn(k)

    def group(fn):
        def one(k):
            n = lax.rem(pos + k, STEPS)
            fn(n, chunk_i(n), seq_of(s, chunk_p(n)))
        for k in sorted(range(1, STEPS), key=lambda k: -min(k % 4, -k % 4)):
            one(k)

    zp = latents.at[0]

    def column(fn):
        for k in sorted(range(1, SEQ), key=lambda k: abs(k - SEQ // 2)):
            fn(lax.rem(j + k, SEQ))

    barrier = pltpu.get_barrier_semaphore()

    def greet(to_i, to_j):
        pl.semaphore_signal(barrier, inc=1, device_id=(to_i, to_j), device_id_type=MESH)

    group(lambda n, ti, tj: greet(ti, tj))
    sends_start = lax.rem(y, 2) == c
    for k in sorted(range(8), key=lambda k: abs(k - 4)):
        for side in range(2):
            to_y = c + 2 * side
            if k:
                greet(i, 4 * lax.rem(z + k, 8) + to_y)
            else:
                @pl.when(y != to_y)
                def _():
                    greet(i, 4 * z + to_y)
    base_j = [seq_of(2 * i + n, source_p) for n in range(2)]
    base_mine = [jnp.logical_and(source_i == i, tj == j) for tj in base_j]
    from_j = [first_block + 2 * n for n in range(2)]
    from_i = lax.div(s, 2)
    from_mine = [jnp.logical_and(from_i == i, tj == j) for tj in from_j]
    for n in range(2):
        @pl.when(jnp.logical_not(from_mine[n]))
        def _():
            greet(from_i, from_j[n])

    head = pl.multiple_of(p * HEAD, HEAD)
    widths = [slice(n * DBLK, (n + 1) * DBLK) for n in range(PARTS)]
    pairs = [(start_hbm, start_ref), (noise_hbm, noise_ref), (gain_hbm, gain_ref), (qg_hbm, qg_ref), (kg_hbm, kg_ref)]
    for part in widths:
        pairs += [(wtime_hbm.at[:, part], wtime.at[:, part]), (wembed_hbm.at[:, part], left.at[0:64, part])]
        pairs += [
            (w.at[part, pl.ds(head, HEAD)], wall.at[part, n * HEAD:(n + 1) * HEAD]) for n, w in enumerate((wq_hbm, wk_hbm, wv_hbm))
        ]
        pairs += [
            (wfinal_hbm.at[:, part], right.at[0:64, part]),
            (wo_hbm.at[pl.ds(head, HEAD), part], left.at[96:224, part]),
        ]
    local = [pltpu.make_async_copy(src, dst, wsem.at[n]) for n, (src, dst) in enumerate(pairs)]
    for copy in local[:19]:
        copy.start()

    local[0].wait()
    z0 = start_ref[...]
    start_dup = jnp.concatenate([z0, z0], axis=1)
    low = low_lanes[0:16]
    own_half = lax.div(lax.broadcasted_iota(jnp.int32, (16, 128), 1), C) == half
    pieces = [start_dup[0:16], start_dup[16:32], start_dup[32:48]]
    packed_start = jnp.concatenate([
        jnp.where(own_half, pieces[0], pieces[1]), jnp.where(own_half, pieces[2], 0.0)], axis=0).astype(BF16)
    zsrc[...] = packed_start
    @pl.when(sends_start)
    def _():
        yin[8 * half + z] = packed_start

    local[1].wait()
    packed_noise = jnp.concatenate([noise_ref[0], noise_ref[1]], axis=1)
    nsrc[...] = packed_noise
    nin[i] = packed_noise

    alone_count = base_mine[0].astype(jnp.int32) + base_mine[1].astype(jnp.int32)
    pl.semaphore_wait(barrier, 15 + 2 - alone_count + 31 * sends_start.astype(jnp.int32))

    @pl.when(sends_start)
    def _():
        column(lambda tj: push(zsrc, yin.at[8 * half + z], ys, yr, i, tj))

    for copy in local[19:]:
        copy.start()


    first = ws_ref[0]
    index = (lax.broadcasted_iota(jnp.int32, (STEPS, 128), 0) + first).astype(F32)
    sigma_now = sigma_of(index)
    delta = sigma_of(index + 1.0) - sigma_now
    coeff = ETA * jnp.sqrt(-delta)
    delta_ref[...] = delta
    coeff_ref[...] = coeff
    own = sigma_of((jnp.zeros((STEPS, 128), jnp.int32) + (first + s)).astype(F32))
    lane = lax.broadcasted_iota(jnp.int32, (STEPS, 128), 1).astype(F32)
    angle = 1000.0 * own * jnp.exp(-math.log(10000.0) * lane / 128)
    feats = jnp.concatenate([jnp.cos(angle), jnp.sin(angle)], axis=1)
    feats = (feats / (1.0 + jnp.exp(-feats))).astype(BF16)
    right[192:256] = jnp.zeros((64, D), BF16)
    vbuf[C:C + 16] = jnp.ones((16, LEN), BF16)
    for n in range(2):
        ztr[128 * n + 64:128 * n + 128] = jnp.where(
            lax.broadcasted_iota(jnp.int32, (64, KBLK), 0) == 0, 1.0, 0.0).astype(BF16)

    each(1, COLS, lambda k: push(nsrc, nin.at[i], ns, nr, lax.rem(i + k, COLS), j))

    for copy in local[2:5]:
        copy.wait()
    sums = [0.0] * 4

    def fold_part(n):
        part = widths[n]
        for copy in local[5 + 7 * n:7 + 7 * n]:
            copy.wait()
        temb = mm(feats, wtime[:, part])
        embed = left[0:64, part]
        emb = embed.astype(F32)
        gain = gain_ref[:, part]
        for m, piece in enumerate(split(jnp.concatenate([emb * gain, temb * gain], axis=0))):
            fold[m * 80:(m + 1) * 80, part] = piece
        for m, piece in enumerate(split(temb)):
            left[64 + 16 * m:80 + 16 * m, part] = piece
        t_row = temb[0:1]
        right[128:192, part] = embed
        for copy in local[7 + 7 * n:12 + 7 * n]:
            copy.wait()
        right[64:128, part] = right[0:64, part]
        terms = (
            jnp.sum(emb * t_row, axis=1, keepdims=True),
            jnp.sum(t_row * t_row, axis=1, keepdims=True),
            mm(fold[:, part], wall[part]),
            lax.dot_general(left[:, part], right[:, part], (((1,), (1,)), ((), ())), preferred_element_type=F32),
        )
        for m, term in enumerate(terms):
            sums[m] = sums[m] + term

    each(0, PARTS - 1, fold_part)

    @pl.when(sends_start)
    def _():
        await_bytes(yin.at[0:15], yr)

    @pl.when(jnp.logical_not(sends_start))
    def _():
        await_bytes(yin, yr)

    for n in range(8):
        below, above = yin[n].astype(F32), yin[8 + n].astype(F32)
        there = rows_of(8 * c + n)
        zp[0, there, :] = jnp.where(low, below[0:16], above[0:16]).astype(BF16)
        zp[1, there, :] = pltpu.roll(jnp.where(low, above[0:16], below[0:16]), C, 1).astype(BF16)
        zp[2, there, :] = jnp.where(low, below[16:32], above[16:32]).astype(BF16)
    core_rows = pl.ds(pl.multiple_of(128 * c, 128), 128)
    push(zp.at[:, core_rows, :], zp.at[:, core_rows, :], cs, cr, i + 1 - 2 * c, j)

    fold_part(PARTS - 1)
    twice_et, t_square, folded, both = sums
    twice_et = 2.0 * twice_et
    folded = folded[0:80] + folded[80:160]
    cdup = both[0:64, 0:128]
    gram = both[0:64, 128:256]
    mout = both[96:224, 0:128]
    lanes64 = lax.broadcasted_iota(jnp.int32, (64, 128), 1)
    diag = jnp.concatenate([jnp.where(lanes64 < C, cdup, 0.0), jnp.where(lanes64 < C, 0.0, cdup)], axis=0)
    for n, part in enumerate(split(diag)):
        cdiag[n * 128:(n + 1) * 128] = part
    crow[...] = both[64:72, 0:128] + both[80:88, 0:128]

    value_fold = jnp.dot(folded[:, 256:384], mout, precision=lax.Precision.HIGHEST, preferred_element_type=F32)
    wide = jnp.concatenate([folded[:, 0:256], value_fold], axis=1)
    wide = jnp.concatenate([wide, jnp.zeros((48, 384), F32)], axis=0).T
    wide = jnp.concatenate([wide[0:320], jnp.where(lanes64 == C, twice_et, gram)], axis=0)
    whi = wide.astype(BF16)
    wqkv[:, 0:128] = whi
    wqkv[:, 128:256] = (wide - whi.astype(F32)).astype(BF16)
    scale_row = qg_ref[...] * kg_ref[...] * (1.0 / math.sqrt(HEAD))
    scale_col = jnp.broadcast_to(scale_row, (128, 128)).T[:, 0:1]

    step_row = lax.broadcasted_iota(jnp.int32, (STEPS, 128), 0)
    coeff_even = jnp.sum(jnp.where(step_row == 2 * i, coeff, 0.0), axis=0, keepdims=True)
    coeff_odd = jnp.sum(jnp.where(step_row == 2 * i + 1, coeff, 0.0), axis=0, keepdims=True)

    def send_base():
        await_bytes(nin.at[0:COLS - 1], nr)

        def noise_of(step_pair):
            both = nin[step_pair].astype(F32)
            turned = pltpu.roll(both, C, 1)
            return jnp.where(low_lanes, both, turned), jnp.where(low_lanes, turned, both)

        base = start_dup
        for pair in range(COLS):
            even, odd = noise_of(pair)
            pair_sum = coeff_ref[2 * pair:2 * pair + 1] * even + coeff_ref[2 * pair + 1:2 * pair + 2] * odd
            base = base + jnp.where(pair < i, pair_sum, 0.0)
        own_even, own_odd = noise_of(i)
        after_even = base + coeff_even * own_even
        after_odd = after_even + coeff_odd * own_odd
        basesrc[0] = base
        basesrc[1] = after_even
        basesrc[2] = after_odd
        for n in range(2):
            @pl.when(base_mine[n])
            def _():
                basein[half] = basesrc[n]

            @pl.when(jnp.logical_not(base_mine[n]))
            def _():
                push(basesrc.at[n], basein.at[half], bs.at[n], br.at[half], source_i, base_j[n])

    chunk = rows_of(pos)
    low = low_lanes[0:16]

    def project(lap, n):
        packed = latents[lap, n].T
        zb = jnp.concatenate([packed[0:64], packed[64:128]], axis=1)
        ztr[0:64] = zb
        ztr[128:192] = zb
        cols = slice(n * KBLK, (n + 1) * KBLK)
        out = mm(wqkv[...], ztr[...])
        yq, yk, yv, yg = out[0:128], out[128:256], out[256:320], out[320:384]
        mean_square = (jnp.sum(zb.astype(F32) * yg, axis=0, keepdims=True) + t_square) * (1.0 / D)
        square = jnp.maximum(mean_square, 0.0) + EPS
        aq = lax.rsqrt(jnp.mean(yq * yq, axis=0, keepdims=True) + EPS * square)
        ak = lax.rsqrt(jnp.mean(yk * yk, axis=0, keepdims=True) + EPS * square)
        qbuf[:, cols] = (yq * aq * scale_col).astype(BF16)
        kbuf[cols, :] = (yk * ak).astype(BF16).T
        vbuf[0:C, cols] = (yv * lax.rsqrt(square)).astype(BF16)

    def attend(block, keys, accs):
        here = slice(keys[0] * KBLK, (keys[-1] + 1) * KBLK)
        scores = [
            mm(kbuf[here], qbuf[:, block * KBLK + side * QBLK:block * KBLK + (side + 1) * QBLK]) for side in range(2)]
        parts = [mm(vbuf[:, here], jnp.exp(score).astype(BF16)) for score in scores]
        return [part if acc is None else acc + part for part, acc in zip(parts, accs)]

    def finish(lap, block, accs):
        outs = [acc[0:C] / acc[C:C + 1] for acc in accs]
        heads[lap, block] = jnp.concatenate(outs, axis=0).astype(BF16).T
        group(lambda n, ti, tj: push(
            heads.at[lap, block, rows_of(n), :], red.at[lap, block, pos], us.at[lap], ur.at[lap, block], ti, tj))

    def reduce_heads(lap, block):
        red[lap, block, pos] = heads[lap, block, chunk, :]
        latent = latents[lap, block, chunk, :]
        total = mm(jnp.concatenate([latent, latent], axis=1), cdiag[...]) + crow[0:1]
        await_bytes(red.at[lap, block, 0:STEPS - 1], ur.at[lap, block])
        for h in range(STEPS):
            total = total + red[lap, block, h].astype(F32)
        return total

    def pack_first(lap, first_part, second_part):
        vpack[lap, 0, 0:16] = jnp.where(low, first_part, pltpu.roll(second_part, C, 1)).astype(BF16)
        vpack[lap, 1, 0:16] = jnp.where(low, pltpu.roll(first_part, C, 1), second_part).astype(BF16)

    def pack_last(lap, part):
        vpack[lap, 0, 16:32] = jnp.where(low, part, 0.0).astype(BF16)
        vpack[lap, 1, 16:32] = jnp.where(low, pltpu.roll(part, C, 1), 0.0).astype(BF16)

    first_i = lax.div(s, 2)

    alone = jnp.logical_and(own_chunk == pos, first_i <= i)

    def to_owners(src, dst, rows, n):
        @pl.when(alone)
        def _():
            dst[s, rows] = src[half, rows]

        def one(k):
            to_i = k // 2
            to_j = first_block + 2 * (k % 2)
            mine = jnp.logical_and(to_i == i, to_j == j)

            @pl.when(jnp.logical_and(to_i >= first_i, jnp.logical_not(mine)))
            def _():
                push(src.at[k % 2, rows], dst.at[s, rows], fs.at[n], fr.at[n], to_i, to_j)
        each(0, 16, one)

    def owners_sent(dst, rows, n):
        for pair in range(COLS):
            for own in range(2):
                @pl.when(jnp.logical_and(first_i == pair, alone == (own == 1)))
                def _():
                    await_bytes(dst.at[0:2 * (COLS - pair) - own, rows], fs.at[n])

    def owner_sums(dst, rows, n):
        for pair in range(COLS):
            for own in range(2):
                @pl.when(jnp.logical_and(i == pair, alone == (own == 1)))
                def _():
                    await_bytes(dst.at[0:2 * pair + 2 - own, rows], fr.at[n])
        even = jnp.zeros((rows.stop - rows.start, 128), F32)
        odd = even
        for k in range(STEPS):
            later = delta_ref[k:k + 1] * dst[k, rows].astype(F32)
            even = even + jnp.where(k <= 2 * i, later, 0.0)
            odd = odd + jnp.where(k == 2 * i + 1, later, 0.0)
        return even, even + odd

    all_rows, early_rows, late_rows = slice(0, 32), slice(0, 16), slice(16, 32)
    blocks = range(3)
    velocities = {}

    def sum_heads(block):
        velocities[block] = reduce_heads(0, block)
        vsrc[block] = velocities[block].astype(BF16)
        gat[block, s] = velocities[block].astype(BF16)

        def send(k):
            to = lax.rem(s + k, STEPS)
            push(vsrc.at[block], gat.at[block, s], gs.at[block], gr.at[block], i, seq_of(to, p))
        for k in sorted(range(1, STEPS), key=lambda k: abs(k - STEPS // 2)):
            send(k)

    def next_latent(block):
        rows = slice(block * 16, (block + 1) * 16)
        latent = jnp.where(low, basein[0, rows], basein[1, rows])
        await_bytes(gat.at[block, 0:STEPS - 1], gr.at[block])
        for n in range(STEPS):
            latent = latent + jnp.where(n < s, delta_ref[n:n + 1] * gat[block, n].astype(F32), 0.0)
        latent = latent.astype(BF16)
        zsend[block] = latent
        latents[1, block, chunk, :] = latent
        group(lambda n, ti, tj: push(
            zsend.at[block], latents.at[1, block, chunk, :], ps.at[block], pr.at[block], ti, tj))

    def await_latents(block):
        await_bytes(latents.at[1, block, 0:15 * 16, :], pr.at[block])

    await_bytes(zp.at[:, 0:128, :], cr)
    for block in blocks:
        project(0, block)
    for block in blocks:
        finish(0, block, attend(block, blocks, (None, None)))
        if block:
            sum_heads(block - 1)
    send_base()
    sum_heads(2)
    for n in range(2):
        @pl.when(jnp.logical_not(from_mine[n]))
        def _():
            await_bytes(basein.at[n], br.at[n])
    next_latent(0)
    next_latent(1)
    pack_first(0, velocities[0], velocities[1])
    pack_last(0, velocities[2])

    await_latents(0)
    project(1, 0)
    next_latent(2)
    to_owners(vpack.at[0], fin0, all_rows, 0)
    await_latents(1)
    project(1, 1)
    early = [attend(block, (0, 1), (None, None)) for block in (0, 1)]
    await_latents(2)
    project(1, 2)
    for block in (0, 1):
        finish(1, block, attend(block, (2,), early[block]))
    finish(1, 2, attend(2, blocks, (None, None)))
    pack_first(1, reduce_heads(1, 0), reduce_heads(1, 1))
    to_owners(vpack.at[1], fin1, early_rows, 1)
    first_sums[0], first_sums[1] = owner_sums(fin0, all_rows, 0)
    pack_last(1, reduce_heads(1, 2))
    to_owners(vpack.at[1], fin1, late_rows, 2)

    even, odd = (
        jnp.concatenate(parts, axis=0) for parts in zip(owner_sums(fin1, early_rows, 1), owner_sums(fin1, late_rows, 2)))
    change_even = even - first_sums[0]
    change_odd = odd - first_sums[1]

    def unpack(x):
        return jnp.concatenate([x[0:16], pltpu.roll(x[0:16], C, 1), x[16:32]], axis=0)

    row = lax.broadcasted_iota(jnp.int32, (2, 128), 0)
    sum_even = jnp.sum(change_even * change_even, axis=0, keepdims=True)
    sum_odd = jnp.sum(change_odd * change_odd, axis=0, keepdims=True)
    partial = jnp.where(row == 0, sum_even, sum_odd)
    esrc[...] = partial
    ein[j] = partial
    column(lambda tj: push(esrc, ein.at[j], es, er, i, tj))
    for n, total in enumerate((basesrc[1] + unpack(even), basesrc[2] + unpack(odd))):
        out_ref[n] = total[:, 0:C]
    for lap in range(2):
        await_bytes(red.at[lap, :, 0:STEPS - 1], us.at[lap])
    for block in blocks:
        await_bytes(gat.at[block, 0:STEPS - 1], gs.at[block])
        await_bytes(latents.at[1, block, 0:15 * 16, :], ps.at[block])
    owners_sent(fin0, all_rows, 0)
    owners_sent(fin1, early_rows, 1)
    owners_sent(fin1, late_rows, 2)
    @pl.when(sends_start)
    def _():
        await_bytes(wall.at[0:31 * 32, 0:128], ys)

    await_bytes(nin.at[0:COLS - 1], ns)
    await_bytes(zp.at[:, 0:128, :], cs)
    for n in range(2):
        @pl.when(jnp.logical_not(base_mine[n]))
        def _():
            await_bytes(basesrc.at[n], bs.at[n])

    await_bytes(ein.at[0:SEQ - 1], er)
    total = ein[0]
    for n in range(1, SEQ):
        total = total + ein[n]
    total = total * (1.0 / (LEN * C))
    err_ref[0] = jnp.sum(total[0:1] / (coeff_even * coeff_even))
    err_ref[1] = jnp.sum(total[1:2] / (coeff_odd * coeff_odd))

    await_bytes(ein.at[0:SEQ - 1], es)


def per_device(
    start_latent, noise, window_start, w_embed, w_time, norm_gain, w_query, w_key, w_value, query_gain, key_gain, w_out, w_final,
):
    vmem = pl.BlockSpec(memory_space=pltpu.VMEM)
    hbm = pl.BlockSpec(memory_space=pltpu.HBM)
    smem = pl.BlockSpec(memory_space=pltpu.SMEM)
    dma = pltpu.SemaphoreType.DMA
    out, errors = pl.pallas_call(
        kernel,
        out_shape=(
            pltpu.VMEM((2, ROWS, C), F32),
            pltpu.SMEM((2,), F32),
        ),
        in_specs=[smem] + [hbm] * 12,
        out_specs=(vmem, smem),
        scratch_shapes=[
            pltpu.VMEM((ROWS, C), F32),
            pltpu.VMEM((2, ROWS, C), BF16),
            pltpu.VMEM((1, D), F32),
            pltpu.VMEM((1, HEAD), F32),
            pltpu.VMEM((1, HEAD), F32),
            pltpu.VMEM((256, D), BF16),
            pltpu.VMEM((D, 3 * HEAD), BF16),
            pltpu.VMEM((160, D), BF16),
            pltpu.VMEM((224, D), BF16),
            pltpu.VMEM((256, D), BF16),
            pltpu.VMEM((384, 256), BF16),
            pltpu.VMEM((256, 128), BF16),
            pltpu.VMEM((8, 128), F32),
            pltpu.VMEM((STEPS, 128), F32),
            pltpu.VMEM((STEPS, 128), F32),
            pltpu.VMEM((32, 128), BF16),
            pltpu.VMEM((16, 32, 128), BF16),
            pltpu.VMEM((ROWS, 128), BF16),
            pltpu.VMEM((COLS, ROWS, 128), BF16),
            pltpu.VMEM((3, ROWS, 128), F32),
            pltpu.VMEM((2, ROWS, 128), F32),
            pltpu.VMEM((2, 3, QBLK, 128), BF16),
            pltpu.VMEM((2, 3, QBLK, 128), BF16),
            pltpu.VMEM((2, 3, STEPS, 16, 128), BF16),
            pltpu.VMEM((3, 16, 128), BF16),
            pltpu.VMEM((2, 2, 32, 128), BF16),
            pltpu.VMEM((3, STEPS, 16, 128), BF16),
            pltpu.VMEM((3, 16, 128), BF16),
            pltpu.VMEM((STEPS, 32, 128), BF16),
            pltpu.VMEM((STEPS, 32, 128), BF16),
            pltpu.VMEM((2, 32, 128), F32),
            pltpu.VMEM((2, 128), F32),
            pltpu.VMEM((SEQ, 2, 128), F32),
            pltpu.VMEM((256, KBLK), BF16),
            pltpu.VMEM((LEN, HEAD), BF16),
            pltpu.VMEM((HEAD, LEN), BF16),
            pltpu.VMEM((C + 16, LEN), BF16),
            dma((5 + 7 * PARTS,)),
            dma, dma, dma, dma, dma, dma, dma((2,)), dma((2,)),
            dma((2,)), dma((2, 3)), dma((3,)), dma((3,)), dma((3,)), dma((3,)), dma((3,)), dma((3,)), dma, dma,
        ],
        compiler_params=pltpu.CompilerParams(
            collective_id=0, has_side_effects=True, vmem_limit_bytes=56 * 1024 * 1024),
    )(
        window_start, start_latent, noise, norm_gain.reshape(1, D), query_gain.reshape(1, HEAD), key_gain.reshape(1, HEAD),
        w_embed, w_time, w_final.T, w_query, w_key, w_value, w_out,
    )
    return out, errors


def solution(mesh):
    return jax.shard_map(
        per_device,
        mesh=mesh,
        in_specs=(
            P("seq", None), P("step", "seq", None), P(), P(), P(), P(),
            P(None, "step"), P(None, "step"), P(None, "step"), P(), P(), P("step", None), P(),
        ),
        out_specs=(P("step", "seq", None), P("step")),
        check_vma=False,
    )
```

```python
import math

import jax
import jax.numpy as jnp
from jax import lax
from jax.experimental import pallas as pl
from jax.experimental.pallas import tpu as pltpu
from jax.sharding import PartitionSpec as P

NSCHED = 28
EPS = 1e-06
SHIFT = 3.0
ETA = 0.5
MESH = pl.DeviceIdType.MESH
F32 = jnp.float32
BF16 = jnp.bfloat16

D = 3072
C = 64
HEAD = 128
LEN = 1536
HALF = LEN // 2
STEPS = 16
ROWS = 48
SEQ = 32
COLS = 8
QBLK = 256
KBLK = 512
PARTS = 4
DBLK = D // PARTS


def sigma_of(index):
    fraction = 1.0 - index / NSCHED
    return SHIFT * fraction / (1.0 + (SHIFT - 1.0) * fraction)


def chunk_i(n):
    return 2 * lax.rem(n, 4) + lax.div(n, 8)


def chunk_p(n):
    return lax.rem(lax.div(n, 4), 2)


def seq_of(step, part):
    return 2 * step + lax.rem(step + part, 2)


def chunk_block(n):
    return 4 * lax.rem(n, 8) + lax.div(n, 8)


def split(x):
    hi = x.astype(BF16)
    return hi, (x - hi.astype(F32)).astype(BF16)


def mm(a, b):
    return jnp.dot(a, b, preferred_element_type=F32)


def kernel(
    ws_ref, start_hbm, noise_hbm, gain_hbm, qg_hbm, kg_hbm,
    wembed_hbm, wtime_hbm, wfinal_hbm, wq_hbm, wk_hbm, wv_hbm, wo_hbm,
    out_ref, err_ref,
    start_ref, noise_ref, gain_ref, qg_ref, kg_ref,
    wtime, wall, fold, left, right, wqkv, cdiag, crow,
    delta_ref, coeff_ref,
    zsrc, yin, nsrc, nin, basesrc, basein,
    latents, heads, red, vsrc, vpack, gat, zsend, fin0, fin1, first_sums, esrc, ein,
    ztr, kbuf, qbuf, vbuf,
    wsem, ys, yr, cs, cr, ns, nr, bs, br, us, ur, gs, gr, ps, pr, fs, fr, es, er,
):
    i = lax.axis_index("step")
    j = lax.axis_index("seq")
    x = lax.div(i, 2)
    c = lax.rem(i, 2)
    z = lax.div(j, 4)
    y = lax.rem(j, 4)
    s = lax.div(j, 2)
    p = lax.rem(j + s, 2)
    pos = 4 * (2 * c + p) + x
    own_chunk = 8 * lax.rem(y, 2) + z
    half = lax.div(y, 2)
    source_i = chunk_i(own_chunk)
    source_p = chunk_p(own_chunk)
    first_block = chunk_block(pos)
    low_lanes = lax.broadcasted_iota(jnp.int32, (ROWS, 128), 1) < C

    def rows_of(n):
        return pl.ds(pl.multiple_of(n * 16, 16), 16)

    def push(src, dst, send, recv, to_i, to_j):
        pltpu.make_async_remote_copy(
            src_ref=src, dst_ref=dst, send_sem=send, recv_sem=recv,
            device_id=(to_i, to_j), device_id_type=MESH,
        ).start()

    def await_bytes(like, sem):
        pltpu.make_async_copy(like, like, sem).wait()

    def each(low, high, fn):
        for k in range(low, high):
            fn(k)

    def group(fn):
        def one(k):
            n = lax.rem(pos + k, STEPS)
            fn(n, chunk_i(n), seq_of(s, chunk_p(n)))
        for k in sorted(range(1, STEPS), key=lambda k: -min(k % 4, -k % 4)):
            one(k)

    zp = latents.at[0]

    def column(fn):
        for k in sorted(range(1, SEQ), key=lambda k: abs(k - SEQ // 2)):
            fn(lax.rem(j + k, SEQ))

    barrier = pltpu.get_barrier_semaphore()

    def greet(to_i, to_j):
        pl.semaphore_signal(barrier, inc=1, device_id=(to_i, to_j), device_id_type=MESH)

    group(lambda n, ti, tj: greet(ti, tj))
    sends_start = lax.rem(y, 2) == c
    for k in sorted(range(8), key=lambda k: abs(k - 4)):
        for side in range(2):
            to_y = c + 2 * side
            if k:
                greet(i, 4 * lax.rem(z + k, 8) + to_y)
            else:
                @pl.when(y != to_y)
                def _():
                    greet(i, 4 * z + to_y)
    base_j = [seq_of(2 * i + n, source_p) for n in range(2)]
    base_mine = [jnp.logical_and(source_i == i, tj == j) for tj in base_j]
    from_j = [first_block + 2 * n for n in range(2)]
    from_i = lax.div(s, 2)
    from_mine = [jnp.logical_and(from_i == i, tj == j) for tj in from_j]
    for n in range(2):
        @pl.when(jnp.logical_not(from_mine[n]))
        def _():
            greet(from_i, from_j[n])

    head = pl.multiple_of(p * HEAD, HEAD)
    widths = [slice(n * DBLK, (n + 1) * DBLK) for n in range(PARTS)]
    pairs = [(start_hbm, start_ref), (noise_hbm, noise_ref), (gain_hbm, gain_ref), (qg_hbm, qg_ref), (kg_hbm, kg_ref)]
    for part in widths:
        pairs += [(wtime_hbm.at[:, part], wtime.at[:, part]), (wembed_hbm.at[:, part], left.at[0:64, part])]
        pairs += [
            (w.at[part, pl.ds(head, HEAD)], wall.at[part, n * HEAD:(n + 1) * HEAD]) for n, w in enumerate((wq_hbm, wk_hbm, wv_hbm))
        ]
        pairs += [
            (wfinal_hbm.at[:, part], right.at[0:64, part]),
            (wo_hbm.at[pl.ds(head, HEAD), part], left.at[96:224, part]),
        ]
    local = [pltpu.make_async_copy(src, dst, wsem.at[n]) for n, (src, dst) in enumerate(pairs)]
    for copy in local[:19]:
        copy.start()

    local[0].wait()
    z0 = start_ref[...]
    start_dup = jnp.concatenate([z0, z0], axis=1)
    low = low_lanes[0:16]
    own_half = lax.div(lax.broadcasted_iota(jnp.int32, (16, 128), 1), C) == half
    pieces = [start_dup[0:16], start_dup[16:32], start_dup[32:48]]
    packed_start = jnp.concatenate([
        jnp.where(own_half, pieces[0], pieces[1]), jnp.where(own_half, pieces[2], 0.0)], axis=0).astype(BF16)
    zsrc[...] = packed_start
    @pl.when(sends_start)
    def _():
        yin[8 * half + z] = packed_start

    local[1].wait()
    packed_noise = jnp.concatenate([noise_ref[0], noise_ref[1]], axis=1)
    nsrc[...] = packed_noise
    nin[i] = packed_noise

    alone_count = base_mine[0].astype(jnp.int32) + base_mine[1].astype(jnp.int32)
    pl.semaphore_wait(barrier, 15 + 2 - alone_count + 31 * sends_start.astype(jnp.int32))

    @pl.when(sends_start)
    def _():
        column(lambda tj: push(zsrc, yin.at[8 * half + z], ys, yr, i, tj))

    for copy in local[19:]:
        copy.start()


    first = ws_ref[0]
    index = (lax.broadcasted_iota(jnp.int32, (STEPS, 128), 0) + first).astype(F32)
    sigma_now = sigma_of(index)
    delta = sigma_of(index + 1.0) - sigma_now
    coeff = ETA * jnp.sqrt(-delta)
    delta_ref[...] = delta
    coeff_ref[...] = coeff
    own = sigma_of((jnp.zeros((STEPS, 128), jnp.int32) + (first + s)).astype(F32))
    lane = lax.broadcasted_iota(jnp.int32, (STEPS, 128), 1).astype(F32)
    angle = 1000.0 * own * jnp.exp(-math.log(10000.0) * lane / 128)
    feats = jnp.concatenate([jnp.cos(angle), jnp.sin(angle)], axis=1)
    feats = (feats / (1.0 + jnp.exp(-feats))).astype(BF16)
    right[192:256] = jnp.zeros((64, D), BF16)
    vbuf[C:C + 16] = jnp.ones((16, LEN), BF16)
    for n in range(2):
        ztr[128 * n + 64:128 * n + 128] = jnp.where(
            lax.broadcasted_iota(jnp.int32, (64, KBLK), 0) == 0, 1.0, 0.0).astype(BF16)

    each(1, COLS, lambda k: push(nsrc, nin.at[i], ns, nr, lax.rem(i + k, COLS), j))

    for copy in local[2:5]:
        copy.wait()
    sums = [0.0] * 4

    def fold_part(n):
        part = widths[n]
        for copy in local[5 + 7 * n:7 + 7 * n]:
            copy.wait()
        temb = mm(feats, wtime[:, part])
        embed = left[0:64, part]
        emb = embed.astype(F32)
        gain = gain_ref[:, part]
        for m, piece in enumerate(split(jnp.concatenate([emb * gain, temb * gain], axis=0))):
            fold[m * 80:(m + 1) * 80, part] = piece
        for m, piece in enumerate(split(temb)):
            left[64 + 16 * m:80 + 16 * m, part] = piece
        t_row = temb[0:1]
        right[128:192, part] = embed
        for copy in local[7 + 7 * n:12 + 7 * n]:
            copy.wait()
        right[64:128, part] = right[0:64, part]
        terms = (
            jnp.sum(emb * t_row, axis=1, keepdims=True),
            jnp.sum(t_row * t_row, axis=1, keepdims=True),
            mm(fold[:, part], wall[part]),
            lax.dot_general(left[:, part], right[:, part], (((1,), (1,)), ((), ())), preferred_element_type=F32),
        )
        for m, term in enumerate(terms):
            sums[m] = sums[m] + term

    each(0, PARTS - 1, fold_part)

    @pl.when(sends_start)
    def _():
        await_bytes(yin.at[0:15], yr)

    @pl.when(jnp.logical_not(sends_start))
    def _():
        await_bytes(yin, yr)

    for n in range(8):
        below, above = yin[n].astype(F32), yin[8 + n].astype(F32)
        there = rows_of(8 * c + n)
        zp[0, there, :] = jnp.where(low, below[0:16], above[0:16]).astype(BF16)
        zp[1, there, :] = pltpu.roll(jnp.where(low, above[0:16], below[0:16]), C, 1).astype(BF16)
        zp[2, there, :] = jnp.where(low, below[16:32], above[16:32]).astype(BF16)
    core_rows = pl.ds(pl.multiple_of(128 * c, 128), 128)
    push(zp.at[:, core_rows, :], zp.at[:, core_rows, :], cs, cr, i + 1 - 2 * c, j)

    fold_part(PARTS - 1)
    twice_et, t_square, folded, both = sums
    twice_et = 2.0 * twice_et
    folded = folded[0:80] + folded[80:160]
    cdup = both[0:64, 0:128]
    gram = both[0:64, 128:256]
    mout = both[96:224, 0:128]
    lanes64 = lax.broadcasted_iota(jnp.int32, (64, 128), 1)
    diag = jnp.concatenate([jnp.where(lanes64 < C, cdup, 0.0), jnp.where(lanes64 < C, 0.0, cdup)], axis=0)
    for n, part in enumerate(split(diag)):
        cdiag[n * 128:(n + 1) * 128] = part
    crow[...] = both[64:72, 0:128] + both[80:88, 0:128]

    value_fold = jnp.dot(folded[:, 256:384], mout, precision=lax.Precision.HIGHEST, preferred_element_type=F32)
    wide = jnp.concatenate([folded[:, 0:256], value_fold], axis=1)
    wide = jnp.concatenate([wide, jnp.zeros((48, 384), F32)], axis=0).T
    wide = jnp.concatenate([wide[0:320], jnp.where(lanes64 == C, twice_et, gram)], axis=0)
    whi = wide.astype(BF16)
    wqkv[:, 0:128] = whi
    wqkv[:, 128:256] = (wide - whi.astype(F32)).astype(BF16)
    scale_row = qg_ref[...] * kg_ref[...] * (1.0 / math.sqrt(HEAD))
    scale_col = jnp.broadcast_to(scale_row, (128, 128)).T[:, 0:1]

    step_row = lax.broadcasted_iota(jnp.int32, (STEPS, 128), 0)
    coeff_even = jnp.sum(jnp.where(step_row == 2 * i, coeff, 0.0), axis=0, keepdims=True)
    coeff_odd = jnp.sum(jnp.where(step_row == 2 * i + 1, coeff, 0.0), axis=0, keepdims=True)

    def send_base():
        await_bytes(nin.at[0:COLS - 1], nr)

        def noise_of(step_pair):
            both = nin[step_pair].astype(F32)
            turned = pltpu.roll(both, C, 1)
            return jnp.where(low_lanes, both, turned), jnp.where(low_lanes, turned, both)

        base = start_dup
        for pair in range(COLS):
            even, odd = noise_of(pair)
            pair_sum = coeff_ref[2 * pair:2 * pair + 1] * even + coeff_ref[2 * pair + 1:2 * pair + 2] * odd
            base = base + jnp.where(pair < i, pair_sum, 0.0)
        own_even, own_odd = noise_of(i)
        after_even = base + coeff_even * own_even
        after_odd = after_even + coeff_odd * own_odd
        basesrc[0] = base
        basesrc[1] = after_even
        basesrc[2] = after_odd
        for n in range(2):
            @pl.when(base_mine[n])
            def _():
                basein[half] = basesrc[n]

            @pl.when(jnp.logical_not(base_mine[n]))
            def _():
                push(basesrc.at[n], basein.at[half], bs.at[n], br.at[half], source_i, base_j[n])

    chunk = rows_of(pos)
    low = low_lanes[0:16]

    def project(lap, n):
        packed = latents[lap, n].astype(F32).T
        zb = jnp.concatenate([packed[0:64], packed[64:128]], axis=1).astype(BF16)
        ztr[0:64] = zb
        ztr[128:192] = zb
        cols = slice(n * KBLK, (n + 1) * KBLK)
        out = mm(wqkv[...], ztr[...])
        yq, yk, yv, yg = out[0:128], out[128:256], out[256:320], out[320:384]
        mean_square = (jnp.sum(zb.astype(F32) * yg, axis=0, keepdims=True) + t_square) * (1.0 / D)
        square = jnp.maximum(mean_square, 0.0) + EPS
        aq = lax.rsqrt(jnp.mean(yq * yq, axis=0, keepdims=True) + EPS * square)
        ak = lax.rsqrt(jnp.mean(yk * yk, axis=0, keepdims=True) + EPS * square)
        qbuf[:, cols] = (yq * aq * scale_col).astype(BF16)
        kbuf[cols, :] = (yk * ak).T.astype(BF16)
        vbuf[0:C, cols] = (yv * lax.rsqrt(square)).astype(BF16)

    def attend(block, keys, accs):
        here = slice(keys[0] * KBLK, (keys[-1] + 1) * KBLK)
        scores = [
            mm(kbuf[here], qbuf[:, block * KBLK + side * QBLK:block * KBLK + (side + 1) * QBLK]) for side in range(2)]
        parts = [mm(vbuf[:, here], jnp.exp(score).astype(BF16)) for score in scores]
        return [part if acc is None else acc + part for part, acc in zip(parts, accs)]

    def finish(lap, block, accs):
        outs = [acc[0:C] / acc[C:C + 1] for acc in accs]
        heads[lap, block] = jnp.concatenate(outs, axis=0).T.astype(BF16)
        group(lambda n, ti, tj: push(
            heads.at[lap, block, rows_of(n), :], red.at[lap, block, pos], us.at[lap], ur.at[lap, block], ti, tj))

    def reduce_heads(lap, block):
        red[lap, block, pos] = heads[lap, block, chunk, :]
        latent = latents[lap, block, chunk, :]
        total = mm(jnp.concatenate([latent, latent], axis=1), cdiag[...]) + crow[0:1]
        await_bytes(red.at[lap, block, 0:STEPS - 1], ur.at[lap, block])
        for h in range(STEPS):
            total = total + red[lap, block, h].astype(F32)
        return total

    def pack_first(lap, first_part, second_part):
        vpack[lap, 0, 0:16] = jnp.where(low, first_part, pltpu.roll(second_part, C, 1)).astype(BF16)
        vpack[lap, 1, 0:16] = jnp.where(low, pltpu.roll(first_part, C, 1), second_part).astype(BF16)

    def pack_last(lap, part):
        vpack[lap, 0, 16:32] = jnp.where(low, part, 0.0).astype(BF16)
        vpack[lap, 1, 16:32] = jnp.where(low, pltpu.roll(part, C, 1), 0.0).astype(BF16)

    first_i = lax.div(s, 2)

    alone = jnp.logical_and(own_chunk == pos, first_i <= i)

    def to_owners(src, dst, rows, n):
        @pl.when(alone)
        def _():
            dst[s, rows] = src[half, rows]

        def one(k):
            to_i = k // 2
            to_j = first_block + 2 * (k % 2)
            mine = jnp.logical_and(to_i == i, to_j == j)

            @pl.when(jnp.logical_and(to_i >= first_i, jnp.logical_not(mine)))
            def _():
                push(src.at[k % 2, rows], dst.at[s, rows], fs.at[n], fr.at[n], to_i, to_j)
        each(0, 16, one)

    def owners_sent(dst, rows, n):
        for pair in range(COLS):
            for own in range(2):
                @pl.when(jnp.logical_and(first_i == pair, alone == (own == 1)))
                def _():
                    await_bytes(dst.at[0:2 * (COLS - pair) - own, rows], fs.at[n])

    def owner_sums(dst, rows, n):
        for pair in range(COLS):
            for own in range(2):
                @pl.when(jnp.logical_and(i == pair, alone == (own == 1)))
                def _():
                    await_bytes(dst.at[0:2 * pair + 2 - own, rows], fr.at[n])
        even = jnp.zeros((rows.stop - rows.start, 128), F32)
        odd = even
        for k in range(STEPS):
            later = delta_ref[k:k + 1] * dst[k, rows].astype(F32)
            even = even + jnp.where(k <= 2 * i, later, 0.0)
            odd = odd + jnp.where(k == 2 * i + 1, later, 0.0)
        return even, even + odd

    all_rows, early_rows, late_rows = slice(0, 32), slice(0, 16), slice(16, 32)
    blocks = range(3)
    velocities = {}

    def sum_heads(block):
        velocities[block] = reduce_heads(0, block)
        vsrc[block] = velocities[block].astype(BF16)
        gat[block, s] = velocities[block].astype(BF16)

        def send(k):
            to = lax.rem(s + k, STEPS)
            push(vsrc.at[block], gat.at[block, s], gs.at[block], gr.at[block], i, seq_of(to, p))
        for k in sorted(range(1, STEPS), key=lambda k: abs(k - STEPS // 2)):
            send(k)

    def next_latent(block):
        rows = slice(block * 16, (block + 1) * 16)
        latent = jnp.where(low, basein[0, rows], basein[1, rows])
        await_bytes(gat.at[block, 0:STEPS - 1], gr.at[block])
        for n in range(STEPS):
            latent = latent + jnp.where(n < s, delta_ref[n:n + 1] * gat[block, n].astype(F32), 0.0)
        latent = latent.astype(BF16)
        zsend[block] = latent
        latents[1, block, chunk, :] = latent
        group(lambda n, ti, tj: push(
            zsend.at[block], latents.at[1, block, chunk, :], ps.at[block], pr.at[block], ti, tj))

    def await_latents(block):
        await_bytes(latents.at[1, block, 0:15 * 16, :], pr.at[block])

    await_bytes(zp.at[:, 0:128, :], cr)
    for block in blocks:
        project(0, block)
    for block in blocks:
        finish(0, block, attend(block, blocks, (None, None)))
        if block:
            sum_heads(block - 1)
    send_base()
    sum_heads(2)
    for n in range(2):
        @pl.when(jnp.logical_not(from_mine[n]))
        def _():
            await_bytes(basein.at[n], br.at[n])
    next_latent(0)
    next_latent(1)
    pack_first(0, velocities[0], velocities[1])
    pack_last(0, velocities[2])

    await_latents(0)
    project(1, 0)
    next_latent(2)
    await_latents(1)
    project(1, 1)
    early = [attend(block, (0, 1), (None, None)) for block in (0, 1)]
    await_latents(2)
    to_owners(vpack.at[0], fin0, all_rows, 0)
    project(1, 2)
    for block in (0, 1):
        finish(1, block, attend(block, (2,), early[block]))
    finish(1, 2, attend(2, blocks, (None, None)))
    pack_first(1, reduce_heads(1, 0), reduce_heads(1, 1))
    to_owners(vpack.at[1], fin1, early_rows, 1)
    first_sums[0], first_sums[1] = owner_sums(fin0, all_rows, 0)
    pack_last(1, reduce_heads(1, 2))
    to_owners(vpack.at[1], fin1, late_rows, 2)

    even, odd = (
        jnp.concatenate(parts, axis=0) for parts in zip(owner_sums(fin1, early_rows, 1), owner_sums(fin1, late_rows, 2)))
    change_even = even - first_sums[0]
    change_odd = odd - first_sums[1]

    def unpack(x):
        return jnp.concatenate([x[0:16], pltpu.roll(x[0:16], C, 1), x[16:32]], axis=0)

    row = lax.broadcasted_iota(jnp.int32, (2, 128), 0)
    sum_even = jnp.sum(change_even * change_even, axis=0, keepdims=True)
    sum_odd = jnp.sum(change_odd * change_odd, axis=0, keepdims=True)
    partial = jnp.where(row == 0, sum_even, sum_odd)
    esrc[...] = partial
    ein[j] = partial
    column(lambda tj: push(esrc, ein.at[j], es, er, i, tj))
    for n, total in enumerate((basesrc[1] + unpack(even), basesrc[2] + unpack(odd))):
        out_ref[n] = total[:, 0:C]
    for lap in range(2):
        await_bytes(red.at[lap, :, 0:STEPS - 1], us.at[lap])
    for block in blocks:
        await_bytes(gat.at[block, 0:STEPS - 1], gs.at[block])
        await_bytes(latents.at[1, block, 0:15 * 16, :], ps.at[block])
    owners_sent(fin0, all_rows, 0)
    owners_sent(fin1, early_rows, 1)
    owners_sent(fin1, late_rows, 2)
    @pl.when(sends_start)
    def _():
        await_bytes(wall.at[0:31 * 32, 0:128], ys)

    await_bytes(nin.at[0:COLS - 1], ns)
    await_bytes(zp.at[:, 0:128, :], cs)
    for n in range(2):
        @pl.when(jnp.logical_not(base_mine[n]))
        def _():
            await_bytes(basesrc.at[n], bs.at[n])

    await_bytes(ein.at[0:SEQ - 1], er)
    total = ein[0]
    for n in range(1, SEQ):
        total = total + ein[n]
    total = total * (1.0 / (LEN * C))
    err_ref[0] = jnp.sum(total[0:1] / (coeff_even * coeff_even))
    err_ref[1] = jnp.sum(total[1:2] / (coeff_odd * coeff_odd))

    await_bytes(ein.at[0:SEQ - 1], es)


def per_device(
    start_latent, noise, window_start, w_embed, w_time, norm_gain, w_query, w_key, w_value, query_gain, key_gain, w_out, w_final,
):
    vmem = pl.BlockSpec(memory_space=pltpu.VMEM)
    hbm = pl.BlockSpec(memory_space=pltpu.HBM)
    smem = pl.BlockSpec(memory_space=pltpu.SMEM)
    dma = pltpu.SemaphoreType.DMA
    out, errors = pl.pallas_call(
        kernel,
        out_shape=(
            pltpu.VMEM((2, ROWS, C), F32),
            pltpu.SMEM((2,), F32),
        ),
        in_specs=[smem] + [hbm] * 12,
        out_specs=(vmem, smem),
        scratch_shapes=[
            pltpu.VMEM((ROWS, C), F32),
            pltpu.VMEM((2, ROWS, C), BF16),
            pltpu.VMEM((1, D), F32),
            pltpu.VMEM((1, HEAD), F32),
            pltpu.VMEM((1, HEAD), F32),
            pltpu.VMEM((256, D), BF16),
            pltpu.VMEM((D, 3 * HEAD), BF16),
            pltpu.VMEM((160, D), BF16),
            pltpu.VMEM((224, D), BF16),
            pltpu.VMEM((256, D), BF16),
            pltpu.VMEM((384, 256), BF16),
            pltpu.VMEM((256, 128), BF16),
            pltpu.VMEM((8, 128), F32),
            pltpu.VMEM((STEPS, 128), F32),
            pltpu.VMEM((STEPS, 128), F32),
            pltpu.VMEM((32, 128), BF16),
            pltpu.VMEM((16, 32, 128), BF16),
            pltpu.VMEM((ROWS, 128), BF16),
            pltpu.VMEM((COLS, ROWS, 128), BF16),
            pltpu.VMEM((3, ROWS, 128), F32),
            pltpu.VMEM((2, ROWS, 128), F32),
            pltpu.VMEM((2, 3, QBLK, 128), BF16),
            pltpu.VMEM((2, 3, QBLK, 128), BF16),
            pltpu.VMEM((2, 3, STEPS, 16, 128), BF16),
            pltpu.VMEM((3, 16, 128), BF16),
            pltpu.VMEM((2, 2, 32, 128), BF16),
            pltpu.VMEM((3, STEPS, 16, 128), BF16),
            pltpu.VMEM((3, 16, 128), BF16),
            pltpu.VMEM((STEPS, 32, 128), BF16),
            pltpu.VMEM((STEPS, 32, 128), BF16),
            pltpu.VMEM((2, 32, 128), F32),
            pltpu.VMEM((2, 128), F32),
            pltpu.VMEM((SEQ, 2, 128), F32),
            pltpu.VMEM((256, KBLK), BF16),
            pltpu.VMEM((LEN, HEAD), BF16),
            pltpu.VMEM((HEAD, LEN), BF16),
            pltpu.VMEM((C + 16, LEN), BF16),
            dma((5 + 7 * PARTS,)),
            dma, dma, dma, dma, dma, dma, dma((2,)), dma((2,)),
            dma((2,)), dma((2, 3)), dma((3,)), dma((3,)), dma((3,)), dma((3,)), dma((3,)), dma((3,)), dma, dma,
        ],
        compiler_params=pltpu.CompilerParams(
            collective_id=0, has_side_effects=True, vmem_limit_bytes=56 * 1024 * 1024),
    )(
        window_start, start_latent, noise, norm_gain.reshape(1, D), query_gain.reshape(1, HEAD), key_gain.reshape(1, HEAD),
        w_embed, w_time, w_final.T, w_query, w_key, w_value, w_out,
    )
    return out, errors


def solution(mesh):
    return jax.shard_map(
        per_device,
        mesh=mesh,
        in_specs=(
            P("seq", None), P("step", "seq", None), P(), P(), P(), P(),
            P(None, "step"), P(None, "step"), P(None, "step"), P(), P(), P("step", None), P(),
        ),
        out_specs=(P("step", "seq", None), P("step")),
        check_vma=False,
    )
```

```python
import math

import jax
import jax.numpy as jnp
from jax import lax
from jax.experimental import pallas as pl
from jax.experimental.pallas import tpu as pltpu
from jax.sharding import PartitionSpec as P

NSCHED = 28
EPS = 1e-06
SHIFT = 3.0
ETA = 0.5
MESH = pl.DeviceIdType.MESH
F32 = jnp.float32
BF16 = jnp.bfloat16

D = 3072
C = 64
HEAD = 128
LEN = 1536
HALF = LEN // 2
STEPS = 16
ROWS = 48
SEQ = 32
COLS = 8
QBLK = 256
KBLK = 512
PARTS = 4
DBLK = D // PARTS


def sigma_of(index):
    fraction = 1.0 - index / NSCHED
    return SHIFT * fraction / (1.0 + (SHIFT - 1.0) * fraction)


def chunk_i(n):
    return 2 * lax.rem(n, 4) + lax.div(n, 8)


def chunk_p(n):
    return lax.rem(lax.div(n, 4), 2)


def seq_of(step, part):
    return 2 * step + lax.rem(step + part, 2)


def chunk_block(n):
    return 4 * lax.rem(n, 8) + lax.div(n, 8)


def split(x):
    hi = x.astype(BF16)
    return hi, (x - hi.astype(F32)).astype(BF16)


def mm(a, b):
    return jnp.dot(a, b, preferred_element_type=F32)


def kernel(
    ws_ref, start_hbm, noise_hbm, gain_hbm, qg_hbm, kg_hbm,
    wembed_hbm, wtime_hbm, wfinal_hbm, wq_hbm, wk_hbm, wv_hbm, wo_hbm,
    out_ref, err_ref,
    start_ref, noise_ref, gain_ref, qg_ref, kg_ref,
    wtime, wall, fold, left, right, wqkv, cdiag, crow,
    delta_ref, coeff_ref,
    zsrc, yin, nsrc, nin, basesrc, basein,
    latents, heads, red, vsrc, vpack, gat, zsend, fin1, tsend, first_sums, esrc, ein,
    ztr, kbuf, qbuf, vbuf,
    wsem, ys, yr, cs, cr, ns, nr, bs, br, us, ur, gs, gr, ps, pr, fs, fr, ts, tr, es, er,
):
    i = lax.axis_index("step")
    j = lax.axis_index("seq")
    x = lax.div(i, 2)
    c = lax.rem(i, 2)
    z = lax.div(j, 4)
    y = lax.rem(j, 4)
    s = lax.div(j, 2)
    p = lax.rem(j + s, 2)
    pos = 4 * (2 * c + p) + x
    own_chunk = 8 * lax.rem(y, 2) + z
    half = lax.div(y, 2)
    source_i = chunk_i(own_chunk)
    source_p = chunk_p(own_chunk)
    first_block = chunk_block(pos)
    low_lanes = lax.broadcasted_iota(jnp.int32, (ROWS, 128), 1) < C

    def rows_of(n):
        return pl.ds(pl.multiple_of(n * 16, 16), 16)

    def push(src, dst, send, recv, to_i, to_j):
        pltpu.make_async_remote_copy(
            src_ref=src, dst_ref=dst, send_sem=send, recv_sem=recv,
            device_id=(to_i, to_j), device_id_type=MESH,
        ).start()

    def await_bytes(like, sem):
        pltpu.make_async_copy(like, like, sem).wait()

    def each(low, high, fn):
        for k in range(low, high):
            fn(k)

    def group(fn):
        def one(k):
            n = lax.rem(pos + k, STEPS)
            fn(n, chunk_i(n), seq_of(s, chunk_p(n)))
        for k in sorted(range(1, STEPS), key=lambda k: -min(k % 4, -k % 4)):
            one(k)

    zp = latents.at[0]

    def column(fn):
        for k in sorted(range(1, SEQ), key=lambda k: abs(k - SEQ // 2)):
            fn(lax.rem(j + k, SEQ))

    barrier = pltpu.get_barrier_semaphore()

    def greet(to_i, to_j):
        pl.semaphore_signal(barrier, inc=1, device_id=(to_i, to_j), device_id_type=MESH)

    group(lambda n, ti, tj: greet(ti, tj))
    column(lambda tj: greet(i, tj))
    base_j = [seq_of(2 * i + n, source_p) for n in range(2)]
    base_mine = [jnp.logical_and(source_i == i, tj == j) for tj in base_j]
    from_j = [first_block + 2 * n for n in range(2)]
    from_i = lax.div(s, 2)
    from_mine = [jnp.logical_and(from_i == i, tj == j) for tj in from_j]
    for n in range(2):
        @pl.when(jnp.logical_not(from_mine[n]))
        def _():
            greet(from_i, from_j[n])

    head = pl.multiple_of(p * HEAD, HEAD)
    widths = [slice(n * DBLK, (n + 1) * DBLK) for n in range(PARTS)]
    pairs = [(start_hbm, start_ref), (noise_hbm, noise_ref), (gain_hbm, gain_ref), (qg_hbm, qg_ref), (kg_hbm, kg_ref)]
    for part in widths:
        pairs += [(wtime_hbm.at[:, part], wtime.at[:, part]), (wembed_hbm.at[:, part], left.at[0:64, part])]
        pairs += [
            (w.at[part, pl.ds(head, HEAD)], wall.at[part, n * HEAD:(n + 1) * HEAD]) for n, w in enumerate((wq_hbm, wk_hbm, wv_hbm))
        ]
        pairs += [
            (wfinal_hbm.at[:, part], right.at[0:64, part]),
            (wo_hbm.at[pl.ds(head, HEAD), part], left.at[96:224, part]),
        ]
    local = [pltpu.make_async_copy(src, dst, wsem.at[n]) for n, (src, dst) in enumerate(pairs)]
    for copy in local:
        copy.start()

    local[0].wait()
    z0 = start_ref[...]
    start_dup = jnp.concatenate([z0, z0], axis=1)
    low = low_lanes[0:16]
    own_half = lax.div(lax.broadcasted_iota(jnp.int32, (16, 128), 1), C) == half
    pieces = [start_dup[0:16], start_dup[16:32], start_dup[32:48]]
    packed_start = jnp.concatenate([
        jnp.where(own_half, pieces[0], pieces[1]), jnp.where(own_half, pieces[2], 0.0)], axis=0).astype(BF16)
    zsrc[...] = packed_start
    sends_start = lax.rem(y, 2) == c

    @pl.when(sends_start)
    def _():
        yin[8 * half + z] = packed_start

    local[1].wait()
    packed_noise = jnp.concatenate([noise_ref[0], noise_ref[1]], axis=1)
    nsrc[...] = packed_noise
    nin[i] = packed_noise

    alone_count = base_mine[0].astype(jnp.int32) + base_mine[1].astype(jnp.int32)
    pl.semaphore_wait(barrier, 15 + 31 + 2 - alone_count)

    @pl.when(sends_start)
    def _():
        column(lambda tj: push(zsrc, yin.at[8 * half + z], ys, yr, i, tj))


    first = ws_ref[0]
    index = (lax.broadcasted_iota(jnp.int32, (STEPS, 128), 0) + first).astype(F32)
    sigma_now = sigma_of(index)
    delta = sigma_of(index + 1.0) - sigma_now
    coeff = ETA * jnp.sqrt(-delta)
    delta_ref[...] = delta
    coeff_ref[...] = coeff
    own = sigma_of((jnp.zeros((STEPS, 128), jnp.int32) + (first + s)).astype(F32))
    lane = lax.broadcasted_iota(jnp.int32, (STEPS, 128), 1).astype(F32)
    angle = 1000.0 * own * jnp.exp(-math.log(10000.0) * lane / 128)
    feats = jnp.concatenate([jnp.cos(angle), jnp.sin(angle)], axis=1)
    feats = (feats / (1.0 + jnp.exp(-feats))).astype(BF16)
    right[192:256] = jnp.zeros((64, D), BF16)
    vbuf[C:C + 16] = jnp.ones((16, LEN), BF16)
    for n in range(2):
        ztr[128 * n + 64:128 * n + 128] = jnp.where(
            lax.broadcasted_iota(jnp.int32, (64, KBLK), 0) == 0, 1.0, 0.0).astype(BF16)

    each(1, COLS, lambda k: push(nsrc, nin.at[i], ns, nr, lax.rem(i + k, COLS), j))

    for copy in local[2:5]:
        copy.wait()
    sums = [0.0] * 4

    def fold_part(n):
        part = widths[n]
        for copy in local[5 + 7 * n:7 + 7 * n]:
            copy.wait()
        temb = mm(feats, wtime[:, part])
        embed = left[0:64, part]
        emb = embed.astype(F32)
        gain = gain_ref[:, part]
        for m, piece in enumerate(split(jnp.concatenate([emb * gain, temb * gain], axis=0))):
            fold[m * 80:(m + 1) * 80, part] = piece
        for m, piece in enumerate(split(temb)):
            left[64 + 16 * m:80 + 16 * m, part] = piece
        t_row = temb[0:1]
        right[128:192, part] = embed
        for copy in local[7 + 7 * n:12 + 7 * n]:
            copy.wait()
        right[64:128, part] = right[0:64, part]
        terms = (
            jnp.sum(emb * t_row, axis=1, keepdims=True),
            jnp.sum(t_row * t_row, axis=1, keepdims=True),
            mm(fold[:, part], wall[part]),
            lax.dot_general(left[:, part], right[:, part], (((1,), (1,)), ((), ())), preferred_element_type=F32),
        )
        for m, term in enumerate(terms):
            sums[m] = sums[m] + term

    each(0, PARTS - 1, fold_part)

    @pl.when(sends_start)
    def _():
        await_bytes(yin.at[0:15], yr)

    @pl.when(jnp.logical_not(sends_start))
    def _():
        await_bytes(yin, yr)

    for n in range(8):
        below, above = yin[n].astype(F32), yin[8 + n].astype(F32)
        there = rows_of(8 * c + n)
        zp[0, there, :] = jnp.where(low, below[0:16], above[0:16]).astype(BF16)
        zp[1, there, :] = pltpu.roll(jnp.where(low, above[0:16], below[0:16]), C, 1).astype(BF16)
        zp[2, there, :] = jnp.where(low, below[16:32], above[16:32]).astype(BF16)
    core_rows = pl.ds(pl.multiple_of(128 * c, 128), 128)
    push(zp.at[:, core_rows, :], zp.at[:, core_rows, :], cs, cr, i + 1 - 2 * c, j)

    fold_part(PARTS - 1)
    twice_et, t_square, folded, both = sums
    twice_et = 2.0 * twice_et
    folded = folded[0:80] + folded[80:160]
    cdup = both[0:64, 0:128]
    gram = both[0:64, 128:256]
    mout = both[96:224, 0:128]
    lanes64 = lax.broadcasted_iota(jnp.int32, (64, 128), 1)
    diag = jnp.concatenate([jnp.where(lanes64 < C, cdup, 0.0), jnp.where(lanes64 < C, 0.0, cdup)], axis=0)
    for n, part in enumerate(split(diag)):
        cdiag[n * 128:(n + 1) * 128] = part
    crow[...] = both[64:72, 0:128] + both[80:88, 0:128]

    value_fold = jnp.dot(folded[:, 256:384], mout, precision=lax.Precision.HIGHEST, preferred_element_type=F32)
    wide = jnp.concatenate([folded[:, 0:256], value_fold], axis=1)
    wide = jnp.concatenate([wide, jnp.zeros((48, 384), F32)], axis=0).T
    wide = jnp.concatenate([wide[0:320], jnp.where(lanes64 == C, twice_et, gram)], axis=0)
    whi = wide.astype(BF16)
    wqkv[:, 0:128] = whi
    wqkv[:, 128:256] = (wide - whi.astype(F32)).astype(BF16)
    scale_row = qg_ref[...] * kg_ref[...] * (math.log2(math.e) / math.sqrt(HEAD))
    scale_col = jnp.broadcast_to(scale_row, (128, 128)).T[:, 0:1]

    step_row = lax.broadcasted_iota(jnp.int32, (STEPS, 128), 0)
    coeff_even = jnp.sum(jnp.where(step_row == 2 * i, coeff, 0.0), axis=0, keepdims=True)
    coeff_odd = jnp.sum(jnp.where(step_row == 2 * i + 1, coeff, 0.0), axis=0, keepdims=True)

    def send_base():
        await_bytes(nin.at[0:COLS - 1], nr)

        def noise_of(step_pair):
            both = nin[step_pair].astype(F32)
            turned = pltpu.roll(both, C, 1)
            return jnp.where(low_lanes, both, turned), jnp.where(low_lanes, turned, both)

        base = start_dup
        for pair in range(COLS):
            even, odd = noise_of(pair)
            pair_sum = coeff_ref[2 * pair:2 * pair + 1] * even + coeff_ref[2 * pair + 1:2 * pair + 2] * odd
            base = base + jnp.where(pair < i, pair_sum, 0.0)
        own_even, own_odd = noise_of(i)
        after_even = base + coeff_even * own_even
        after_odd = after_even + coeff_odd * own_odd
        basesrc[0] = base
        basesrc[1] = after_even
        basesrc[2] = after_odd
        for n in range(2):
            @pl.when(base_mine[n])
            def _():
                basein[half] = basesrc[n]

            @pl.when(jnp.logical_not(base_mine[n]))
            def _():
                push(basesrc.at[n], basein.at[half], bs.at[n], br.at[half], source_i, base_j[n])

    chunk = rows_of(pos)
    low = low_lanes[0:16]

    def project(lap, n):
        packed = latents[lap, n].T
        zb = jnp.concatenate([packed[0:64], packed[64:128]], axis=1)
        ztr[0:64] = zb
        ztr[128:192] = zb
        cols = slice(n * KBLK, (n + 1) * KBLK)
        out = mm(wqkv[...], ztr[...])
        yq, yk, yv, yg = out[0:128], out[128:256], out[256:320], out[320:384]
        mean_square = (jnp.sum(zb.astype(F32) * yg, axis=0, keepdims=True) + t_square) * (1.0 / D)
        square = jnp.maximum(mean_square, 0.0) + EPS
        aq = lax.rsqrt(jnp.mean(yq * yq, axis=0, keepdims=True) + EPS * square)
        ak = lax.rsqrt(jnp.mean(yk * yk, axis=0, keepdims=True) + EPS * square)
        qbuf[:, cols] = (yq * aq * scale_col).astype(BF16)
        kbuf[cols, :] = (yk * ak).astype(BF16).T
        vbuf[0:C, cols] = (yv * lax.rsqrt(square)).astype(BF16)

    def attend(block, keys, accs):
        here = slice(keys[0] * KBLK, (keys[-1] + 1) * KBLK)
        scores = [
            mm(kbuf[here], qbuf[:, block * KBLK + side * QBLK:block * KBLK + (side + 1) * QBLK]) for side in range(2)]
        parts = [mm(vbuf[:, here], jnp.exp2(score).astype(BF16)) for score in scores]
        return [part if acc is None else acc + part for part, acc in zip(parts, accs)]

    def finish(lap, block, accs):
        outs = [acc[0:C] / acc[C:C + 1] for acc in accs]
        heads[lap, block] = jnp.concatenate(outs, axis=0).astype(BF16).T
        group(lambda n, ti, tj: push(
            heads.at[lap, block, rows_of(n), :], red.at[lap, block, pos], us.at[lap], ur.at[lap, block], ti, tj))

    def reduce_heads(lap, block):
        red[lap, block, pos] = heads[lap, block, chunk, :]
        latent = latents[lap, block, chunk, :]
        total = mm(jnp.concatenate([latent, latent], axis=1), cdiag[...]) + crow[0:1]
        await_bytes(red.at[lap, block, 0:STEPS - 1], ur.at[lap, block])
        for h in range(STEPS):
            total = total + red[lap, block, h].astype(F32)
        return total

    def pack_first(lap, first_part, second_part):
        vpack[lap, 0, 0:16] = jnp.where(low, first_part, pltpu.roll(second_part, C, 1)).astype(BF16)
        vpack[lap, 1, 0:16] = jnp.where(low, pltpu.roll(first_part, C, 1), second_part).astype(BF16)

    def pack_last(lap, part):
        vpack[lap, 0, 16:32] = jnp.where(low, part, 0.0).astype(BF16)
        vpack[lap, 1, 16:32] = jnp.where(low, pltpu.roll(part, C, 1), 0.0).astype(BF16)

    first_i = lax.div(s, 2)

    alone = jnp.logical_and(own_chunk == pos, first_i <= i)

    def to_owners(src, dst, rows, n):
        @pl.when(alone)
        def _():
            dst[s, rows] = src[half, rows]

        def one(k):
            to_i = k // 2
            to_j = first_block + 2 * (k % 2)
            mine = jnp.logical_and(to_i == i, to_j == j)

            @pl.when(jnp.logical_and(to_i >= first_i, jnp.logical_not(mine)))
            def _():
                push(src.at[k % 2, rows], dst.at[s, rows], fs.at[n], fr.at[n], to_i, to_j)
        for k in reversed(range(16)):
            one(k)

    def owners_sent(dst, rows, n):
        for pair in range(COLS):
            for own in range(2):
                @pl.when(jnp.logical_and(first_i == pair, alone == (own == 1)))
                def _():
                    await_bytes(dst.at[0:2 * (COLS - pair) - own, rows], fs.at[n])

    def owner_sums(dst, rows, n):
        for pair in range(COLS):
            for own in range(2):
                @pl.when(jnp.logical_and(i == pair, alone == (own == 1)))
                def _():
                    await_bytes(dst.at[0:2 * pair + 2 - own, rows], fr.at[n])
        even = jnp.zeros((rows.stop - rows.start, 128), F32)
        odd = even
        for k in range(STEPS):
            later = delta_ref[k:k + 1] * dst[k, rows].astype(F32)
            even = even + jnp.where(k <= 2 * i, later, 0.0)
            odd = odd + jnp.where(k == 2 * i + 1, later, 0.0)
        return even, even + odd

    early_rows, late_rows = slice(0, 16), slice(16, 32)
    blocks = range(3)
    velocities = {}
    through = {}
    own_delta = jnp.sum(jnp.where(step_row == s, delta, 0.0), axis=0, keepdims=True)

    def sum_heads(block):
        velocities[block] = reduce_heads(0, block)
        vsrc[block] = velocities[block].astype(BF16)
        gat[block, s] = velocities[block].astype(BF16)

        def send(k):
            to = lax.rem(s + k, STEPS)
            push(vsrc.at[block], gat.at[block, s], gs.at[block], gr.at[block], i, seq_of(to, p))
        for k in sorted(range(1, STEPS), key=lambda k: abs(k - STEPS // 2)):
            send(k)

    def next_latent(block):
        rows = slice(block * 16, (block + 1) * 16)
        await_bytes(gat.at[block, 0:STEPS - 1], gr.at[block])
        before = jnp.zeros((16, 128), F32)
        for n in range(STEPS):
            before = before + jnp.where(n < s, delta_ref[n:n + 1] * gat[block, n].astype(F32), 0.0)
        latent = (jnp.where(low, basein[0, rows], basein[1, rows]) + before).astype(BF16)
        zsend[block] = latent
        latents[1, block, chunk, :] = latent
        group(lambda n, ti, tj: push(
            zsend.at[block], latents.at[1, block, chunk, :], ps.at[block], pr.at[block], ti, tj))
        through[block] = before + own_delta * vsrc[block].astype(F32)

    def send_through():
        first_part, second_part, third_part = through[0], through[1], through[2]
        tsend[0, 0:16] = jnp.where(low, first_part, pltpu.roll(second_part, C, 1))
        tsend[1, 0:16] = jnp.where(low, pltpu.roll(first_part, C, 1), second_part)
        tsend[0, 16:32] = jnp.where(low, third_part, 0.0)
        tsend[1, 16:32] = jnp.where(low, pltpu.roll(third_part, C, 1), 0.0)
        slot = lax.rem(s, 2)
        for n in range(2):
            @pl.when(from_mine[n])
            def _():
                first_sums[slot] = tsend[n]

            @pl.when(jnp.logical_not(from_mine[n]))
            def _():
                push(tsend.at[n], first_sums.at[slot], ts.at[n], tr.at[slot], from_i, from_j[n])

    def await_latents(block):
        await_bytes(latents.at[1, block, 0:15 * 16, :], pr.at[block])

    await_bytes(zp.at[:, 0:128, :], cr)
    for block in blocks:
        project(0, block)
    for block in blocks:
        finish(0, block, attend(block, blocks, (None, None)))
        if block:
            sum_heads(block - 1)
    send_base()
    sum_heads(2)
    for n in range(2):
        @pl.when(jnp.logical_not(from_mine[n]))
        def _():
            await_bytes(basein.at[n], br.at[n])
    next_latent(0)
    next_latent(1)

    await_latents(0)
    project(1, 0)
    next_latent(2)
    send_through()
    await_latents(1)
    project(1, 1)
    early = [attend(block, (0, 1), (None, None)) for block in (0, 1)]
    await_latents(2)
    project(1, 2)
    for block in (0, 1):
        finish(1, block, attend(block, (2,), early[block]))
    finish(1, 2, attend(2, blocks, (None, None)))
    pack_first(1, reduce_heads(1, 0), reduce_heads(1, 1))
    to_owners(vpack.at[1], fin1, early_rows, 1)
    for n in range(2):
        @pl.when(jnp.logical_not(base_mine[n]))
        def _():
            await_bytes(first_sums.at[n], tr.at[n])
    pack_last(1, reduce_heads(1, 2))
    to_owners(vpack.at[1], fin1, late_rows, 2)

    even, odd = (
        jnp.concatenate(parts, axis=0) for parts in zip(owner_sums(fin1, early_rows, 1), owner_sums(fin1, late_rows, 2)))
    change_even = even - first_sums[0]
    change_odd = odd - first_sums[1]

    def unpack(x):
        return jnp.concatenate([x[0:16], pltpu.roll(x[0:16], C, 1), x[16:32]], axis=0)

    row = lax.broadcasted_iota(jnp.int32, (2, 128), 0)
    sum_even = jnp.sum(change_even * change_even, axis=0, keepdims=True)
    sum_odd = jnp.sum(change_odd * change_odd, axis=0, keepdims=True)
    partial = jnp.where(row == 0, sum_even, sum_odd)
    esrc[...] = partial
    ein[j] = partial
    column(lambda tj: push(esrc, ein.at[j], es, er, i, tj))
    for n, total in enumerate((basesrc[1] + unpack(even), basesrc[2] + unpack(odd))):
        out_ref[n] = total[:, 0:C]
    for lap in range(2):
        await_bytes(red.at[lap, :, 0:STEPS - 1], us.at[lap])
    for block in blocks:
        await_bytes(gat.at[block, 0:STEPS - 1], gs.at[block])
        await_bytes(latents.at[1, block, 0:15 * 16, :], ps.at[block])
    for n in range(2):
        @pl.when(jnp.logical_not(from_mine[n]))
        def _():
            await_bytes(tsend.at[n], ts.at[n])
    owners_sent(fin1, early_rows, 1)
    owners_sent(fin1, late_rows, 2)
    @pl.when(sends_start)
    def _():
        await_bytes(wall.at[0:31 * 32, 0:128], ys)

    await_bytes(nin.at[0:COLS - 1], ns)
    await_bytes(zp.at[:, 0:128, :], cs)
    for n in range(2):
        @pl.when(jnp.logical_not(base_mine[n]))
        def _():
            await_bytes(basesrc.at[n], bs.at[n])

    await_bytes(ein.at[0:SEQ - 1], er)
    total = ein[0]
    for n in range(1, SEQ):
        total = total + ein[n]
    total = total * (1.0 / (LEN * C))
    err_ref[0] = jnp.sum(total[0:1] / (coeff_even * coeff_even))
    err_ref[1] = jnp.sum(total[1:2] / (coeff_odd * coeff_odd))

    await_bytes(ein.at[0:SEQ - 1], es)


def per_device(
    start_latent, noise, window_start, w_embed, w_time, norm_gain, w_query, w_key, w_value, query_gain, key_gain, w_out, w_final,
):
    vmem = pl.BlockSpec(memory_space=pltpu.VMEM)
    hbm = pl.BlockSpec(memory_space=pltpu.HBM)
    smem = pl.BlockSpec(memory_space=pltpu.SMEM)
    dma = pltpu.SemaphoreType.DMA
    out, errors = pl.pallas_call(
        kernel,
        out_shape=(
            pltpu.VMEM((2, ROWS, C), F32),
            pltpu.SMEM((2,), F32),
        ),
        in_specs=[smem] + [hbm] * 12,
        out_specs=(vmem, smem),
        scratch_shapes=[
            pltpu.VMEM((ROWS, C), F32),
            pltpu.VMEM((2, ROWS, C), BF16),
            pltpu.VMEM((1, D), F32),
            pltpu.VMEM((1, HEAD), F32),
            pltpu.VMEM((1, HEAD), F32),
            pltpu.VMEM((256, D), BF16),
            pltpu.VMEM((D, 3 * HEAD), BF16),
            pltpu.VMEM((160, D), BF16),
            pltpu.VMEM((224, D), BF16),
            pltpu.VMEM((256, D), BF16),
            pltpu.VMEM((384, 256), BF16),
            pltpu.VMEM((256, 128), BF16),
            pltpu.VMEM((8, 128), F32),
            pltpu.VMEM((STEPS, 128), F32),
            pltpu.VMEM((STEPS, 128), F32),
            pltpu.VMEM((32, 128), BF16),
            pltpu.VMEM((16, 32, 128), BF16),
            pltpu.VMEM((ROWS, 128), BF16),
            pltpu.VMEM((COLS, ROWS, 128), BF16),
            pltpu.VMEM((3, ROWS, 128), F32),
            pltpu.VMEM((2, ROWS, 128), F32),
            pltpu.VMEM((2, 3, QBLK, 128), BF16),
            pltpu.VMEM((2, 3, QBLK, 128), BF16),
            pltpu.VMEM((2, 3, STEPS, 16, 128), BF16),
            pltpu.VMEM((3, 16, 128), BF16),
            pltpu.VMEM((2, 2, 32, 128), BF16),
            pltpu.VMEM((3, STEPS, 16, 128), BF16),
            pltpu.VMEM((3, 16, 128), BF16),
            pltpu.VMEM((STEPS, 32, 128), BF16),
            pltpu.VMEM((2, 32, 128), F32),
            pltpu.VMEM((2, 32, 128), F32),
            pltpu.VMEM((2, 128), F32),
            pltpu.VMEM((SEQ, 2, 128), F32),
            pltpu.VMEM((256, KBLK), BF16),
            pltpu.VMEM((LEN, HEAD), BF16),
            pltpu.VMEM((HEAD, LEN), BF16),
            pltpu.VMEM((C + 16, LEN), BF16),
            dma((5 + 7 * PARTS,)),
            dma, dma, dma, dma, dma, dma, dma((2,)), dma((2,)),
            dma((2,)), dma((2, 3)), dma((3,)), dma((3,)), dma((3,)), dma((3,)), dma((3,)), dma((3,)), dma((2,)), dma((2,)), dma, dma,
        ],
        compiler_params=pltpu.CompilerParams(
            collective_id=0, has_side_effects=True, vmem_limit_bytes=56 * 1024 * 1024),
    )(
        window_start, start_latent, noise, norm_gain.reshape(1, D), query_gain.reshape(1, HEAD), key_gain.reshape(1, HEAD),
        w_embed, w_time, w_final.T, w_query, w_key, w_value, w_out,
    )
    return out, errors


def solution(mesh):
    return jax.shard_map(
        per_device,
        mesh=mesh,
        in_specs=(
            P("seq", None), P("step", "seq", None), P(), P(), P(), P(),
            P(None, "step"), P(None, "step"), P(None, "step"), P(), P(), P("step", None), P(),
        ),
        out_specs=(P("step", "seq", None), P("step")),
        check_vma=False,
    )
```

```python
import math

import jax
import jax.numpy as jnp
from jax import lax
from jax.experimental import pallas as pl
from jax.experimental.pallas import tpu as pltpu
from jax.sharding import PartitionSpec as P

NSCHED = 28
EPS = 1e-06
SHIFT = 3.0
ETA = 0.5
MESH = pl.DeviceIdType.MESH
F32 = jnp.float32
BF16 = jnp.bfloat16

D = 3072
C = 64
HEAD = 128
LEN = 1536
HALF = LEN // 2
STEPS = 16
ROWS = 48
SEQ = 32
COLS = 8
QBLK = 256
KBLK = 512
PARTS = 4
DBLK = D // PARTS


def sigma_of(index):
    fraction = 1.0 - index / NSCHED
    return SHIFT * fraction / (1.0 + (SHIFT - 1.0) * fraction)


def chunk_i(n):
    return 2 * lax.rem(n, 4) + lax.div(n, 8)


def chunk_p(n):
    return lax.rem(lax.div(n, 4), 2)


def seq_of(step, part):
    return 2 * step + lax.rem(step + part, 2)


def chunk_block(n):
    return 4 * lax.rem(n, 8) + lax.div(n, 8)


def split(x):
    hi = x.astype(BF16)
    return hi, (x - hi.astype(F32)).astype(BF16)


def mm(a, b):
    return jnp.dot(a, b, preferred_element_type=F32)


def kernel(
    ws_ref, start_hbm, noise_hbm, gain_hbm, qg_hbm, kg_hbm,
    wembed_hbm, wtime_hbm, wfinal_hbm, wq_hbm, wk_hbm, wv_hbm, wo_hbm,
    out_ref, err_ref,
    start_ref, noise_ref, gain_ref, qg_ref, kg_ref,
    wtime, wall, fold, left, right, wqkv, cdiag, crow,
    delta_ref, coeff_ref,
    zsrc, yin, nsrc, nin, basesrc, basein,
    latents, heads, red, vsrc, vpack, gat, zsend, fin1, tsend, first_sums, esrc, ein,
    ztr, kbuf, qbuf, vbuf,
    wsem, ys, yr, cs, cr, ns, nr, bs, br, us, ur, gs, gr, ps, pr, fs, fr, ts, tr, es, er,
):
    i = lax.axis_index("step")
    j = lax.axis_index("seq")
    x = lax.div(i, 2)
    c = lax.rem(i, 2)
    z = lax.div(j, 4)
    y = lax.rem(j, 4)
    s = lax.div(j, 2)
    p = lax.rem(j + s, 2)
    pos = 4 * (2 * c + p) + x
    own_chunk = 8 * lax.rem(y, 2) + z
    half = lax.div(y, 2)
    source_i = chunk_i(own_chunk)
    source_p = chunk_p(own_chunk)
    first_block = chunk_block(pos)
    low_lanes = lax.broadcasted_iota(jnp.int32, (ROWS, 128), 1) < C

    def rows_of(n):
        return pl.ds(pl.multiple_of(n * 16, 16), 16)

    def push(src, dst, send, recv, to_i, to_j):
        pltpu.make_async_remote_copy(
            src_ref=src, dst_ref=dst, send_sem=send, recv_sem=recv,
            device_id=(to_i, to_j), device_id_type=MESH,
        ).start()

    def await_bytes(like, sem):
        pltpu.make_async_copy(like, like, sem).wait()

    def each(low, high, fn):
        for k in range(low, high):
            fn(k)

    def group(fn):
        def one(k):
            n = lax.rem(pos + k, STEPS)
            fn(n, chunk_i(n), seq_of(s, chunk_p(n)))
        for k in sorted(range(1, STEPS), key=lambda k: -min(k % 4, -k % 4)):
            one(k)

    zp = latents.at[0]

    def column(fn):
        for k in sorted(range(1, SEQ), key=lambda k: abs(k - SEQ // 2)):
            fn(lax.rem(j + k, SEQ))

    barrier = pltpu.get_barrier_semaphore()

    def greet(to_i, to_j):
        pl.semaphore_signal(barrier, inc=1, device_id=(to_i, to_j), device_id_type=MESH)

    group(lambda n, ti, tj: greet(ti, tj))
    column(lambda tj: greet(i, tj))
    base_j = [seq_of(2 * i + n, source_p) for n in range(2)]
    base_mine = [jnp.logical_and(source_i == i, tj == j) for tj in base_j]
    from_j = [first_block + 2 * n for n in range(2)]
    from_i = lax.div(s, 2)
    from_mine = [jnp.logical_and(from_i == i, tj == j) for tj in from_j]
    for n in range(2):
        @pl.when(jnp.logical_not(from_mine[n]))
        def _():
            greet(from_i, from_j[n])

    head = pl.multiple_of(p * HEAD, HEAD)
    widths = [slice(n * DBLK, (n + 1) * DBLK) for n in range(PARTS)]
    pairs = [(start_hbm, start_ref), (noise_hbm, noise_ref), (gain_hbm, gain_ref), (qg_hbm, qg_ref), (kg_hbm, kg_ref)]
    for part in widths:
        pairs += [(wtime_hbm.at[:, part], wtime.at[:, part]), (wembed_hbm.at[:, part], left.at[0:64, part])]
        pairs += [
            (w.at[part, pl.ds(head, HEAD)], wall.at[part, n * HEAD:(n + 1) * HEAD]) for n, w in enumerate((wq_hbm, wk_hbm, wv_hbm))
        ]
        pairs += [
            (wfinal_hbm.at[:, part], right.at[0:64, part]),
            (wo_hbm.at[pl.ds(head, HEAD), part], left.at[96:224, part]),
        ]
    local = [pltpu.make_async_copy(src, dst, wsem.at[n]) for n, (src, dst) in enumerate(pairs)]
    for copy in local:
        copy.start()

    local[0].wait()
    z0 = start_ref[...]
    start_dup = jnp.concatenate([z0, z0], axis=1)
    low = low_lanes[0:16]
    own_half = lax.div(lax.broadcasted_iota(jnp.int32, (16, 128), 1), C) == half
    pieces = [start_dup[0:16], start_dup[16:32], start_dup[32:48]]
    packed_start = jnp.concatenate([
        jnp.where(own_half, pieces[0], pieces[1]), jnp.where(own_half, pieces[2], 0.0)], axis=0).astype(BF16)
    zsrc[...] = packed_start
    sends_start = lax.rem(y, 2) == c

    @pl.when(sends_start)
    def _():
        yin[8 * half + z] = packed_start

    local[1].wait()
    packed_noise = jnp.concatenate([noise_ref[0], noise_ref[1]], axis=1)
    nsrc[...] = packed_noise
    nin[i] = packed_noise

    alone_count = base_mine[0].astype(jnp.int32) + base_mine[1].astype(jnp.int32)
    pl.semaphore_wait(barrier, 15 + 31 + 2 - alone_count)

    @pl.when(sends_start)
    def _():
        column(lambda tj: push(zsrc, yin.at[8 * half + z], ys, yr, i, tj))


    first = ws_ref[0]
    index = (lax.broadcasted_iota(jnp.int32, (STEPS, 128), 0) + first).astype(F32)
    sigma_now = sigma_of(index)
    delta = sigma_of(index + 1.0) - sigma_now
    coeff = ETA * jnp.sqrt(-delta)
    delta_ref[...] = delta
    coeff_ref[...] = coeff
    own = sigma_of((jnp.zeros((STEPS, 128), jnp.int32) + (first + s)).astype(F32))
    lane = lax.broadcasted_iota(jnp.int32, (STEPS, 128), 1).astype(F32)
    angle = 1000.0 * own * jnp.exp(-math.log(10000.0) * lane / 128)
    feats = jnp.concatenate([jnp.cos(angle), jnp.sin(angle)], axis=1)
    feats = (feats / (1.0 + jnp.exp(-feats))).astype(BF16)
    right[192:256] = jnp.zeros((64, D), BF16)
    vbuf[C:C + 16] = jnp.ones((16, LEN), BF16)
    for n in range(2):
        ztr[128 * n + 64:128 * n + 128] = jnp.where(
            lax.broadcasted_iota(jnp.int32, (64, KBLK), 0) == 0, 1.0, 0.0).astype(BF16)

    each(1, COLS, lambda k: push(nsrc, nin.at[i], ns, nr, lax.rem(i + k, COLS), j))

    for copy in local[2:5]:
        copy.wait()
    sums = [0.0] * 4

    def fold_part(n):
        part = widths[n]
        for copy in local[5 + 7 * n:7 + 7 * n]:
            copy.wait()
        temb = mm(feats, wtime[:, part])
        embed = left[0:64, part]
        emb = embed.astype(F32)
        gain = gain_ref[:, part]
        for m, piece in enumerate(split(jnp.concatenate([emb * gain, temb * gain], axis=0))):
            fold[m * 80:(m + 1) * 80, part] = piece
        for m, piece in enumerate(split(temb)):
            left[64 + 16 * m:80 + 16 * m, part] = piece
        t_row = temb[0:1]
        right[128:192, part] = embed
        for copy in local[7 + 7 * n:12 + 7 * n]:
            copy.wait()
        right[64:128, part] = right[0:64, part]
        terms = (
            jnp.sum(emb * t_row, axis=1, keepdims=True),
            jnp.sum(t_row * t_row, axis=1, keepdims=True),
            mm(fold[:, part], wall[part]),
            lax.dot_general(left[:, part], right[:, part], (((1,), (1,)), ((), ())), preferred_element_type=F32),
        )
        for m, term in enumerate(terms):
            sums[m] = sums[m] + term

    each(0, PARTS - 1, fold_part)

    @pl.when(sends_start)
    def _():
        await_bytes(yin.at[0:15], yr)

    @pl.when(jnp.logical_not(sends_start))
    def _():
        await_bytes(yin, yr)

    for n in range(8):
        below, above = yin[n].astype(F32), yin[8 + n].astype(F32)
        there = rows_of(8 * c + n)
        zp[0, there, :] = jnp.where(low, below[0:16], above[0:16]).astype(BF16)
        zp[1, there, :] = pltpu.roll(jnp.where(low, above[0:16], below[0:16]), C, 1).astype(BF16)
        zp[2, there, :] = jnp.where(low, below[16:32], above[16:32]).astype(BF16)
    core_rows = pl.ds(pl.multiple_of(128 * c, 128), 128)
    push(zp.at[:, core_rows, :], zp.at[:, core_rows, :], cs, cr, i + 1 - 2 * c, j)

    fold_part(PARTS - 1)
    twice_et, t_square, folded, both = sums
    twice_et = 2.0 * twice_et
    folded = folded[0:80] + folded[80:160]
    cdup = both[0:64, 0:128]
    gram = both[0:64, 128:256]
    mout = both[96:224, 0:128]
    lanes64 = lax.broadcasted_iota(jnp.int32, (64, 128), 1)
    diag = jnp.concatenate([jnp.where(lanes64 < C, cdup, 0.0), jnp.where(lanes64 < C, 0.0, cdup)], axis=0)
    for n, part in enumerate(split(diag)):
        cdiag[n * 128:(n + 1) * 128] = part
    crow[...] = both[64:72, 0:128] + both[80:88, 0:128]

    value_fold = jnp.dot(folded[:, 256:384], mout, precision=lax.Precision.HIGHEST, preferred_element_type=F32)
    wide = jnp.concatenate([folded[:, 0:256], value_fold], axis=1)
    wide = jnp.concatenate([wide, jnp.zeros((48, 384), F32)], axis=0).T
    wide = jnp.concatenate([wide[0:320], jnp.where(lanes64 == C, twice_et, gram)], axis=0)
    whi = wide.astype(BF16)
    wqkv[:, 0:128] = whi
    wqkv[:, 128:256] = (wide - whi.astype(F32)).astype(BF16)
    scale_row = qg_ref[...] * kg_ref[...] * (math.log2(math.e) / math.sqrt(HEAD))
    scale_col = jnp.broadcast_to(scale_row, (128, 128)).T[:, 0:1]

    step_row = lax.broadcasted_iota(jnp.int32, (STEPS, 128), 0)
    coeff_even = jnp.sum(jnp.where(step_row == 2 * i, coeff, 0.0), axis=0, keepdims=True)
    coeff_odd = jnp.sum(jnp.where(step_row == 2 * i + 1, coeff, 0.0), axis=0, keepdims=True)

    def send_base():
        await_bytes(nin.at[0:COLS - 1], nr)

        def noise_of(step_pair):
            both = nin[step_pair].astype(F32)
            turned = pltpu.roll(both, C, 1)
            return jnp.where(low_lanes, both, turned), jnp.where(low_lanes, turned, both)

        base = start_dup
        for pair in range(COLS):
            even, odd = noise_of(pair)
            pair_sum = coeff_ref[2 * pair:2 * pair + 1] * even + coeff_ref[2 * pair + 1:2 * pair + 2] * odd
            base = base + jnp.where(pair < i, pair_sum, 0.0)
        own_even, own_odd = noise_of(i)
        after_even = base + coeff_even * own_even
        after_odd = after_even + coeff_odd * own_odd
        basesrc[0] = base
        basesrc[1] = after_even
        basesrc[2] = after_odd
        for n in range(2):
            @pl.when(base_mine[n])
            def _():
                basein[half] = basesrc[n]

            @pl.when(jnp.logical_not(base_mine[n]))
            def _():
                push(basesrc.at[n], basein.at[half], bs.at[n], br.at[half], source_i, base_j[n])

    chunk = rows_of(pos)
    low = low_lanes[0:16]

    def project(lap, n):
        packed = latents[lap, n].T
        zb = jnp.concatenate([packed[0:64], packed[64:128]], axis=1)
        ztr[0:64] = zb
        ztr[128:192] = zb
        cols = slice(n * KBLK, (n + 1) * KBLK)
        out = mm(wqkv[...], ztr[...])
        yq, yk, yv, yg = out[0:128], out[128:256], out[256:320], out[320:384]
        mean_square = (jnp.sum(zb.astype(F32) * yg, axis=0, keepdims=True) + t_square) * (1.0 / D)
        square = jnp.maximum(mean_square, 0.0) + EPS
        aq = lax.rsqrt(jnp.mean(yq * yq, axis=0, keepdims=True) + EPS * square)
        ak = lax.rsqrt(jnp.mean(yk * yk, axis=0, keepdims=True) + EPS * square)
        qbuf[:, cols] = (yq * aq * scale_col).astype(BF16)
        kbuf[cols, :] = (yk * ak).astype(BF16).T
        vbuf[0:C, cols] = (yv * lax.rsqrt(square)).astype(BF16)

    def attend(block, keys, accs):
        here = slice(keys[0] * KBLK, (keys[-1] + 1) * KBLK)
        scores = [
            mm(kbuf[here], qbuf[:, block * KBLK + side * QBLK:block * KBLK + (side + 1) * QBLK]) for side in range(2)]
        parts = [mm(vbuf[:, here], jnp.exp2(score).astype(BF16)) for score in scores]
        return [part if acc is None else acc + part for part, acc in zip(parts, accs)]

    def finish(lap, block, accs):
        outs = [acc[0:C] / acc[C:C + 1] for acc in accs]
        heads[lap, block] = jnp.concatenate(outs, axis=0).astype(BF16).T
        group(lambda n, ti, tj: push(
            heads.at[lap, block, rows_of(n), :], red.at[lap, block, pos], us.at[lap], ur.at[lap, block], ti, tj))

    def reduce_heads(lap, block):
        red[lap, block, pos] = heads[lap, block, chunk, :]
        latent = latents[lap, block, chunk, :]
        total = mm(jnp.concatenate([latent, latent], axis=1), cdiag[...]) + crow[0:1]
        await_bytes(red.at[lap, block, 0:STEPS - 1], ur.at[lap, block])
        for h in range(STEPS):
            total = total + red[lap, block, h].astype(F32)
        return total

    def pack_first(lap, first_part, second_part):
        vpack[lap, 0, 0:16] = jnp.where(low, first_part, pltpu.roll(second_part, C, 1)).astype(BF16)
        vpack[lap, 1, 0:16] = jnp.where(low, pltpu.roll(first_part, C, 1), second_part).astype(BF16)

    def pack_last(lap, part):
        vpack[lap, 0, 16:32] = jnp.where(low, part, 0.0).astype(BF16)
        vpack[lap, 1, 16:32] = jnp.where(low, pltpu.roll(part, C, 1), 0.0).astype(BF16)

    first_i = lax.div(s, 2)

    alone = jnp.logical_and(own_chunk == pos, first_i <= i)

    def to_owners(src, dst, rows, n):
        @pl.when(alone)
        def _():
            dst[s, rows] = src[half, rows]

        def one(k):
            to_i = k // 2
            to_j = first_block + 2 * (k % 2)
            mine = jnp.logical_and(to_i == i, to_j == j)

            @pl.when(jnp.logical_and(to_i >= first_i, jnp.logical_not(mine)))
            def _():
                push(src.at[k % 2, rows], dst.at[s, rows], fs.at[n], fr.at[n], to_i, to_j)
        for k in reversed(range(16)):
            one(k)

    def owners_sent(dst, rows, n):
        for pair in range(COLS):
            for own in range(2):
                @pl.when(jnp.logical_and(first_i == pair, alone == (own == 1)))
                def _():
                    await_bytes(dst.at[0:2 * (COLS - pair) - own, rows], fs.at[n])

    def owner_sums(dst, rows, n):
        for pair in range(COLS):
            for own in range(2):
                @pl.when(jnp.logical_and(i == pair, alone == (own == 1)))
                def _():
                    await_bytes(dst.at[0:2 * pair + 2 - own, rows], fr.at[n])
        even = jnp.zeros((rows.stop - rows.start, 128), F32)
        odd = even
        for k in range(STEPS):
            later = delta_ref[k:k + 1] * dst[k, rows].astype(F32)
            even = even + jnp.where(k <= 2 * i, later, 0.0)
            odd = odd + jnp.where(k == 2 * i + 1, later, 0.0)
        return even, even + odd

    early_rows, late_rows = slice(0, 16), slice(16, 32)
    blocks = range(3)
    velocities = {}
    through = {}
    own_delta = jnp.sum(jnp.where(step_row == s, delta, 0.0), axis=0, keepdims=True)

    def sum_heads(block):
        velocities[block] = reduce_heads(0, block)
        vsrc[block] = velocities[block].astype(BF16)
        gat[block, s] = velocities[block].astype(BF16)

        def send(k):
            to = lax.rem(s + k, STEPS)
            push(vsrc.at[block], gat.at[block, s], gs.at[block], gr.at[block], i, seq_of(to, p))
        for k in sorted(range(1, STEPS), key=lambda k: abs(k - STEPS // 2)):
            send(k)

    def next_latent(block):
        rows = slice(block * 16, (block + 1) * 16)
        await_bytes(gat.at[block, 0:STEPS - 1], gr.at[block])
        before = jnp.zeros((16, 128), F32)
        for n in range(STEPS):
            before = before + jnp.where(n < s, delta_ref[n:n + 1] * gat[block, n].astype(F32), 0.0)
        latent = (jnp.where(low, basein[0, rows], basein[1, rows]) + before).astype(BF16)
        zsend[block] = latent
        latents[1, block, chunk, :] = latent
        group(lambda n, ti, tj: push(
            zsend.at[block], latents.at[1, block, chunk, :], ps.at[block], pr.at[block], ti, tj))
        through[block] = before + own_delta * vsrc[block].astype(F32)

    def send_through():
        first_part, second_part, third_part = through[0], through[1], through[2]
        tsend[0, 0:16] = jnp.where(low, first_part, pltpu.roll(second_part, C, 1))
        tsend[1, 0:16] = jnp.where(low, pltpu.roll(first_part, C, 1), second_part)
        tsend[0, 16:32] = jnp.where(low, third_part, 0.0)
        tsend[1, 16:32] = jnp.where(low, pltpu.roll(third_part, C, 1), 0.0)
        slot = lax.rem(s, 2)
        for n in range(2):
            @pl.when(from_mine[n])
            def _():
                first_sums[slot] = tsend[n]

            @pl.when(jnp.logical_not(from_mine[n]))
            def _():
                push(tsend.at[n], first_sums.at[slot], ts.at[n], tr.at[slot], from_i, from_j[n])

    def await_latents(block):
        await_bytes(latents.at[1, block, 0:15 * 16, :], pr.at[block])

    send_base()
    await_bytes(zp.at[:, 0:128, :], cr)
    for block in blocks:
        project(0, block)
    for block in blocks:
        finish(0, block, attend(block, blocks, (None, None)))
        if block:
            sum_heads(block - 1)
    sum_heads(2)
    for n in range(2):
        @pl.when(jnp.logical_not(from_mine[n]))
        def _():
            await_bytes(basein.at[n], br.at[n])
    next_latent(0)
    next_latent(1)

    await_latents(0)
    project(1, 0)
    next_latent(2)
    send_through()
    await_latents(1)
    project(1, 1)
    early = [attend(block, (0, 1), (None, None)) for block in (0, 1)]
    await_latents(2)
    project(1, 2)
    for block in (0, 1):
        finish(1, block, attend(block, (2,), early[block]))
    finish(1, 2, attend(2, blocks, (None, None)))
    pack_first(1, reduce_heads(1, 0), reduce_heads(1, 1))
    to_owners(vpack.at[1], fin1, early_rows, 1)
    for n in range(2):
        @pl.when(jnp.logical_not(base_mine[n]))
        def _():
            await_bytes(first_sums.at[n], tr.at[n])
    pack_last(1, reduce_heads(1, 2))
    to_owners(vpack.at[1], fin1, late_rows, 2)

    even, odd = (
        jnp.concatenate(parts, axis=0) for parts in zip(owner_sums(fin1, early_rows, 1), owner_sums(fin1, late_rows, 2)))
    change_even = even - first_sums[0]
    change_odd = odd - first_sums[1]

    def unpack(x):
        return jnp.concatenate([x[0:16], pltpu.roll(x[0:16], C, 1), x[16:32]], axis=0)

    row = lax.broadcasted_iota(jnp.int32, (2, 128), 0)
    sum_even = jnp.sum(change_even * change_even, axis=0, keepdims=True)
    sum_odd = jnp.sum(change_odd * change_odd, axis=0, keepdims=True)
    partial = jnp.where(row == 0, sum_even, sum_odd)
    esrc[...] = partial
    ein[j] = partial
    column(lambda tj: push(esrc, ein.at[j], es, er, i, tj))
    for n, total in enumerate((basesrc[1] + unpack(even), basesrc[2] + unpack(odd))):
        out_ref[n] = total[:, 0:C]
    for lap in range(2):
        await_bytes(red.at[lap, :, 0:STEPS - 1], us.at[lap])
    for block in blocks:
        await_bytes(gat.at[block, 0:STEPS - 1], gs.at[block])
        await_bytes(latents.at[1, block, 0:15 * 16, :], ps.at[block])
    for n in range(2):
        @pl.when(jnp.logical_not(from_mine[n]))
        def _():
            await_bytes(tsend.at[n], ts.at[n])
    owners_sent(fin1, early_rows, 1)
    owners_sent(fin1, late_rows, 2)
    @pl.when(sends_start)
    def _():
        await_bytes(wall.at[0:31 * 32, 0:128], ys)

    await_bytes(nin.at[0:COLS - 1], ns)
    await_bytes(zp.at[:, 0:128, :], cs)
    for n in range(2):
        @pl.when(jnp.logical_not(base_mine[n]))
        def _():
            await_bytes(basesrc.at[n], bs.at[n])

    await_bytes(ein.at[0:SEQ - 1], er)
    total = ein[0]
    for n in range(1, SEQ):
        total = total + ein[n]
    total = total * (1.0 / (LEN * C))
    err_ref[0] = jnp.sum(total[0:1] / (coeff_even * coeff_even))
    err_ref[1] = jnp.sum(total[1:2] / (coeff_odd * coeff_odd))

    await_bytes(ein.at[0:SEQ - 1], es)


def per_device(
    start_latent, noise, window_start, w_embed, w_time, norm_gain, w_query, w_key, w_value, query_gain, key_gain, w_out, w_final,
):
    vmem = pl.BlockSpec(memory_space=pltpu.VMEM)
    hbm = pl.BlockSpec(memory_space=pltpu.HBM)
    smem = pl.BlockSpec(memory_space=pltpu.SMEM)
    dma = pltpu.SemaphoreType.DMA
    out, errors = pl.pallas_call(
        kernel,
        out_shape=(
            pltpu.VMEM((2, ROWS, C), F32),
            pltpu.SMEM((2,), F32),
        ),
        in_specs=[smem] + [hbm] * 12,
        out_specs=(vmem, smem),
        scratch_shapes=[
            pltpu.VMEM((ROWS, C), F32),
            pltpu.VMEM((2, ROWS, C), BF16),
            pltpu.VMEM((1, D), F32),
            pltpu.VMEM((1, HEAD), F32),
            pltpu.VMEM((1, HEAD), F32),
            pltpu.VMEM((256, D), BF16),
            pltpu.VMEM((D, 3 * HEAD), BF16),
            pltpu.VMEM((160, D), BF16),
            pltpu.VMEM((224, D), BF16),
            pltpu.VMEM((256, D), BF16),
            pltpu.VMEM((384, 256), BF16),
            pltpu.VMEM((256, 128), BF16),
            pltpu.VMEM((8, 128), F32),
            pltpu.VMEM((STEPS, 128), F32),
            pltpu.VMEM((STEPS, 128), F32),
            pltpu.VMEM((32, 128), BF16),
            pltpu.VMEM((16, 32, 128), BF16),
            pltpu.VMEM((ROWS, 128), BF16),
            pltpu.VMEM((COLS, ROWS, 128), BF16),
            pltpu.VMEM((3, ROWS, 128), F32),
            pltpu.VMEM((2, ROWS, 128), F32),
            pltpu.VMEM((2, 3, QBLK, 128), BF16),
            pltpu.VMEM((2, 3, QBLK, 128), BF16),
            pltpu.VMEM((2, 3, STEPS, 16, 128), BF16),
            pltpu.VMEM((3, 16, 128), BF16),
            pltpu.VMEM((2, 2, 32, 128), BF16),
            pltpu.VMEM((3, STEPS, 16, 128), BF16),
            pltpu.VMEM((3, 16, 128), BF16),
            pltpu.VMEM((STEPS, 32, 128), BF16),
            pltpu.VMEM((2, 32, 128), F32),
            pltpu.VMEM((2, 32, 128), F32),
            pltpu.VMEM((2, 128), F32),
            pltpu.VMEM((SEQ, 2, 128), F32),
            pltpu.VMEM((256, KBLK), BF16),
            pltpu.VMEM((LEN, HEAD), BF16),
            pltpu.VMEM((HEAD, LEN), BF16),
            pltpu.VMEM((C + 16, LEN), BF16),
            dma((5 + 7 * PARTS,)),
            dma, dma, dma, dma, dma, dma, dma((2,)), dma((2,)),
            dma((2,)), dma((2, 3)), dma((3,)), dma((3,)), dma((3,)), dma((3,)), dma((3,)), dma((3,)), dma((2,)), dma((2,)), dma, dma,
        ],
        compiler_params=pltpu.CompilerParams(
            collective_id=0, has_side_effects=True, vmem_limit_bytes=56 * 1024 * 1024),
    )(
        window_start, start_latent, noise, norm_gain.reshape(1, D), query_gain.reshape(1, HEAD), key_gain.reshape(1, HEAD),
        w_embed, w_time, w_final.T, w_query, w_key, w_value, w_out,
    )
    return out, errors


def solution(mesh):
    return jax.shard_map(
        per_device,
        mesh=mesh,
        in_specs=(
            P("seq", None), P("step", "seq", None), P(), P(), P(), P(),
            P(None, "step"), P(None, "step"), P(None, "step"), P(), P(), P("step", None), P(),
        ),
        out_specs=(P("step", "seq", None), P("step")),
        check_vma=False,
    )
```

```python
import math

import jax
import jax.numpy as jnp
from jax import lax
from jax.experimental import pallas as pl
from jax.experimental.pallas import tpu as pltpu
from jax.sharding import PartitionSpec as P

NSCHED = 28
EPS = 1e-06
SHIFT = 3.0
ETA = 0.5
MESH = pl.DeviceIdType.MESH
F32 = jnp.float32
BF16 = jnp.bfloat16

D = 3072
C = 64
HEAD = 128
LEN = 1536
HALF = LEN // 2
STEPS = 16
ROWS = 48
SEQ = 32
COLS = 8
QBLK = 256
KBLK = 512
PARTS = 4
DBLK = D // PARTS


def sigma_of(index):
    fraction = 1.0 - index / NSCHED
    return SHIFT * fraction / (1.0 + (SHIFT - 1.0) * fraction)


def chunk_i(n):
    return 2 * lax.rem(n, 4) + lax.div(n, 8)


def chunk_p(n):
    return lax.rem(lax.div(n, 4), 2)


def seq_of(step, part):
    return 2 * step + lax.rem(step + part, 2)


def chunk_block(n):
    return 4 * lax.rem(n, 8) + lax.div(n, 8)


def split(x):
    hi = x.astype(BF16)
    return hi, (x - hi.astype(F32)).astype(BF16)


def mm(a, b):
    return jnp.dot(a, b, preferred_element_type=F32)


def kernel(
    ws_ref, start_hbm, noise_hbm, gain_hbm, qg_hbm, kg_hbm,
    wembed_hbm, wtime_hbm, wfinal_hbm, wq_hbm, wk_hbm, wv_hbm, wo_hbm,
    out_ref, err_ref,
    start_ref, noise_ref, gain_ref, qg_ref, kg_ref,
    wtime, wall, fold, left, right, wqkv, cdiag, crow,
    delta_ref, coeff_ref,
    zsrc, yin, nsrc, nin, basesrc, basein,
    latents, heads, red, vsrc, vpack, gat, zsend, fin1, tsend, first_sums, esrc, ein,
    ztr, kbuf, qbuf, vbuf,
    wsem, ys, yr, cs, cr, ns, nr, bs, br, us, ur, gs, gr, ps, pr, fs, fr, ts, tr, es, er,
):
    i = lax.axis_index("step")
    j = lax.axis_index("seq")
    x = lax.div(i, 2)
    c = lax.rem(i, 2)
    z = lax.div(j, 4)
    y = lax.rem(j, 4)
    s = lax.div(j, 2)
    p = lax.rem(j + s, 2)
    pos = 4 * (2 * c + p) + x
    own_chunk = 8 * lax.rem(y, 2) + z
    half = lax.div(y, 2)
    source_i = chunk_i(own_chunk)
    source_p = chunk_p(own_chunk)
    first_block = chunk_block(pos)
    low_lanes = lax.broadcasted_iota(jnp.int32, (ROWS, 128), 1) < C

    def rows_of(n):
        return pl.ds(pl.multiple_of(n * 16, 16), 16)

    def push(src, dst, send, recv, to_i, to_j):
        pltpu.make_async_remote_copy(
            src_ref=src, dst_ref=dst, send_sem=send, recv_sem=recv,
            device_id=(to_i, to_j), device_id_type=MESH,
        ).start()

    def await_bytes(like, sem):
        pltpu.make_async_copy(like, like, sem).wait()

    def each(low, high, fn):
        for k in range(low, high):
            fn(k)

    def group(fn):
        def one(k):
            n = lax.rem(pos + k, STEPS)
            fn(n, chunk_i(n), seq_of(s, chunk_p(n)))
        for k in sorted(range(1, STEPS), key=lambda k: -min(k % 4, -k % 4)):
            one(k)

    zp = latents.at[0]

    def column(fn):
        for k in sorted(range(1, SEQ), key=lambda k: abs(k - SEQ // 2)):
            fn(lax.rem(j + k, SEQ))

    barrier = pltpu.get_barrier_semaphore()

    def greet(to_i, to_j):
        pl.semaphore_signal(barrier, inc=1, device_id=(to_i, to_j), device_id_type=MESH)

    group(lambda n, ti, tj: greet(ti, tj))
    column(lambda tj: greet(i, tj))
    base_j = [seq_of(2 * i + n, source_p) for n in range(2)]
    base_mine = [jnp.logical_and(source_i == i, tj == j) for tj in base_j]
    from_j = [first_block + 2 * n for n in range(2)]
    from_i = lax.div(s, 2)
    from_mine = [jnp.logical_and(from_i == i, tj == j) for tj in from_j]
    for n in range(2):
        @pl.when(jnp.logical_not(from_mine[n]))
        def _():
            greet(from_i, from_j[n])

    head = pl.multiple_of(p * HEAD, HEAD)
    widths = [slice(n * DBLK, (n + 1) * DBLK) for n in range(PARTS)]
    pairs = [(start_hbm, start_ref), (noise_hbm, noise_ref), (gain_hbm, gain_ref), (qg_hbm, qg_ref), (kg_hbm, kg_ref)]
    for part in widths:
        pairs += [(wtime_hbm.at[:, part], wtime.at[:, part]), (wembed_hbm.at[:, part], left.at[0:64, part])]
        pairs += [
            (w.at[part, pl.ds(head, HEAD)], wall.at[part, n * HEAD:(n + 1) * HEAD]) for n, w in enumerate((wq_hbm, wk_hbm, wv_hbm))
        ]
        pairs += [
            (wfinal_hbm.at[:, part], right.at[0:64, part]),
            (wo_hbm.at[pl.ds(head, HEAD), part], left.at[96:224, part]),
        ]
    local = [pltpu.make_async_copy(src, dst, wsem.at[n]) for n, (src, dst) in enumerate(pairs)]
    for copy in local:
        copy.start()

    local[0].wait()
    z0 = start_ref[...]
    start_dup = jnp.concatenate([z0, z0], axis=1)
    low = low_lanes[0:16]
    own_half = lax.div(lax.broadcasted_iota(jnp.int32, (16, 128), 1), C) == half
    pieces = [start_dup[0:16], start_dup[16:32], start_dup[32:48]]
    packed_start = jnp.concatenate([
        jnp.where(own_half, pieces[0], pieces[1]), jnp.where(own_half, pieces[2], 0.0)], axis=0).astype(BF16)
    zsrc[...] = packed_start
    sends_start = lax.rem(y, 2) == c

    @pl.when(sends_start)
    def _():
        yin[8 * half + z] = packed_start

    local[1].wait()
    packed_noise = jnp.concatenate([noise_ref[0], noise_ref[1]], axis=1)
    nsrc[...] = packed_noise
    nin[i] = packed_noise

    alone_count = base_mine[0].astype(jnp.int32) + base_mine[1].astype(jnp.int32)
    pl.semaphore_wait(barrier, 15 + 31 + 2 - alone_count)

    @pl.when(sends_start)
    def _():
        column(lambda tj: push(zsrc, yin.at[8 * half + z], ys, yr, i, tj))


    first = ws_ref[0]
    index = (lax.broadcasted_iota(jnp.int32, (STEPS, 128), 0) + first).astype(F32)
    sigma_now = sigma_of(index)
    delta = sigma_of(index + 1.0) - sigma_now
    coeff = ETA * jnp.sqrt(-delta)
    delta_ref[...] = delta
    coeff_ref[...] = coeff
    own = sigma_of((jnp.zeros((STEPS, 128), jnp.int32) + (first + s)).astype(F32))
    lane = lax.broadcasted_iota(jnp.int32, (STEPS, 128), 1).astype(F32)
    angle = 1000.0 * own * jnp.exp(-math.log(10000.0) * lane / 128)
    feats = jnp.concatenate([jnp.cos(angle), jnp.sin(angle)], axis=1)
    feats = (feats / (1.0 + jnp.exp(-feats))).astype(BF16)
    right[192:256] = jnp.zeros((64, D), BF16)
    vbuf[C:C + 16] = jnp.ones((16, LEN), BF16)
    for n in range(2):
        ztr[128 * n + 64:128 * n + 128] = jnp.where(
            lax.broadcasted_iota(jnp.int32, (64, KBLK), 0) == 0, 1.0, 0.0).astype(BF16)

    each(1, COLS, lambda k: push(nsrc, nin.at[i], ns, nr, lax.rem(i + k, COLS), j))

    for copy in local[2:5]:
        copy.wait()
    sums = [0.0] * 4

    def fold_part(n):
        part = widths[n]
        for copy in local[5 + 7 * n:7 + 7 * n]:
            copy.wait()
        temb = mm(feats, wtime[:, part])
        embed = left[0:64, part]
        emb = embed.astype(F32)
        gain = gain_ref[:, part]
        for m, piece in enumerate(split(jnp.concatenate([emb * gain, temb * gain], axis=0))):
            fold[m * 80:(m + 1) * 80, part] = piece
        for m, piece in enumerate(split(temb)):
            left[64 + 16 * m:80 + 16 * m, part] = piece
        t_row = temb[0:1]
        right[128:192, part] = embed
        for copy in local[7 + 7 * n:12 + 7 * n]:
            copy.wait()
        right[64:128, part] = right[0:64, part]
        terms = (
            jnp.sum(emb * t_row, axis=1, keepdims=True),
            jnp.sum(t_row * t_row, axis=1, keepdims=True),
            mm(fold[:, part], wall[part]),
            lax.dot_general(left[:, part], right[:, part], (((1,), (1,)), ((), ())), preferred_element_type=F32),
        )
        for m, term in enumerate(terms):
            sums[m] = sums[m] + term

    each(0, PARTS - 1, fold_part)

    @pl.when(sends_start)
    def _():
        await_bytes(yin.at[0:15], yr)

    @pl.when(jnp.logical_not(sends_start))
    def _():
        await_bytes(yin, yr)

    for n in range(8):
        below, above = yin[n].astype(F32), yin[8 + n].astype(F32)
        there = rows_of(8 * c + n)
        zp[0, there, :] = jnp.where(low, below[0:16], above[0:16]).astype(BF16)
        zp[1, there, :] = pltpu.roll(jnp.where(low, above[0:16], below[0:16]), C, 1).astype(BF16)
        zp[2, there, :] = jnp.where(low, below[16:32], above[16:32]).astype(BF16)
    core_rows = pl.ds(pl.multiple_of(128 * c, 128), 128)
    push(zp.at[:, core_rows, :], zp.at[:, core_rows, :], cs, cr, i + 1 - 2 * c, j)

    fold_part(PARTS - 1)
    twice_et, t_square, folded, both = sums
    twice_et = 2.0 * twice_et
    folded = folded[0:80] + folded[80:160]
    cdup = both[0:64, 0:128]
    gram = both[0:64, 128:256]
    mout = both[96:224, 0:128]
    lanes64 = lax.broadcasted_iota(jnp.int32, (64, 128), 1)
    diag = jnp.concatenate([jnp.where(lanes64 < C, cdup, 0.0), jnp.where(lanes64 < C, 0.0, cdup)], axis=0)
    for n, part in enumerate(split(diag)):
        cdiag[n * 128:(n + 1) * 128] = part
    crow[...] = both[64:72, 0:128] + both[80:88, 0:128]

    value_fold = jnp.dot(folded[:, 256:384], mout, precision=lax.Precision.HIGHEST, preferred_element_type=F32)
    wide = jnp.concatenate([folded[:, 0:256], value_fold], axis=1)
    wide = jnp.concatenate([wide, jnp.zeros((48, 384), F32)], axis=0).T
    wide = jnp.concatenate([wide[0:320], jnp.where(lanes64 == C, twice_et, gram)], axis=0)
    whi = wide.astype(BF16)
    wqkv[:, 0:128] = whi
    wqkv[:, 128:256] = (wide - whi.astype(F32)).astype(BF16)
    scale_row = qg_ref[...] * kg_ref[...] * (math.log2(math.e) / math.sqrt(HEAD))
    scale_col = jnp.broadcast_to(scale_row, (128, 128)).T[:, 0:1]

    step_row = lax.broadcasted_iota(jnp.int32, (STEPS, 128), 0)
    coeff_even = jnp.sum(jnp.where(step_row == 2 * i, coeff, 0.0), axis=0, keepdims=True)
    coeff_odd = jnp.sum(jnp.where(step_row == 2 * i + 1, coeff, 0.0), axis=0, keepdims=True)

    def send_base():
        await_bytes(nin.at[0:COLS - 1], nr)

        def noise_of(step_pair):
            both = nin[step_pair].astype(F32)
            turned = pltpu.roll(both, C, 1)
            return jnp.where(low_lanes, both, turned), jnp.where(low_lanes, turned, both)

        base = start_dup
        for pair in range(COLS):
            even, odd = noise_of(pair)
            pair_sum = coeff_ref[2 * pair:2 * pair + 1] * even + coeff_ref[2 * pair + 1:2 * pair + 2] * odd
            base = base + jnp.where(pair < i, pair_sum, 0.0)
        own_even, own_odd = noise_of(i)
        after_even = base + coeff_even * own_even
        after_odd = after_even + coeff_odd * own_odd
        basesrc[0] = base
        basesrc[1] = after_even
        basesrc[2] = after_odd
        for n in range(2):
            @pl.when(base_mine[n])
            def _():
                basein[half] = basesrc[n]

            @pl.when(jnp.logical_not(base_mine[n]))
            def _():
                push(basesrc.at[n], basein.at[half], bs.at[n], br.at[half], source_i, base_j[n])

    chunk = rows_of(pos)
    low = low_lanes[0:16]

    def project(lap, n):
        packed = latents[lap, n].T
        zb = jnp.concatenate([packed[0:64], packed[64:128]], axis=1)
        ztr[0:64] = zb
        ztr[128:192] = zb
        cols = slice(n * KBLK, (n + 1) * KBLK)
        out = mm(wqkv[...], ztr[...])
        yq, yk, yv, yg = out[0:128], out[128:256], out[256:320], out[320:384]
        mean_square = (jnp.sum(zb.astype(F32) * yg, axis=0, keepdims=True) + t_square) * (1.0 / D)
        square = jnp.maximum(mean_square, 0.0) + EPS
        aq = lax.rsqrt(jnp.mean(yq * yq, axis=0, keepdims=True) + EPS * square)
        ak = lax.rsqrt(jnp.mean(yk * yk, axis=0, keepdims=True) + EPS * square)
        qbuf[:, cols] = (yq * aq * scale_col).astype(BF16)
        kbuf[cols, :] = (yk * ak).astype(BF16).T
        vbuf[0:C, cols] = (yv * lax.rsqrt(square)).astype(BF16)

    def attend(block, keys, accs):
        here = slice(keys[0] * KBLK, (keys[-1] + 1) * KBLK)
        scores = [
            mm(kbuf[here], qbuf[:, block * KBLK + side * QBLK:block * KBLK + (side + 1) * QBLK]) for side in range(2)]
        parts = [mm(vbuf[:, here], jnp.exp2(score).astype(BF16)) for score in scores]
        return [part if acc is None else acc + part for part, acc in zip(parts, accs)]

    def finish(lap, block, accs):
        outs = [acc[0:C] / acc[C:C + 1] for acc in accs]
        heads[lap, block] = jnp.concatenate(outs, axis=0).astype(BF16).T
        group(lambda n, ti, tj: push(
            heads.at[lap, block, rows_of(n), :], red.at[lap, block, pos], us.at[lap], ur.at[lap, block], ti, tj))

    def reduce_heads(lap, block):
        red[lap, block, pos] = heads[lap, block, chunk, :]
        latent = latents[lap, block, chunk, :]
        total = mm(jnp.concatenate([latent, latent], axis=1), cdiag[...]) + crow[0:1]
        await_bytes(red.at[lap, block, 0:STEPS - 1], ur.at[lap, block])
        for h in range(STEPS):
            total = total + red[lap, block, h].astype(F32)
        return total

    def pack_first(lap, first_part, second_part):
        vpack[lap, 0, 0:16] = jnp.where(low, first_part, pltpu.roll(second_part, C, 1)).astype(BF16)
        vpack[lap, 1, 0:16] = jnp.where(low, pltpu.roll(first_part, C, 1), second_part).astype(BF16)

    def pack_last(lap, part):
        vpack[lap, 0, 16:32] = jnp.where(low, part, 0.0).astype(BF16)
        vpack[lap, 1, 16:32] = jnp.where(low, pltpu.roll(part, C, 1), 0.0).astype(BF16)

    first_i = lax.div(s, 2)

    alone = jnp.logical_and(own_chunk == pos, first_i <= i)

    def to_owners(src, dst, rows, n):
        @pl.when(alone)
        def _():
            dst[s, rows] = src[half, rows]

        def one(k):
            to_i = k // 2
            to_j = first_block + 2 * (k % 2)
            mine = jnp.logical_and(to_i == i, to_j == j)

            @pl.when(jnp.logical_and(to_i >= first_i, jnp.logical_not(mine)))
            def _():
                push(src.at[k % 2, rows], dst.at[s, rows], fs.at[n], fr.at[n], to_i, to_j)
        for k in reversed(range(16)):
            one(k)

    def owners_sent(dst, rows, n):
        for pair in range(COLS):
            for own in range(2):
                @pl.when(jnp.logical_and(first_i == pair, alone == (own == 1)))
                def _():
                    await_bytes(dst.at[0:2 * (COLS - pair) - own, rows], fs.at[n])

    def owner_sums(dst, rows, n):
        for pair in range(COLS):
            for own in range(2):
                @pl.when(jnp.logical_and(i == pair, alone == (own == 1)))
                def _():
                    await_bytes(dst.at[0:2 * pair + 2 - own, rows], fr.at[n])
        even = jnp.zeros((rows.stop - rows.start, 128), F32)
        odd = even
        for k in range(STEPS):
            later = delta_ref[k:k + 1] * dst[k, rows].astype(F32)
            even = even + jnp.where(k <= 2 * i, later, 0.0)
            odd = odd + jnp.where(k == 2 * i + 1, later, 0.0)
        return even, even + odd

    early_rows, late_rows = slice(0, 16), slice(16, 32)
    blocks = range(3)
    velocities = {}
    through = {}
    own_delta = jnp.sum(jnp.where(step_row == s, delta, 0.0), axis=0, keepdims=True)

    def sum_heads(block):
        velocities[block] = reduce_heads(0, block)
        vsrc[block] = velocities[block].astype(BF16)
        gat[block, s] = velocities[block].astype(BF16)

        def send(k):
            to = lax.rem(s + k, STEPS)
            push(vsrc.at[block], gat.at[block, s], gs.at[block], gr.at[block], i, seq_of(to, p))
        for k in sorted(range(1, STEPS), key=lambda k: abs(k - STEPS // 2)):
            send(k)

    def next_latent(block):
        rows = slice(block * 16, (block + 1) * 16)
        await_bytes(gat.at[block, 0:STEPS - 1], gr.at[block])
        before = jnp.zeros((16, 128), F32)
        for n in range(STEPS):
            before = before + jnp.where(n < s, delta_ref[n:n + 1] * gat[block, n].astype(F32), 0.0)
        latent = (jnp.where(low, basein[0, rows], basein[1, rows]) + before).astype(BF16)
        zsend[block] = latent
        latents[1, block, chunk, :] = latent
        group(lambda n, ti, tj: push(
            zsend.at[block], latents.at[1, block, chunk, :], ps.at[block], pr.at[block], ti, tj))
        through[block] = before + own_delta * vsrc[block].astype(F32)

    def send_through():
        first_part, second_part, third_part = through[0], through[1], through[2]
        tsend[0, 0:16] = jnp.where(low, first_part, pltpu.roll(second_part, C, 1))
        tsend[1, 0:16] = jnp.where(low, pltpu.roll(first_part, C, 1), second_part)
        tsend[0, 16:32] = jnp.where(low, third_part, 0.0)
        tsend[1, 16:32] = jnp.where(low, pltpu.roll(third_part, C, 1), 0.0)
        slot = lax.rem(s, 2)
        for n in range(2):
            @pl.when(from_mine[n])
            def _():
                first_sums[slot] = tsend[n]

            @pl.when(jnp.logical_not(from_mine[n]))
            def _():
                push(tsend.at[n], first_sums.at[slot], ts.at[n], tr.at[slot], from_i, from_j[n])

    def await_latents(block):
        await_bytes(latents.at[1, block, 0:15 * 16, :], pr.at[block])

    send_base()
    await_bytes(zp.at[:, 0:128, :], cr)
    for block in blocks:
        project(0, block)
    for block in blocks:
        finish(0, block, attend(block, blocks, (None, None)))
        if block:
            sum_heads(block - 1)
    for n in range(2):
        @pl.when(jnp.logical_not(from_mine[n]))
        def _():
            await_bytes(basein.at[n], br.at[n])
    next_latent(0)
    sum_heads(2)
    next_latent(1)

    await_latents(0)
    project(1, 0)
    next_latent(2)
    send_through()
    await_latents(1)
    project(1, 1)
    early = [attend(block, (0, 1), (None, None)) for block in (0, 1)]
    await_latents(2)
    project(1, 2)
    for block in (0, 1):
        finish(1, block, attend(block, (2,), early[block]))
    finish(1, 2, attend(2, blocks, (None, None)))
    pack_first(1, reduce_heads(1, 0), reduce_heads(1, 1))
    to_owners(vpack.at[1], fin1, early_rows, 1)
    for n in range(2):
        @pl.when(jnp.logical_not(base_mine[n]))
        def _():
            await_bytes(first_sums.at[n], tr.at[n])
    pack_last(1, reduce_heads(1, 2))
    to_owners(vpack.at[1], fin1, late_rows, 2)

    even, odd = (
        jnp.concatenate(parts, axis=0) for parts in zip(owner_sums(fin1, early_rows, 1), owner_sums(fin1, late_rows, 2)))
    change_even = even - first_sums[0]
    change_odd = odd - first_sums[1]

    def unpack(x):
        return jnp.concatenate([x[0:16], pltpu.roll(x[0:16], C, 1), x[16:32]], axis=0)

    row = lax.broadcasted_iota(jnp.int32, (2, 128), 0)
    sum_even = jnp.sum(change_even * change_even, axis=0, keepdims=True)
    sum_odd = jnp.sum(change_odd * change_odd, axis=0, keepdims=True)
    partial = jnp.where(row == 0, sum_even, sum_odd)
    esrc[...] = partial
    ein[j] = partial
    column(lambda tj: push(esrc, ein.at[j], es, er, i, tj))
    for n, total in enumerate((basesrc[1] + unpack(even), basesrc[2] + unpack(odd))):
        out_ref[n] = total[:, 0:C]
    for lap in range(2):
        await_bytes(red.at[lap, :, 0:STEPS - 1], us.at[lap])
    for block in blocks:
        await_bytes(gat.at[block, 0:STEPS - 1], gs.at[block])
        await_bytes(latents.at[1, block, 0:15 * 16, :], ps.at[block])
    for n in range(2):
        @pl.when(jnp.logical_not(from_mine[n]))
        def _():
            await_bytes(tsend.at[n], ts.at[n])
    owners_sent(fin1, early_rows, 1)
    owners_sent(fin1, late_rows, 2)
    @pl.when(sends_start)
    def _():
        await_bytes(wall.at[0:31 * 32, 0:128], ys)

    await_bytes(nin.at[0:COLS - 1], ns)
    await_bytes(zp.at[:, 0:128, :], cs)
    for n in range(2):
        @pl.when(jnp.logical_not(base_mine[n]))
        def _():
            await_bytes(basesrc.at[n], bs.at[n])

    await_bytes(ein.at[0:SEQ - 1], er)
    total = ein[0]
    for n in range(1, SEQ):
        total = total + ein[n]
    total = total * (1.0 / (LEN * C))
    err_ref[0] = jnp.sum(total[0:1] / (coeff_even * coeff_even))
    err_ref[1] = jnp.sum(total[1:2] / (coeff_odd * coeff_odd))

    await_bytes(ein.at[0:SEQ - 1], es)


def per_device(
    start_latent, noise, window_start, w_embed, w_time, norm_gain, w_query, w_key, w_value, query_gain, key_gain, w_out, w_final,
):
    vmem = pl.BlockSpec(memory_space=pltpu.VMEM)
    hbm = pl.BlockSpec(memory_space=pltpu.HBM)
    smem = pl.BlockSpec(memory_space=pltpu.SMEM)
    dma = pltpu.SemaphoreType.DMA
    out, errors = pl.pallas_call(
        kernel,
        out_shape=(
            pltpu.VMEM((2, ROWS, C), F32),
            pltpu.SMEM((2,), F32),
        ),
        in_specs=[smem] + [hbm] * 12,
        out_specs=(vmem, smem),
        scratch_shapes=[
            pltpu.VMEM((ROWS, C), F32),
            pltpu.VMEM((2, ROWS, C), BF16),
            pltpu.VMEM((1, D), F32),
            pltpu.VMEM((1, HEAD), F32),
            pltpu.VMEM((1, HEAD), F32),
            pltpu.VMEM((256, D), BF16),
            pltpu.VMEM((D, 3 * HEAD), BF16),
            pltpu.VMEM((160, D), BF16),
            pltpu.VMEM((224, D), BF16),
            pltpu.VMEM((256, D), BF16),
            pltpu.VMEM((384, 256), BF16),
            pltpu.VMEM((256, 128), BF16),
            pltpu.VMEM((8, 128), F32),
            pltpu.VMEM((STEPS, 128), F32),
            pltpu.VMEM((STEPS, 128), F32),
            pltpu.VMEM((32, 128), BF16),
            pltpu.VMEM((16, 32, 128), BF16),
            pltpu.VMEM((ROWS, 128), BF16),
            pltpu.VMEM((COLS, ROWS, 128), BF16),
            pltpu.VMEM((3, ROWS, 128), F32),
            pltpu.VMEM((2, ROWS, 128), F32),
            pltpu.VMEM((2, 3, QBLK, 128), BF16),
            pltpu.VMEM((2, 3, QBLK, 128), BF16),
            pltpu.VMEM((2, 3, STEPS, 16, 128), BF16),
            pltpu.VMEM((3, 16, 128), BF16),
            pltpu.VMEM((2, 2, 32, 128), BF16),
            pltpu.VMEM((3, STEPS, 16, 128), BF16),
            pltpu.VMEM((3, 16, 128), BF16),
            pltpu.VMEM((STEPS, 32, 128), BF16),
            pltpu.VMEM((2, 32, 128), F32),
            pltpu.VMEM((2, 32, 128), F32),
            pltpu.VMEM((2, 128), F32),
            pltpu.VMEM((SEQ, 2, 128), F32),
            pltpu.VMEM((256, KBLK), BF16),
            pltpu.VMEM((LEN, HEAD), BF16),
            pltpu.VMEM((HEAD, LEN), BF16),
            pltpu.VMEM((C + 16, LEN), BF16),
            dma((5 + 7 * PARTS,)),
            dma, dma, dma, dma, dma, dma, dma((2,)), dma((2,)),
            dma((2,)), dma((2, 3)), dma((3,)), dma((3,)), dma((3,)), dma((3,)), dma((3,)), dma((3,)), dma((2,)), dma((2,)), dma, dma,
        ],
        compiler_params=pltpu.CompilerParams(
            collective_id=0, has_side_effects=True, vmem_limit_bytes=56 * 1024 * 1024),
    )(
        window_start, start_latent, noise, norm_gain.reshape(1, D), query_gain.reshape(1, HEAD), key_gain.reshape(1, HEAD),
        w_embed, w_time, w_final.T, w_query, w_key, w_value, w_out,
    )
    return out, errors


def solution(mesh):
    return jax.shard_map(
        per_device,
        mesh=mesh,
        in_specs=(
            P("seq", None), P("step", "seq", None), P(), P(), P(), P(),
            P(None, "step"), P(None, "step"), P(None, "step"), P(), P(), P("step", None), P(),
        ),
        out_specs=(P("step", "seq", None), P("step")),
        check_vma=False,
    )
```
